128 devices in a mesh: lon: 32 (over y, z, core), lat: 4 (over x).
Axes of the slice: x: 4, y: 4, z: 4, core: 2. Of those that a mesh axis runs over, the one named last changes fastest.
Arguments:
- kappa_sq: float32 [2048, 2048], P('lon', 'lat'), may hold values from 0.05 to 1
- prior_scale: float32 [2048, 2048], P('lon', 'lat'), may hold values from 0.02 to 0.2
- templates: bfloat16 [64, 128, 256], replicated, may hold values from -0.375 to 0.375
- block_counts: int32 [128], P(('lon', 'lat')), may hold values from 1 to 128, 8192 in all
- anchor_lon: int32 [32, 512], P('lon', 'lat'), may hold values from 0 to 48
- anchor_lat: int32 [32, 512], P('lon', 'lat'), may hold values from 0 to 496
- template_ids: int32 [32, 512], P('lon', 'lat'), may hold values from 0 to 63
- readings: float32 [32, 512, 128], P('lon', 'lat'), may hold values from -12 to 12
- noise_prec: float32 [32, 512, 128], P('lon', 'lat'), may hold values from 0.3 to 3
Outputs:
- solution_field: float32 [2048, 2048], P('lon', 'lat')
- residual: float32 [2048, 2048], P('lon', 'lat')
The draws below stay inside these ranges and needn't reach their ends.
Inputs may be any that keep to these rules, and one draw needn't show every extreme that they name: `block_counts`: slots of a tile at or past its count are ignored; some tile lists exactly 128 blocks. `anchor_lon`: every patch lies inside its own tile. `anchor_lat`: every patch lies inside its own tile.
All inputs are finite; a program needn't handle non-finite values.
Results may differ from the reference program's by a relative error of at most 0.0003.
Values sent between devices are 32-bit elements; how exact they have to be, the bound alone decides.
A program may use at most 64 MiB of HBM per device.

```python
import math
import jax
import jax.numpy as jnp
import numpy as np
from jax import lax

CX = 64
CY = 512
PSIDE = 16
READS = 128
TEMPLATES = 64
BMEAN = 64
ITERS = 3
TCELLS = 256
BCAP = 128
NX = 2048
NY = 2048
N_LON = 32
N_LAT = 4
DEVICES = 128


def draw_readings(key, part):
    key = jax.random.fold_in(key, 7)
    shape = (N_LON, N_LAT * BCAP, READS)
    ramp = jnp.arange(N_LON, dtype=jnp.float32)[:, None, None] / max(N_LON - 1, 1)
    values = jnp.clip(jax.random.normal(key, shape, jnp.float32), -4.0, 4.0)
    factor = 1.0 + 2.0 * ramp
    return (values * factor).astype(jnp.float32)


def set_ends(result, key, least, largest):
    dims = result.shape
    place = [jax.random.randint(jax.random.fold_in(key, axis), (), 0, dims[axis]) for axis in range(len(dims))]
    result = result.at[tuple(place)].set(least)
    longest = dims.index(max(dims))
    place[longest] = (place[longest] + 1) % dims[longest]
    return result.at[tuple(place)].set(largest)


def shard_levels(stream_key, extent, pieces, low, largest):
    gain, own = 1.0, jax.random.fold_in(stream_key, 6)
    for axis_at, parts in pieces:
        steps = jnp.exp(jax.random.uniform(jax.random.fold_in(own, axis_at), (parts,), jnp.float32, low / len(pieces), largest / len(pieces)))
        gain = gain * jnp.repeat(steps, extent[axis_at] // parts).reshape([-1 if axis == axis_at else 1 for axis in range(len(extent))])
    return gain


def rank_table(count, skew):
    portions = [(1 << 20) // math.isqrt(rank ** skew) + 1 for rank in range(1, count + 1)]
    deviation = 1 + sum(portions) // (1 << 30)
    return np.cumsum(np.array([max(1, weight // deviation) for weight in portions]))


def ranked(rng, dims, count, lean):
    table = rank_table(count, lean)
    lot = jax.random.randint(jax.random.fold_in(rng, 1), dims, 0, int(table[count - 1]))
    standing = jnp.searchsorted(jnp.asarray(table, jnp.int32), lot, side="right")
    return jax.random.permutation(jax.random.fold_in(rng, 2), count)[standing].astype(jnp.int32)


def length_profile(count, total, most, skew):
    weights = [(1 << 20) // math.isqrt(grade ** skew) + 1 for grade in range(2, count + 1)]
    spare, holding = total - most - (count - 1), [1] * (count - 1)
    while spare > 0:
        candidates = [i for i in range(count - 1) if holding[i] < most]
        pool, remaining = sum([weights[i] for i in candidates]), spare
        for i in candidates:
            addition = min(most - holding[i], max(1, remaining * weights[i] // pool), spare)
            holding[i] = holding[i] + addition
            spare = spare - addition
    return np.array([most] + holding)


def uneven_parts(stream_key, number_of, total, most, slope):
    if number_of == 2:
        one = jax.random.randint(stream_key, (), max(1, total - most), min(most, total - 1) + 1)
        return jnp.stack([one, total - one])
    sizes = jnp.asarray(length_profile(number_of, total, most, slope), jnp.int32)
    twos = (number_of - 1) // 2
    donor, receiver = sizes[1:1 + 2 * twos:2], sizes[2:2 + 2 * twos:2]
    room = jnp.minimum(donor - 1, most - receiver)
    shifted = jax.random.randint(jax.random.fold_in(stream_key, 1), (twos,), 0, 1 << 20) % (room + 1)
    sizes = sizes.at[1:1 + 2 * twos:2].set(donor - shifted).at[2:2 + 2 * twos:2].set(receiver + shifted)
    return sizes[jax.random.permutation(jax.random.fold_in(stream_key, 2), number_of)]


def noise(rng, extent, spread, limit, kind=jnp.bfloat16):
    result = jax.random.normal(rng, extent, jnp.float32) * spread
    return jnp.minimum(jnp.maximum(result, -limit), limit).astype(kind)


def setup_inputs(seed: int = 0) -> dict:
    keys = jax.random.split(jax.random.key(seed), 10)
    kappa_sq = jnp.clip(jnp.exp(math.log(1.0) - 2.9957323 * jax.random.uniform(keys[0], (NX, NY), jnp.float32) ** shard_levels(keys[0], (NX, NY), ((0, 32), (1, 4)), -0.2, 0.2)), 0.05, 1.0)
    prior_scale = jnp.clip(jnp.exp(math.log(0.2) - 2.3025851 * jax.random.uniform(keys[1], (NX, NY), jnp.float32) ** shard_levels(keys[1], (NX, NY), ((0, 32), (1, 4)), -0.2, 0.2)), 0.02, 0.2)
    templates = noise(keys[2], (TEMPLATES, READS, TCELLS), TCELLS ** -0.5, 0.375)
    block_counts = uneven_parts(keys[3], DEVICES, DEVICES * BMEAN, BCAP, 2).astype(jnp.int32)
    anchor_lon = set_ends(jax.random.randint(keys[4], (N_LON, N_LAT * BCAP), 0, CX - PSIDE + 1), jax.random.fold_in(keys[4], 1), 0, CX - PSIDE).astype(jnp.int32)
    anchor_lat = set_ends(jax.random.randint(keys[5], (N_LON, N_LAT * BCAP), 0, CY - PSIDE + 1), jax.random.fold_in(keys[5], 1), 0, CY - PSIDE).astype(jnp.int32)
    template_ids = set_ends(ranked(keys[6], (N_LON, N_LAT * BCAP), TEMPLATES, 2), jax.random.fold_in(keys[6], 3), 0, TEMPLATES - 1).astype(jnp.int32)
    readings = draw_readings(jax.random.fold_in(keys[9], 71), 0)
    noise_prec = jnp.clip(jnp.exp(math.log(3.0) - 2.3025851 * jax.random.uniform(keys[8], (N_LON, N_LAT * BCAP, READS), jnp.float32) ** shard_levels(keys[8], (N_LON, N_LAT * BCAP, READS), ((0, 32), (1, 4)), -0.2, 0.2)), 0.3, 3.0)
    return dict(kappa_sq=kappa_sq, prior_scale=prior_scale, templates=templates, block_counts=block_counts, anchor_lon=anchor_lon, anchor_lat=anchor_lat, template_ids=template_ids, readings=readings, noise_prec=noise_prec)


def stencil(field, coeff):
    east = jnp.roll(field, -1, 0)
    west = jnp.roll(field, 1, 0)
    north = jnp.concatenate([field[:, 1:], jnp.zeros_like(field[:, :1])], 1)
    south = jnp.concatenate([jnp.zeros_like(field[:, :1]), field[:, :-1]], 1)
    return (coeff + 4.0) * field - (east + west + north + south)


def reference(kappa_sq, prior_scale, templates, block_counts, anchor_lon, anchor_lat, template_ids, readings, noise_prec):
    nlon, width = template_ids.shape
    tile_lon = jnp.arange(nlon, dtype=jnp.int32)[:, None]
    column = jnp.arange(width, dtype=jnp.int32)[None, :]
    tile_lat = column // BCAP
    slot = column % BCAP
    counts = block_counts.reshape(nlon, N_LAT)
    live = slot < counts[tile_lon, tile_lat]
    glon = tile_lon * CX + anchor_lon
    glat = tile_lat * CY + anchor_lat
    cell = jnp.arange(TCELLS, dtype=jnp.int32)
    cell_index = ((glon[..., None] + cell // PSIDE) * NY + glat[..., None] + cell % PSIDE).astype(jnp.int32)
    cell_index = cell_index.reshape(-1, TCELLS)
    idents = jnp.where(live, template_ids, -1).reshape(-1, BCAP)
    weights = jnp.where(live[..., None], noise_prec, 0.0).reshape(-1, READS)
    weighted = (weights * readings.reshape(-1, READS)).reshape(-1, BCAP, READS)
    weights = weights.reshape(-1, BCAP, READS)

    def group_terms(inputs):
        patch, ident, weight, extra = inputs
        chosen = templates[jnp.maximum(ident, 0)].astype(jnp.float32)
        image = jnp.einsum("gri,gi->gr", chosen, patch, precision=lax.Precision.HIGHEST)
        mixed = weight * image + extra
        return jnp.einsum("gri,gr->gi", chosen, mixed, precision=lax.Precision.HIGHEST)

    def spread_terms(terms):
        flat = jnp.zeros((NX * NY,), jnp.float32).at[cell_index.reshape(-1)].add(terms.reshape(-1))
        return flat.reshape(NX, NY)

    def observe(field):
        patches = field.reshape(-1)[cell_index].reshape(-1, BCAP, TCELLS)
        terms = lax.map(group_terms, (patches, idents, weights, jnp.zeros_like(weights)))
        return spread_terms(terms)

    def operator(field):
        return stencil(prior_scale * stencil(field, kappa_sq), kappa_sq) + observe(field)

    zero_patch = jnp.zeros((weights.shape[0], BCAP, TCELLS), jnp.float32)
    right = spread_terms(lax.map(group_terms, (zero_patch, idents, weights, weighted)))
    solution_field = jnp.zeros_like(right)
    residual, direction = right, right
    norm_now = jnp.sum(residual * residual)
    for turn in range(ITERS):
        image = operator(direction)
        alpha = norm_now / jnp.sum(direction * image)
        solution_field = solution_field + alpha * direction
        residual = residual - alpha * image
        norm_next = jnp.sum(residual * residual)
        direction = residual + (norm_next / norm_now) * direction
        norm_now = norm_next
    return solution_field, residual
```

```python
import functools

import jax
import jax.numpy as jnp
from jax import lax
from jax.experimental import pallas as pl
from jax.experimental.pallas import tpu as pltpu
from jax.sharding import PartitionSpec as P

PSIDE = 16
ITERS = 3
LANES = 128
ROWS = 8
PER_TILE = LANES // PSIDE
F32 = jnp.float32
BF16 = jnp.bfloat16
MESH = pl.DeviceIdType.MESH
NT = (((1,), (1,)), ((), ()))


def split(value):
    high = value.astype(BF16)
    low = (value - high.astype(F32)).astype(BF16)
    return high, low


def block_transpose(value):
    row = lax.broadcasted_iota(jnp.int32, value.shape, 1)
    chunk = lax.broadcasted_iota(jnp.int32, value.shape, 2) // PSIDE
    for k in (4, 2, 1):
        row_bit = (row // k) % 2
        chunk_bit = (chunk // k) % 2
        ahead = pltpu.roll(pltpu.roll(value, ROWS - k, 1), PSIDE * k, 2)
        if k == 4:
            other = ahead
        else:
            behind = pltpu.roll(pltpu.roll(value, k, 1), LANES - PSIDE * k, 2)
            other = jnp.where(row_bit == 0, ahead, behind)
        value = jnp.where(row_bit == chunk_bit, value, other)
    return value


def fold(value):
    total = jnp.sum(value.reshape(value.shape[0] // ROWS, ROWS, value.shape[1]), axis=0)
    parts = [total[:, i : i + LANES] for i in range(0, total.shape[1], LANES)]
    return functools.reduce(jnp.add, parts)


def shifted(field, prev_lon, next_lon, prev_lat, next_lat, has_prev, has_next):
    rows, cols = field.shape
    row = lax.broadcasted_iota(jnp.int32, field.shape, 0)
    lane = lax.broadcasted_iota(jnp.int32, prev_lat.shape, 1)
    west = jnp.where(row == 0, prev_lon[ROWS - 1 : ROWS, :], pltpu.roll(field, 1, 0))
    east = jnp.where(row == rows - 1, next_lon[0:1, :], pltpu.roll(field, rows - 1, 0))
    south = pltpu.roll(field, 1, 1)
    north = pltpu.roll(field, cols - 1, 1)
    first = jnp.where(lane == 0, pltpu.roll(prev_lat, 1, 1) * has_prev, south[:, :LANES])
    last = jnp.where(
        lane == LANES - 1, pltpu.roll(next_lat, LANES - 1, 1) * has_next, north[:, cols - LANES :]
    )
    south = jnp.concatenate([first, south[:, LANES:]], 1)
    north = jnp.concatenate([north[:, : cols - LANES], last], 1)
    return west + east + south + north


def kernel(
    n_lon,
    n_lat,
    kappa_ref,
    prior_ref,
    templates_hbm,
    count_ref,
    lon_ref,
    lat_ref,
    ids_ref,
    readings_ref,
    noise_ref,
    x_ref,
    r_ref,
    templates_ref,
    select_ref,
    columns_ref,
    padded_ref,
    placed_ref,
    spread_ref,
    patch_ref,
    ids_rows_ref,
    weights_ref,
    term_ref,
    p_ref,
    s_ref,
    u_ref,
    edge_lon,
    edge_lat,
    sum_a,
    sum_b,
    template_sem,
    edge_send,
    edge_recv,
    a_send,
    a_recv,
    b_send,
    b_recv,
):
    kinds, reads, cells = templates_ref.shape
    rows, cols = kappa_ref.shape
    blocks = ids_ref.shape[1]
    tiles = blocks // PER_TILE
    lon, lat = lax.axis_index("lon"), lax.axis_index("lat")
    group_a, group_b = 2 * n_lat, n_lon // 2
    core, me_b = lon % 2, lon // 2
    me_a = lat * 2 + core

    def peer_a(step):
        index = (me_a + step) % group_a
        return (me_b * 2 + index % 2, index // 2)

    def peer_b(step):
        return (((me_b + step) % group_b) * 2 + core, lat)

    lon_next, lon_prev = ((lon + 1) % n_lon, lat), ((lon + n_lon - 1) % n_lon, lat)
    lat_next, lat_prev = (lon, (lat + 1) % n_lat), (lon, (lat + n_lat - 1) % n_lat)

    template_copy = pltpu.make_async_copy(templates_hbm, templates_ref, template_sem)
    template_copy.start()

    barrier = pltpu.get_barrier_semaphore()
    peers = [lon_next, lon_prev, lat_next, lat_prev]
    peers += [peer_a(step) for step in range(1, group_a)]
    peers += [peer_b(step) for step in range(1, group_b)]
    for peer in peers:
        pl.semaphore_signal(barrier, inc=1, device_id=peer, device_id_type=MESH)

    def edges(source, kind, turn):
        pieces = [
            (source.at[pl.ds(rows - ROWS, ROWS), :], edge_lon.at[kind, turn, 0], lon_next),
            (source.at[pl.ds(0, ROWS), :], edge_lon.at[kind, turn, 1], lon_prev),
            (source.at[:, pl.ds(cols - LANES, LANES)], edge_lat.at[kind, turn, 0], lat_next),
            (source.at[:, pl.ds(0, LANES)], edge_lat.at[kind, turn, 1], lat_prev),
        ]
        return [
            pltpu.make_async_remote_copy(
                src_ref=src,
                dst_ref=dst,
                send_sem=edge_send.at[kind, turn, place],
                recv_sem=edge_recv.at[kind, turn, place],
                device_id=peer,
                device_id_type=MESH,
            )
            for place, (src, dst, peer) in enumerate(pieces)
        ]

    def sums(buffer, me, send, recv, turn, peers):
        return [
            pltpu.make_async_remote_copy(
                src_ref=buffer.at[turn, me],
                dst_ref=buffer.at[turn, me],
                send_sem=send.at[turn, step],
                recv_sem=recv.at[turn, step],
                device_id=peer,
                device_id_type=MESH,
            )
            for step, peer in enumerate(peers)
        ]

    has_prev = (lat > 0).astype(F32)
    has_next = (lat < n_lat - 1).astype(F32)

    def neighbours(field, kind, turn):
        return shifted(
            field,
            edge_lon[kind, turn, 0],
            edge_lon[kind, turn, 1],
            edge_lat[kind, turn, 0],
            edge_lat[kind, turn, 1],
            has_prev,
            has_next,
        )

    offset = lax.broadcasted_iota(jnp.int32, (PSIDE, cols), 1) - lax.broadcasted_iota(
        jnp.int32, (PSIDE, cols), 0
    )

    def one_selector(block, carry):
        start = pl.multiple_of(block * PSIDE, PSIDE)
        chosen = jnp.where(offset == lat_ref[0, block], 1.0, 0.0)
        select_ref[pl.ds(start, PSIDE), :] = chosen.astype(BF16)
        return carry

    lax.fori_loop(0, blocks, one_selector, 0)
    padded_ref[...] = jnp.zeros(padded_ref.shape, F32)
    p_ref[...] = jnp.zeros(p_ref.shape, F32)
    s_ref[...] = jnp.zeros(s_ref.shape, F32)
    x_ref[...] = jnp.zeros(x_ref.shape, F32)
    slot = lax.broadcasted_iota(jnp.int32, (blocks, reads), 0)
    weights_ref[...] = jnp.where(slot < count_ref[0], noise_ref[...], 0.0)
    ids_row = jnp.broadcast_to(ids_ref[...].astype(F32), (blocks, blocks))
    ids_rows_ref[...] = jnp.transpose(ids_row)
    chunk = lax.broadcasted_iota(jnp.int32, (ROWS, LANES), 1) // PSIDE

    def read(field):
        high, low = split(field)
        both = lax.dot_general(
            jnp.concatenate([high, low], 0), select_ref[...], NT, preferred_element_type=F32
        )
        both = both[:rows] + both[rows:]
        for tile in range(tiles):
            columns_ref[tile] = both[:, tile * LANES : (tile + 1) * LANES]

        def one_tile(tile, carry):
            halves = []
            for half in range(2):
                picked = jnp.zeros((ROWS, LANES), F32)
                for place in range(PER_TILE):
                    start = lon_ref[0, tile * PER_TILE + place] + half * ROWS
                    window = columns_ref[tile, pl.ds(start, ROWS), :]
                    picked = jnp.where(chunk == place, window, picked)
                halves.append(picked)
            turned = block_transpose(jnp.stack(halves))
            start = pl.multiple_of(tile * ROWS, ROWS)
            patch_ref[pl.ds(start, ROWS), 0:LANES] = turned[0]
            patch_ref[pl.ds(start, ROWS), LANES : 2 * LANES] = turned[1]
            return carry

        lax.fori_loop(0, tiles, one_tile, 0)
        high, low = split(jnp.transpose(patch_ref[...]))
        patches = jnp.concatenate([high, low], 1)
        ids = jnp.broadcast_to(ids_ref[...], (ROWS, blocks))
        some = 8

        def some_kinds(turn, acc):
            first = turn * some
            table = templates_ref[pl.ds(first, some)].reshape(some * reads, cells)
            result = jnp.dot(table, patches, preferred_element_type=F32)
            result = result[:, :blocks] + result[:, blocks:]
            for kind in range(some):
                mine = (ids == first + kind)[:1]
                acc = jnp.where(mine, result[kind * reads : (kind + 1) * reads], acc)
            return acc

        acc = lax.fori_loop(0, kinds // some, some_kinds, jnp.zeros((reads, blocks), F32))
        return jnp.transpose(acc)

    def spread(mixed):
        high, low = split(mixed)
        both = jnp.concatenate([high, low], 0)
        ids = ids_rows_ref[...].astype(BF16)
        ids = jnp.concatenate([ids, ids], 0)
        for kind in range(kinds):
            placed_ref[:, kind * reads : (kind + 1) * reads] = jnp.where(
                ids == kind, both, jnp.zeros_like(both)
            )
        terms = jnp.dot(
            placed_ref[...],
            templates_ref[...].reshape(kinds * reads, cells),
            preferred_element_type=F32,
        )
        terms = terms[:blocks] + terms[blocks:]
        lead = rows - PSIDE
        for half in range(2):
            part = terms[:, half * LANES : (half + 1) * LANES].reshape(tiles, ROWS, LANES)
            padded_ref[:, lead + half * ROWS : lead + (half + 1) * ROWS, :] = block_transpose(part)

        def one_tile(tile, carry):
            picked = jnp.zeros((rows, LANES), F32)
            wide = lax.broadcasted_iota(jnp.int32, (rows, LANES), 1) // PSIDE
            for place in range(PER_TILE):
                start = lead - lon_ref[0, tile * PER_TILE + place]
                window = padded_ref[tile, pl.ds(start, rows), :]
                picked = jnp.where(wide == place, window, picked)
            high, low = split(picked)
            start = pl.multiple_of(tile * LANES, LANES)
            spread_ref[0:rows, pl.ds(start, LANES)] = high
            spread_ref[rows : 2 * rows, pl.ds(start, LANES)] = low
            return carry

        lax.fori_loop(0, tiles, one_tile, 0)
        both = jnp.dot(spread_ref[...], select_ref[...], preferred_element_type=F32)
        return both[:rows] + both[rows:]

    template_copy.wait()
    r_ref[...] = spread(weights_ref[...] * readings_ref[...])
    pl.semaphore_wait(barrier, len(peers))

    def one_turn(turn, carry):
        norm_old, alpha_old = carry
        r_copies = edges(r_ref, 0, turn)
        for copy in r_copies:
            copy.start()
        residual = r_ref[...]
        image = read(residual)
        mixed = weights_ref[...] * image
        term_ref[...] = mixed
        for copy in r_copies:
            copy.wait_recv()
        first = (kappa_ref[...] + 4.0) * residual - neighbours(residual, 0, turn)
        scaled = prior_ref[...] * first
        u_ref[...] = scaled
        u_copies = edges(u_ref, 1, turn)
        for copy in u_copies:
            copy.start()
        sum_a[turn, me_a, 0:ROWS] = fold(residual * residual)
        sum_a[turn, me_a, ROWS : 2 * ROWS] = fold(scaled * first) + fold(mixed * image)
        a_copies = sums(
            sum_a, me_a, a_send, a_recv, turn, [peer_a(step) for step in range(1, group_a)]
        )
        for copy in a_copies:
            copy.start()
        observed = spread(term_ref[...])
        for copy in a_copies:
            copy.wait_recv()
        sum_b[turn, me_b] = jnp.sum(sum_a[turn], axis=0)
        b_copies = sums(
            sum_b, me_b, b_send, b_recv, turn, [peer_b(step) for step in range(1, group_b)]
        )
        for copy in b_copies:
            copy.start()
        for copy in u_copies:
            copy.wait_recv()
        scaled = u_ref[...]
        w = (kappa_ref[...] + 4.0) * scaled - neighbours(scaled, 1, turn) + observed
        for copy in b_copies:
            copy.wait_recv()
        total = jnp.sum(sum_b[turn], axis=0)
        norm = jnp.sum(total[:ROWS], keepdims=True)
        curve = jnp.sum(total[ROWS:], keepdims=True)
        beta = jnp.where(turn > 0, norm / norm_old, 0.0)
        alpha = norm / (curve - beta * norm / alpha_old)
        for copy in r_copies + u_copies + a_copies + b_copies:
            copy.wait_send()
        p = r_ref[...] + beta * p_ref[...]
        s = w + beta * s_ref[...]
        p_ref[...] = p
        s_ref[...] = s
        x_ref[...] += alpha * p
        r_ref[...] -= alpha * s
        return norm, alpha

    one = jnp.ones((1, 1), F32)
    lax.fori_loop(0, ITERS, one_turn, (one, one))


def on_device(
    n_lon,
    n_lat,
    kappa_sq,
    prior_scale,
    templates,
    block_counts,
    anchor_lon,
    anchor_lat,
    template_ids,
    readings,
    noise_prec,
):
    rows, cols = kappa_sq.shape
    kinds, reads, cells = templates.shape
    blocks = template_ids.shape[1]
    tiles = blocks // PER_TILE
    group_a, group_b = 2 * n_lat, n_lon // 2
    vmem = pl.BlockSpec(memory_space=pltpu.VMEM)
    smem = pl.BlockSpec(memory_space=pltpu.SMEM)
    dma = pltpu.SemaphoreType.DMA
    field = jax.ShapeDtypeStruct((rows, cols), F32)
    return pl.pallas_call(
        functools.partial(kernel, n_lon, n_lat),
        out_shape=(field, field),
        in_specs=[
            vmem,
            vmem,
            pl.BlockSpec(memory_space=pl.ANY),
            smem,
            smem,
            smem,
            vmem,
            vmem,
            vmem,
        ],
        out_specs=(vmem, vmem),
        scratch_shapes=[
            pltpu.VMEM((kinds, reads, cells), BF16),
            pltpu.VMEM((blocks * PSIDE, cols), BF16),
            pltpu.VMEM((tiles, rows, LANES), F32),
            pltpu.VMEM((tiles, 2 * rows - PSIDE, LANES), F32),
            pltpu.VMEM((2 * blocks, kinds * reads), BF16),
            pltpu.VMEM((2 * rows, blocks * PSIDE), BF16),
            pltpu.VMEM((blocks, cells), F32),
            pltpu.VMEM((blocks, blocks), F32),
            pltpu.VMEM((blocks, reads), F32),
            pltpu.VMEM((blocks, reads), F32),
            pltpu.VMEM((rows, cols), F32),
            pltpu.VMEM((rows, cols), F32),
            pltpu.VMEM((rows, cols), F32),
            pltpu.VMEM((2, ITERS, 2, ROWS, cols), F32),
            pltpu.VMEM((2, ITERS, 2, rows, LANES), F32),
            pltpu.VMEM((ITERS, group_a, 2 * ROWS, LANES), F32),
            pltpu.VMEM((ITERS, group_b, 2 * ROWS, LANES), F32),
            dma,
            dma((2, ITERS, 4)),
            dma((2, ITERS, 4)),
            dma((ITERS, group_a - 1)),
            dma((ITERS, group_a - 1)),
            dma((ITERS, group_b - 1)),
            dma((ITERS, group_b - 1)),
        ],
        compiler_params=pltpu.CompilerParams(
            collective_id=0, has_side_effects=True, vmem_limit_bytes=48 * 1024 * 1024
        ),
    )(
        kappa_sq,
        prior_scale,
        templates,
        block_counts,
        anchor_lon,
        anchor_lat,
        template_ids,
        readings[0],
        noise_prec[0],
    )


def solution(mesh):
    return jax.shard_map(
        functools.partial(on_device, mesh.shape["lon"], mesh.shape["lat"]),
        mesh=mesh,
        in_specs=(
            P("lon", "lat"),
            P("lon", "lat"),
            P(),
            P(("lon", "lat")),
            P("lon", "lat"),
            P("lon", "lat"),
            P("lon", "lat"),
            P("lon", "lat", None),
            P("lon", "lat", None),
        ),
        out_specs=(P("lon", "lat"), P("lon", "lat")),
        check_vma=False,
    )
```

```python
import functools

import jax
import jax.numpy as jnp
from jax import lax
from jax.experimental import pallas as pl
from jax.experimental.pallas import tpu as pltpu
from jax.sharding import PartitionSpec as P

PSIDE = 16
ITERS = 3
LANES = 128
ROWS = 8
PER_TILE = LANES // PSIDE
F32 = jnp.float32
BF16 = jnp.bfloat16
MESH = pl.DeviceIdType.MESH


def split(value):
    high = value.astype(BF16)
    low = (value - high.astype(F32)).astype(BF16)
    return high, low


def block_transpose(value):
    row = lax.broadcasted_iota(jnp.int32, value.shape, 1)
    chunk = lax.broadcasted_iota(jnp.int32, value.shape, 2) // PSIDE
    for k in (4, 2, 1):
        row_bit = (row // k) % 2
        chunk_bit = (chunk // k) % 2
        ahead = pltpu.roll(pltpu.roll(value, ROWS - k, 1), PSIDE * k, 2)
        if k == 4:
            other = ahead
        else:
            behind = pltpu.roll(pltpu.roll(value, k, 1), LANES - PSIDE * k, 2)
            other = jnp.where(row_bit == 0, ahead, behind)
        value = jnp.where(row_bit == chunk_bit, value, other)
    return value


def fold(value):
    total = jnp.sum(value.reshape(value.shape[0] // ROWS, ROWS, value.shape[1]), axis=0)
    parts = [total[:, i : i + LANES] for i in range(0, total.shape[1], LANES)]
    return functools.reduce(jnp.add, parts)


def shifted(field, prev_lon, next_lon, prev_lat, next_lat, has_prev, has_next):
    rows, cols = field.shape
    row = lax.broadcasted_iota(jnp.int32, field.shape, 0)
    lane = lax.broadcasted_iota(jnp.int32, prev_lat.shape, 1)
    west = jnp.where(row == 0, prev_lon[ROWS - 1 : ROWS, :], pltpu.roll(field, 1, 0))
    east = jnp.where(row == rows - 1, next_lon[0:1, :], pltpu.roll(field, rows - 1, 0))
    south = pltpu.roll(field, 1, 1)
    north = pltpu.roll(field, cols - 1, 1)
    first = jnp.where(lane == 0, pltpu.roll(prev_lat, 1, 1) * has_prev, south[:, :LANES])
    last = jnp.where(
        lane == LANES - 1, pltpu.roll(next_lat, LANES - 1, 1) * has_next, north[:, cols - LANES :]
    )
    south = jnp.concatenate([first, south[:, LANES:]], 1)
    north = jnp.concatenate([north[:, : cols - LANES], last], 1)
    return west + east + south + north


def kernel(
    n_lon,
    n_lat,
    kappa_hbm,
    prior_hbm,
    templates_hbm,
    count_hbm,
    lon_hbm,
    lat_hbm,
    ids_hbm,
    readings_hbm,
    noise_hbm,
    x_ref,
    r_ref,
    kappa_ref,
    prior_ref,
    templates_ref,
    count_ref,
    lon_ref,
    lat_ref,
    ids_ref,
    readings_ref,
    weights_ref,
    select_ref,
    turned_ref,
    columns_ref,
    padded_ref,
    spread_ref,
    patch_ref,
    ids_rows_ref,
    term_ref,
    r0_ref,
    w0_ref,
    r1_ref,
    w1_ref,
    v_ref,
    u_ref,
    first_ref,
    edge_lon,
    edge_lat,
    first_a,
    first_b,
    last_a,
    last_b,
    load_sem,
    edge_send,
    edge_recv,
    first_a_send,
    first_a_recv,
    first_b_send,
    first_b_recv,
    last_a_send,
    last_a_recv,
    last_b_send,
    last_b_recv,
):
    kinds, reads, cells = templates_ref.shape
    rows, cols = kappa_ref.shape
    blocks = ids_ref.shape[1]
    tiles = blocks // PER_TILE
    lon, lat = lax.axis_index("lon"), lax.axis_index("lat")
    chips_lon = n_lon // 2
    core, chip = lon % 2, lon // 2

    loads = [
        pltpu.make_async_copy(source, target, load_sem.at[place])
        for place, (source, target) in enumerate(
            [
                (lat_hbm, lat_ref),
                (lon_hbm, lon_ref),
                (ids_hbm, ids_ref),
                (count_hbm, count_ref),
                (noise_hbm, weights_ref),
                (readings_hbm, readings_ref),
                (templates_hbm, templates_ref),
                (kappa_hbm, kappa_ref),
                (prior_hbm, prior_ref),
            ]
        )
    ]
    for copy in loads:
        copy.start()

    me_a = lat * 2 + core
    group_a = 2 * n_lat

    def peer_a(step):
        index = (me_a + step) % group_a
        return (chip * 2 + index % 2, index // 2)

    peers_a = [peer_a(step) for step in range(1, group_a)]
    peers_b = [(((chip + step) % chips_lon) * 2 + core, lat) for step in range(1, chips_lon)]
    twin = (chip * 2 + 1 - core, lat)
    peers_far = [
        (((chip + along) % chips_lon) * 2 + core, (lat + across) % n_lat)
        for across, along in far_first(n_lat, chips_lon)
    ]
    lon_next, lon_prev = ((lon + 1) % n_lon, lat), ((lon + n_lon - 1) % n_lon, lat)
    lat_next, lat_prev = (lon, (lat + 1) % n_lat), (lon, (lat + n_lat - 1) % n_lat)

    barrier = pltpu.get_barrier_semaphore()
    peers = [lon_next, lon_prev, lat_next, lat_prev, twin] + peers_a + peers_b + peers_far
    for peer in peers:
        pl.semaphore_signal(barrier, inc=1, device_id=peer, device_id_type=MESH)

    def edges(source, kind, turn):
        pieces = [
            (source.at[pl.ds(rows - ROWS, ROWS), :], edge_lon.at[kind, turn, 0], lon_next),
            (source.at[pl.ds(0, ROWS), :], edge_lon.at[kind, turn, 1], lon_prev),
            (source.at[:, pl.ds(cols - LANES, LANES)], edge_lat.at[kind, turn, 0], lat_next),
            (source.at[:, pl.ds(0, LANES)], edge_lat.at[kind, turn, 1], lat_prev),
        ]
        return [
            pltpu.make_async_remote_copy(
                src_ref=src,
                dst_ref=dst,
                send_sem=edge_send.at[kind, turn, place],
                recv_sem=edge_recv.at[kind, turn, place],
                device_id=peer,
                device_id_type=MESH,
            )
            for place, (src, dst, peer) in enumerate(pieces)
        ]

    def sums(buffer, me, send, recv, peers):
        return [
            pltpu.make_async_remote_copy(
                src_ref=buffer.at[me],
                dst_ref=buffer.at[me],
                send_sem=send.at[step],
                recv_sem=recv.at[step],
                device_id=peer,
                device_id_type=MESH,
            )
            for step, peer in enumerate(peers)
        ]

    first_a_copies = sums(first_a, me_a, first_a_send, first_a_recv, peers_a)
    first_b_copies = sums(first_b, chip, first_b_send, first_b_recv, peers_b)
    last_a_copies = sums(last_a, core, last_a_send, last_a_recv, [twin])
    me_far = chip * n_lat + lat
    last_b_copies = sums(last_b, me_far, last_b_send, last_b_recv, peers_far)

    has_prev = (lat > 0).astype(F32)
    has_next = (lat < n_lat - 1).astype(F32)

    def neighbours(field, kind, turn):
        return shifted(
            field,
            edge_lon[kind, turn, 0],
            edge_lon[kind, turn, 1],
            edge_lat[kind, turn, 0],
            edge_lat[kind, turn, 1],
            has_prev,
            has_next,
        )

    padded_ref[...] = jnp.zeros(padded_ref.shape, F32)
    offset = lax.broadcasted_iota(jnp.int32, (PSIDE, cols), 1) - lax.broadcasted_iota(
        jnp.int32, (PSIDE, cols), 0
    )

    def one_selector(block, carry):
        start = pl.multiple_of(block * PSIDE, PSIDE)
        chosen = jnp.where(offset == lat_ref[0, block], 1.0, 0.0)
        select_ref[pl.ds(start, PSIDE), :] = chosen.astype(BF16)
        return carry

    loads[0].wait()
    lax.fori_loop(0, blocks, one_selector, 0, unroll=16)
    lane = lax.broadcasted_iota(jnp.int32, (ROWS, LANES), 1)
    chunk = lane // PSIDE
    cell = lax.broadcasted_iota(jnp.int32, (cols, LANES), 0)

    def one_turned(tile, carry):
        place = jnp.zeros((ROWS, LANES), jnp.int32)
        for block in range(PER_TILE):
            place = jnp.where(chunk == block, lat_ref[0, tile * PER_TILE + block], place)
        place = (place + lane % PSIDE)[:1]
        start = pl.multiple_of(tile * LANES, LANES)
        turned_ref[:, pl.ds(start, LANES)] = jnp.where(cell == place, 1.0, 0.0).astype(BF16)
        return carry

    lax.fori_loop(0, tiles, one_turned, 0, unroll=2)
    for copy in loads[1:6]:
        copy.wait()
    slot = lax.broadcasted_iota(jnp.int32, (blocks, reads), 0)
    weights = jnp.where(slot < count_ref[0], weights_ref[...], 0.0)
    weights_ref[...] = weights
    term_ref[...] = weights * readings_ref[...]
    ids_row = jnp.broadcast_to(ids_ref[...].astype(F32), (blocks, blocks))
    ids_rows_ref[...] = jnp.transpose(ids_row)

    def gather(field):
        high, low = split(field)
        both = jnp.dot(
            jnp.concatenate([high, low], 0), turned_ref[...], preferred_element_type=F32
        )
        both = both[:rows] + both[rows:]
        for tile in range(tiles):
            columns_ref[tile] = both[:, tile * LANES : (tile + 1) * LANES]
        for tile in range(tiles):
            halves = []
            for half in range(2):
                picked = jnp.zeros((ROWS, LANES), F32)
                for place in range(PER_TILE):
                    start = lon_ref[0, tile * PER_TILE + place] + half * ROWS
                    window = columns_ref[tile, pl.ds(start, ROWS), :]
                    picked = jnp.where(chunk == place, window, picked)
                halves.append(picked)
            done = block_transpose(jnp.stack(halves))
            for half in range(2):
                patch_ref[
                    tile * ROWS : (tile + 1) * ROWS, half * LANES : (half + 1) * LANES
                ] = done[half]

    def read():
        high, low = split(jnp.transpose(patch_ref[...]))
        patches = jnp.concatenate([high, low], 1)
        ids = jnp.broadcast_to(ids_ref[...], (ROWS, blocks))
        ids = jnp.concatenate([ids, ids], 1)
        acc = jnp.zeros((reads, 2 * blocks), F32)
        for kind in range(kinds):
            result = jnp.dot(templates_ref[kind], patches, preferred_element_type=F32)
            acc = jnp.where((ids == kind)[:1], result, acc)
        return jnp.transpose(acc[:, :blocks] + acc[:, blocks:])

    def spread(mixed):
        high, low = split(mixed)
        both = jnp.concatenate([high, low], 0)
        ids = ids_rows_ref[...].astype(BF16)
        ids = jnp.concatenate([ids, ids], 0)
        terms = jnp.zeros((2 * blocks, cells), F32)
        some = 8
        for first in range(0, kinds, some):
            left = [
                jnp.where(ids == kind, both, jnp.zeros_like(both))
                for kind in range(first, first + some)
            ]
            table = templates_ref[first : first + some].reshape(some * reads, cells)
            terms += jnp.dot(jnp.concatenate(left, 1), table, preferred_element_type=F32)
        terms = terms[:blocks] + terms[blocks:]
        lead = rows - PSIDE
        for half in range(2):
            part = terms[:, half * LANES : (half + 1) * LANES].reshape(tiles, ROWS, LANES)
            padded_ref[:, lead + half * ROWS : lead + (half + 1) * ROWS, :] = block_transpose(part)
        wide = lax.broadcasted_iota(jnp.int32, (rows, LANES), 1) // PSIDE

        def one_tile(tile, carry):
            picked = jnp.zeros((rows, LANES), F32)
            for place in range(PER_TILE):
                start = lead - lon_ref[0, tile * PER_TILE + place]
                window = padded_ref[tile, pl.ds(start, rows), :]
                picked = jnp.where(wide == place, window, picked)
            high, low = split(picked)
            start = pl.multiple_of(tile * LANES, LANES)
            spread_ref[0:rows, pl.ds(start, LANES)] = high
            spread_ref[rows : 2 * rows, pl.ds(start, LANES)] = low
            return carry

        lax.fori_loop(0, tiles, one_tile, 0, unroll=4)
        both = jnp.dot(spread_ref[...], select_ref[...], preferred_element_type=F32)
        return both[:rows] + both[rows:]

    row_at = lax.broadcasted_iota(jnp.int32, (ROWS, LANES), 0)

    def packed(parts):
        parts = [jnp.sum(part, axis=0, keepdims=True) for part in parts]
        parts += [jnp.zeros((1, LANES), F32)] * (ROWS - len(parts))
        total = jnp.sum(jnp.concatenate(parts, 0), axis=1, keepdims=True)
        return jnp.sum(jnp.where(row_at == lane, total, 0.0), axis=0, keepdims=True)

    def unpacked(total, count):
        return [
            jnp.sum(jnp.where(lane[:1] == place, total, 0.0), axis=1, keepdims=True)
            for place in range(count)
        ]

    for copy in loads[6:]:
        copy.wait()
    right = spread(term_ref[...])
    r0_ref[...] = right
    v_ref[...] = right
    pl.semaphore_wait(barrier, len(peers))

    def one_turn(turn, carry):
        v_copies = edges(v_ref, 0, turn)
        for copy in v_copies:
            copy.start()
        gather(v_ref[...])

        @pl.when(turn == 1)
        def _():
            for copy in first_a_copies:
                copy.wait_recv()
            first_b[chip] = jnp.sum(first_a[...], axis=0)
            for copy in first_b_copies:
                copy.start()

        image = read()
        mixed = weights_ref[...] * image
        term_ref[...] = mixed
        for copy in v_copies:
            copy.wait_recv()
        field = v_ref[...]
        inner = (kappa_ref[...] + 4.0) * field - neighbours(field, 0, turn)
        scaled = prior_ref[...] * inner
        u_ref[...] = scaled
        u_copies = edges(u_ref, 1, turn)
        for copy in u_copies:
            copy.start()
        curve = fold(scaled * inner) + fold(mixed * image)

        @pl.when(turn == 0)
        def _():
            first_a[me_a] = packed([fold(r0_ref[...] * r0_ref[...]), curve])
            for copy in first_a_copies:
                copy.start()

        @pl.when(turn == 2)
        def _():
            r0, w0, r1, w1 = r0_ref[...], w0_ref[...], r1_ref[...], w1_ref[...]
            pairs = [(r0, r1), (r1, r1), (r1, w1), (r0, w1), (w0, w1), (w1, w1)]
            last_a[core] = packed([fold(one * two) for one, two in pairs] + [curve])
            for copy in last_a_copies:
                copy.start()
            for copy in last_a_copies:
                copy.wait_recv()
            last_b[me_far] = jnp.sum(last_a[...], axis=0)
            for copy in last_b_copies:
                copy.start()

        observed = spread(term_ref[...])
        for copy in u_copies:
            copy.wait_recv()
        scaled = u_ref[...]
        image = (kappa_ref[...] + 4.0) * scaled - neighbours(scaled, 1, turn) + observed
        for copy in v_copies + u_copies:
            copy.wait_send()

        @pl.when(turn == 0)
        def _():
            w0_ref[...] = image
            v_ref[...] = image

        @pl.when(turn == 1)
        def _():
            for copy in first_b_copies:
                copy.wait_recv()
            norm, curve = unpacked(jnp.sum(first_b[...], axis=0), 2)
            alpha = norm / curve
            w0 = w0_ref[...]
            w1 = w0 - alpha * image
            r1_ref[...] = r0_ref[...] - alpha * w0
            w1_ref[...] = w1
            v_ref[...] = w1
            lane_row = lane[:1]
            first_ref[...] = jnp.where(lane_row == 0, alpha, jnp.where(lane_row == 1, curve, 0.0))

        @pl.when(turn == 2)
        def _():
            for copy in last_b_copies:
                copy.wait_recv()
            sizes = unpacked(jnp.sum(last_b[...], axis=0), 7)
            alpha, a = unpacked(first_ref[...], 2)
            g0, g1, d, b, c, e, f = sizes
            g2 = d
            l1, l2 = b / a, c / a
            d, e, f = d - l1 * b, e - l1 * c, f - l2 * c
            m = e / d
            f = f - m * e
            g1 = g1 - l1 * g0
            g2 = g2 - l2 * g0 - m * g1
            c2 = g2 / f
            c1 = g1 / d - m * c2
            c0 = g0 / a - l1 * c1 - l2 * c2
            w1, r1 = w1_ref[...], r1_ref[...]
            x_ref[...] = (alpha + c0) * r0_ref[...] + c1 * r1 + c2 * w1
            r_ref[...] = r1 - c0 * w0_ref[...] - c1 * w1 - c2 * image

        return carry

    lax.fori_loop(0, ITERS, one_turn, 0)
    for copy in first_a_copies + first_b_copies + last_a_copies + last_b_copies:
        copy.wait_send()


def far_first(n_lat, chips_lon):
    side = max(1, round(chips_lon**0.5))

    def away(step, size):
        return min(step, size - step)

    steps = [
        (across, along)
        for across in range(n_lat)
        for along in range(chips_lon)
        if across or along
    ]

    def distance(step):
        across, along = step
        return away(across, n_lat) + away(along // side, side) + away(along % side, side)

    return sorted(steps, key=distance, reverse=True)


def on_device(
    n_lon,
    n_lat,
    kappa_sq,
    prior_scale,
    templates,
    block_counts,
    anchor_lon,
    anchor_lat,
    template_ids,
    readings,
    noise_prec,
):
    rows, cols = kappa_sq.shape
    kinds, reads, cells = templates.shape
    blocks = template_ids.shape[1]
    tiles = blocks // PER_TILE
    group_a, chips_lon = 2 * n_lat, n_lon // 2
    chips = n_lat * chips_lon
    vmem = pl.BlockSpec(memory_space=pltpu.VMEM)
    dma = pltpu.SemaphoreType.DMA
    field = jax.ShapeDtypeStruct((rows, cols), F32)
    plane = pltpu.VMEM((rows, cols), F32)
    return pl.pallas_call(
        functools.partial(kernel, n_lon, n_lat),
        out_shape=(field, field),
        in_specs=[pl.BlockSpec(memory_space=pl.ANY)] * 9,
        out_specs=(vmem, vmem),
        scratch_shapes=[
            plane,
            plane,
            pltpu.VMEM((kinds, reads, cells), BF16),
            pltpu.SMEM((1,), jnp.int32),
            pltpu.SMEM((1, blocks), jnp.int32),
            pltpu.SMEM((1, blocks), jnp.int32),
            pltpu.VMEM((1, blocks), jnp.int32),
            pltpu.VMEM((blocks, reads), F32),
            pltpu.VMEM((blocks, reads), F32),
            pltpu.VMEM((blocks * PSIDE, cols), BF16),
            pltpu.VMEM((cols, blocks * PSIDE), BF16),
            pltpu.VMEM((tiles, rows, LANES), F32),
            pltpu.VMEM((tiles, 2 * rows - PSIDE, LANES), F32),
            pltpu.VMEM((2 * rows, blocks * PSIDE), BF16),
            pltpu.VMEM((blocks, cells), F32),
            pltpu.VMEM((blocks, blocks), F32),
            pltpu.VMEM((blocks, reads), F32),
            plane,
            plane,
            plane,
            plane,
            plane,
            plane,
            pltpu.VMEM((1, LANES), F32),
            pltpu.VMEM((2, ITERS, 2, ROWS, cols), F32),
            pltpu.VMEM((2, ITERS, 2, rows, LANES), F32),
            pltpu.VMEM((group_a, 1, LANES), F32),
            pltpu.VMEM((chips_lon, 1, LANES), F32),
            pltpu.VMEM((2, 1, LANES), F32),
            pltpu.VMEM((chips, 1, LANES), F32),
            dma((9,)),
            dma((2, ITERS, 4)),
            dma((2, ITERS, 4)),
            dma((group_a - 1,)),
            dma((group_a - 1,)),
            dma((chips_lon - 1,)),
            dma((chips_lon - 1,)),
            dma((1,)),
            dma((1,)),
            dma((chips - 1,)),
            dma((chips - 1,)),
        ],
        compiler_params=pltpu.CompilerParams(
            collective_id=0, has_side_effects=True, vmem_limit_bytes=60 * 1024 * 1024
        ),
    )(
        kappa_sq,
        prior_scale,
        templates,
        block_counts,
        anchor_lon,
        anchor_lat,
        template_ids,
        readings[0],
        noise_prec[0],
    )


def solution(mesh):
    return jax.shard_map(
        functools.partial(on_device, mesh.shape["lon"], mesh.shape["lat"]),
        mesh=mesh,
        in_specs=(
            P("lon", "lat"),
            P("lon", "lat"),
            P(),
            P(("lon", "lat")),
            P("lon", "lat"),
            P("lon", "lat"),
            P("lon", "lat"),
            P("lon", "lat", None),
            P("lon", "lat", None),
        ),
        out_specs=(P("lon", "lat"), P("lon", "lat")),
        check_vma=False,
    )
```

```python
import functools

import jax
import jax.numpy as jnp
from jax import lax
from jax.experimental import pallas as pl
from jax.experimental.pallas import tpu as pltpu
from jax.sharding import PartitionSpec as P

PSIDE = 16
ITERS = 3
TEMPLATE_PARTS = 8
LANES = 128
ROWS = 8
PER_TILE = LANES // PSIDE
F32 = jnp.float32
BF16 = jnp.bfloat16
MESH = pl.DeviceIdType.MESH


def split(value):
    high = value.astype(BF16)
    low = (value - high.astype(F32)).astype(BF16)
    return high, low


def block_transpose(value):
    row = lax.broadcasted_iota(jnp.int32, value.shape, 1)
    chunk = lax.broadcasted_iota(jnp.int32, value.shape, 2) // PSIDE
    for k in (4, 2, 1):
        row_bit = (row // k) % 2
        chunk_bit = (chunk // k) % 2
        ahead = pltpu.roll(pltpu.roll(value, ROWS - k, 1), PSIDE * k, 2)
        if k == 4:
            other = ahead
        else:
            behind = pltpu.roll(pltpu.roll(value, k, 1), LANES - PSIDE * k, 2)
            other = jnp.where(row_bit == 0, ahead, behind)
        value = jnp.where(row_bit == chunk_bit, value, other)
    return value


def fold(value):
    total = jnp.sum(value.reshape(value.shape[0] // ROWS, ROWS, value.shape[1]), axis=0)
    parts = [total[:, i : i + LANES] for i in range(0, total.shape[1], LANES)]
    return functools.reduce(jnp.add, parts)


def shifted(field, prev_lon, next_lon, prev_lat, next_lat, has_prev, has_next):
    rows, cols = field.shape
    row = lax.broadcasted_iota(jnp.int32, field.shape, 0)
    lane = lax.broadcasted_iota(jnp.int32, prev_lat.shape, 1)
    west = jnp.where(row == 0, prev_lon[ROWS - 1 : ROWS, :], pltpu.roll(field, 1, 0))
    east = jnp.where(row == rows - 1, next_lon[0:1, :], pltpu.roll(field, rows - 1, 0))
    south = pltpu.roll(field, 1, 1)
    north = pltpu.roll(field, cols - 1, 1)
    first = jnp.where(lane == 0, pltpu.roll(prev_lat, 1, 1) * has_prev, south[:, :LANES])
    last = jnp.where(
        lane == LANES - 1, pltpu.roll(next_lat, LANES - 1, 1) * has_next, north[:, cols - LANES :]
    )
    south = jnp.concatenate([first, south[:, LANES:]], 1)
    north = jnp.concatenate([north[:, : cols - LANES], last], 1)
    return west + east + south + north


def kernel(
    n_lon,
    n_lat,
    kappa_hbm,
    prior_hbm,
    templates_hbm,
    count_hbm,
    lon_hbm,
    lat_hbm,
    ids_hbm,
    readings_hbm,
    noise_hbm,
    x_ref,
    r_ref,
    kappa_ref,
    prior_ref,
    templates_ref,
    count_ref,
    lon_ref,
    lat_ref,
    ids_ref,
    readings_ref,
    weights_ref,
    select_ref,
    turned_ref,
    columns_ref,
    padded_ref,
    spread_ref,
    patch_ref,
    ids_rows_ref,
    term_ref,
    r0_ref,
    w0_ref,
    r1_ref,
    w1_ref,
    image_ref,
    v_ref,
    u_ref,
    first_ref,
    edge_lon,
    edge_lat,
    first_a,
    first_b,
    last_a,
    last_b,
    load_sem,
    edge_send,
    edge_recv,
    first_a_send,
    first_a_recv,
    first_b_send,
    first_b_recv,
    last_a_send,
    last_a_recv,
    last_b_send,
    last_b_recv,
):
    kinds, reads, cells = templates_ref.shape
    rows, cols = kappa_ref.shape
    blocks = ids_ref.shape[1]
    tiles = blocks // PER_TILE
    lon, lat = lax.axis_index("lon"), lax.axis_index("lat")
    chips_lon = n_lon // 2
    core, chip = lon % 2, lon // 2

    part = kinds // TEMPLATE_PARTS
    loads = [
        pltpu.make_async_copy(source, target, load_sem.at[place])
        for place, (source, target) in enumerate(
            [
                (lat_hbm, lat_ref),
                (lon_hbm, lon_ref),
                (ids_hbm, ids_ref),
                (count_hbm, count_ref),
                (noise_hbm, weights_ref),
                (readings_hbm, readings_ref),
            ]
            + [
                (templates_hbm.at[pl.ds(i * part, part)], templates_ref.at[pl.ds(i * part, part)])
                for i in range(TEMPLATE_PARTS)
            ]
            + [
                (kappa_hbm, kappa_ref),
                (prior_hbm, prior_ref),
            ]
        )
    ]
    for copy in loads:
        copy.start()

    me_a = lat * 2 + core
    group_a = 2 * n_lat

    def peer_a(step):
        index = (me_a + step) % group_a
        return (chip * 2 + index % 2, index // 2)

    peers_a = [peer_a(step) for step in range(1, group_a)]
    peers_b = [(((chip + step) % chips_lon) * 2 + core, lat) for step in range(1, chips_lon)]
    twin = (chip * 2 + 1 - core, lat)
    peers_far = [
        (((chip + along) % chips_lon) * 2 + core, (lat + across) % n_lat)
        for across, along in far_first(n_lat, chips_lon)
    ]
    lon_next, lon_prev = ((lon + 1) % n_lon, lat), ((lon + n_lon - 1) % n_lon, lat)
    lat_next, lat_prev = (lon, (lat + 1) % n_lat), (lon, (lat + n_lat - 1) % n_lat)

    barrier = pltpu.get_barrier_semaphore()
    peers = [lon_next, lon_prev, lat_next, lat_prev] + peers_a + peers_b
    for peer in peers:
        pl.semaphore_signal(barrier, inc=1, device_id=peer, device_id_type=MESH)

    def edges(source, kind, turn):
        pieces = [
            (source.at[pl.ds(rows - ROWS, ROWS), :], edge_lon.at[kind, turn, 0], lon_next),
            (source.at[pl.ds(0, ROWS), :], edge_lon.at[kind, turn, 1], lon_prev),
            (source.at[:, pl.ds(cols - LANES, LANES)], edge_lat.at[kind, turn, 0], lat_next),
            (source.at[:, pl.ds(0, LANES)], edge_lat.at[kind, turn, 1], lat_prev),
        ]
        return [
            pltpu.make_async_remote_copy(
                src_ref=src,
                dst_ref=dst,
                send_sem=edge_send.at[kind, turn, place],
                recv_sem=edge_recv.at[kind, turn, place],
                device_id=peer,
                device_id_type=MESH,
            )
            for place, (src, dst, peer) in enumerate(pieces)
        ]

    def sums(buffer, me, send, recv, peers):
        return [
            pltpu.make_async_remote_copy(
                src_ref=buffer.at[me],
                dst_ref=buffer.at[me],
                send_sem=send.at[step],
                recv_sem=recv.at[step],
                device_id=peer,
                device_id_type=MESH,
            )
            for step, peer in enumerate(peers)
        ]

    first_a_copies = sums(first_a, me_a, first_a_send, first_a_recv, peers_a)
    first_b_copies = sums(first_b, chip, first_b_send, first_b_recv, peers_b)
    last_a_copies = sums(last_a, core, last_a_send, last_a_recv, [twin])
    me_far = chip * n_lat + lat
    last_b_copies = sums(last_b, me_far, last_b_send, last_b_recv, peers_far)

    has_prev = (lat > 0).astype(F32)
    has_next = (lat < n_lat - 1).astype(F32)

    def neighbours(field, kind, turn):
        return shifted(
            field,
            edge_lon[kind, turn, 0],
            edge_lon[kind, turn, 1],
            edge_lat[kind, turn, 0],
            edge_lat[kind, turn, 1],
            has_prev,
            has_next,
        )

    padded_ref[...] = jnp.zeros(padded_ref.shape, F32)
    offset = lax.broadcasted_iota(jnp.int32, (PSIDE, cols), 1) - lax.broadcasted_iota(
        jnp.int32, (PSIDE, cols), 0
    )

    def one_selector(block, carry):
        start = pl.multiple_of(block * PSIDE, PSIDE)
        chosen = jnp.where(offset == lat_ref[0, block], 1.0, 0.0)
        select_ref[pl.ds(start, PSIDE), :] = chosen.astype(BF16)
        return carry

    loads[0].wait()
    lax.fori_loop(0, blocks, one_selector, 0, unroll=16)
    lane = lax.broadcasted_iota(jnp.int32, (ROWS, LANES), 1)
    chunk = lane // PSIDE
    cell = lax.broadcasted_iota(jnp.int32, (cols, LANES), 0)

    def one_turned(tile, carry):
        place = jnp.zeros((ROWS, LANES), jnp.int32)
        for block in range(PER_TILE):
            place = jnp.where(chunk == block, lat_ref[0, tile * PER_TILE + block], place)
        place = (place + lane % PSIDE)[:1]
        start = pl.multiple_of(tile * LANES, LANES)
        turned_ref[:, pl.ds(start, LANES)] = jnp.where(cell == place, 1.0, 0.0).astype(BF16)
        return carry

    lax.fori_loop(0, tiles, one_turned, 0, unroll=2)
    for copy in loads[1:6]:
        copy.wait()
    slot = lax.broadcasted_iota(jnp.int32, (blocks, reads), 0)
    weights = jnp.where(slot < count_ref[0], weights_ref[...], 0.0)
    weights_ref[...] = weights
    term_ref[...] = weights * readings_ref[...]
    ids_row = jnp.broadcast_to(ids_ref[...].astype(F32), (blocks, blocks))
    ids_rows_ref[...] = jnp.transpose(ids_row)

    def gather(field):
        high, low = split(field)
        both = jnp.dot(
            jnp.concatenate([high, low], 0), turned_ref[...], preferred_element_type=F32
        )
        both = both[:rows] + both[rows:]
        for tile in range(tiles):
            columns_ref[tile] = both[:, tile * LANES : (tile + 1) * LANES]
        for tile in range(tiles):
            halves = []
            for half in range(2):
                picked = jnp.zeros((ROWS, LANES), F32)
                for place in range(PER_TILE):
                    start = lon_ref[0, tile * PER_TILE + place] + half * ROWS
                    window = columns_ref[tile, pl.ds(start, ROWS), :]
                    picked = jnp.where(chunk == place, window, picked)
                halves.append(picked)
            done = block_transpose(jnp.stack(halves))
            for half in range(2):
                patch_ref[
                    tile * ROWS : (tile + 1) * ROWS, half * LANES : (half + 1) * LANES
                ] = done[half]

    def read():
        high, low = split(jnp.transpose(patch_ref[...]))
        patches = jnp.concatenate([high, low], 1)
        ids = jnp.broadcast_to(ids_ref[...], (ROWS, blocks))
        ids = jnp.concatenate([ids, ids], 1)
        acc = jnp.zeros((reads, 2 * blocks), F32)
        for kind in range(kinds):
            result = jnp.dot(templates_ref[kind], patches, preferred_element_type=F32)
            acc = jnp.where((ids == kind)[:1], result, acc)
        return jnp.transpose(acc[:, :blocks] + acc[:, blocks:])

    def spread(mixed):
        high, low = split(mixed)
        both = jnp.concatenate([high, low], 0)
        ids = ids_rows_ref[...].astype(BF16)
        ids = jnp.concatenate([ids, ids], 0)
        terms = jnp.zeros((2 * blocks, cells), F32)
        some = 8
        for first in range(0, kinds, some):
            left = [
                jnp.where(ids == kind, both, jnp.zeros_like(both))
                for kind in range(first, first + some)
            ]
            table = templates_ref[first : first + some].reshape(some * reads, cells)
            terms += jnp.dot(jnp.concatenate(left, 1), table, preferred_element_type=F32)
        terms = terms[:blocks] + terms[blocks:]
        lead = rows - PSIDE
        for half in range(2):
            part = terms[:, half * LANES : (half + 1) * LANES].reshape(tiles, ROWS, LANES)
            padded_ref[:, lead + half * ROWS : lead + (half + 1) * ROWS, :] = block_transpose(part)
        wide = lax.broadcasted_iota(jnp.int32, (rows, LANES), 1) // PSIDE

        def one_tile(tile, carry):
            picked = jnp.zeros((rows, LANES), F32)
            for place in range(PER_TILE):
                start = lead - lon_ref[0, tile * PER_TILE + place]
                window = padded_ref[tile, pl.ds(start, rows), :]
                picked = jnp.where(wide == place, window, picked)
            high, low = split(picked)
            start = pl.multiple_of(tile * LANES, LANES)
            spread_ref[0:rows, pl.ds(start, LANES)] = high
            spread_ref[rows : 2 * rows, pl.ds(start, LANES)] = low
            return carry

        lax.fori_loop(0, tiles, one_tile, 0, unroll=tiles)
        both = jnp.dot(spread_ref[...], select_ref[...], preferred_element_type=F32)
        return both[:rows] + both[rows:]

    row_at = lax.broadcasted_iota(jnp.int32, (ROWS, LANES), 0)

    def packed(parts):
        parts = [jnp.sum(part, axis=0, keepdims=True) for part in parts]
        parts += [jnp.zeros((1, LANES), F32)] * (ROWS - len(parts))
        total = jnp.sum(jnp.concatenate(parts, 0), axis=1, keepdims=True)
        return jnp.sum(jnp.where(row_at == lane, total, 0.0), axis=0, keepdims=True)

    def unpacked(total, count):
        return [
            jnp.sum(jnp.where(lane[:1] == place, total, 0.0), axis=1, keepdims=True)
            for place in range(count)
        ]

    for copy in loads[6:]:
        copy.wait()

    def one_turn(turn, carry):
        image_ref[...] = spread(term_ref[...])

        @pl.when(turn > 0)
        def _():
            v_copies, u_copies = edges(v_ref, 0, turn - 1), edges(u_ref, 1, turn - 1)
            for copy in u_copies:
                copy.wait_recv()
            scaled = u_ref[...]
            around = neighbours(scaled, 1, turn - 1)
            image_ref[...] += (kappa_ref[...] + 4.0) * scaled - around
            for copy in v_copies + u_copies:
                copy.wait_send()

        @pl.when(turn == 0)
        def _():
            right = image_ref[...]
            r0_ref[...] = right
            v_ref[...] = right
            pl.semaphore_wait(barrier, len(peers))

        @pl.when(turn == 1)
        def _():
            image = image_ref[...]
            w0_ref[...] = image
            v_ref[...] = image

        @pl.when(turn == 2)
        def _():
            for copy in first_b_copies:
                copy.wait_recv()
            norm, curve = unpacked(jnp.sum(first_b[...], axis=0), 2)
            alpha = norm / curve
            w0 = w0_ref[...]
            w1 = w0 - alpha * image_ref[...]
            r1_ref[...] = r0_ref[...] - alpha * w0
            w1_ref[...] = w1
            v_ref[...] = w1
            lane_row = lane[:1]
            first_ref[...] = jnp.where(lane_row == 0, alpha, jnp.where(lane_row == 1, curve, 0.0))

        @pl.when(turn == ITERS)
        def _():
            for copy in last_b_copies:
                copy.wait_recv()
            sizes = unpacked(jnp.sum(last_b[...], axis=0), 7)
            alpha, a = unpacked(first_ref[...], 2)
            g0, g1, d, b, c, e, f = sizes
            g2 = d
            l1, l2 = b / a, c / a
            d, e, f = d - l1 * b, e - l1 * c, f - l2 * c
            m = e / d
            f = f - m * e
            g1 = g1 - l1 * g0
            g2 = g2 - l2 * g0 - m * g1
            c2 = g2 / f
            c1 = g1 / d - m * c2
            c0 = g0 / a - l1 * c1 - l2 * c2
            w1, r1 = w1_ref[...], r1_ref[...]
            x_ref[...] = (alpha + c0) * r0_ref[...] + c1 * r1 + c2 * w1
            r_ref[...] = r1 - c0 * w0_ref[...] - c1 * w1 - c2 * image_ref[...]

        @pl.when(turn < ITERS)
        def _():
            v_copies, u_copies = edges(v_ref, 0, turn), edges(u_ref, 1, turn)
            for copy in v_copies:
                copy.start()
            gather(v_ref[...])

            @pl.when(turn == 1)
            def _():
                for copy in first_a_copies:
                    copy.wait_recv()
                first_b[chip] = jnp.sum(first_a[...], axis=0)
                for copy in first_b_copies:
                    copy.start()

            image = read()
            mixed = weights_ref[...] * image
            term_ref[...] = mixed
            for copy in v_copies:
                copy.wait_recv()
            field = v_ref[...]
            inner = (kappa_ref[...] + 4.0) * field - neighbours(field, 0, turn)
            scaled = prior_ref[...] * inner
            u_ref[...] = scaled
            for copy in u_copies:
                copy.start()
            curve = fold(scaled * inner) + fold(mixed * image)

            @pl.when(turn == 0)
            def _():
                first_a[me_a] = packed([fold(r0_ref[...] * r0_ref[...]), curve])
                for copy in first_a_copies:
                    copy.start()

            @pl.when(turn == 2)
            def _():
                r0, w0, r1, w1 = r0_ref[...], w0_ref[...], r1_ref[...], w1_ref[...]
                pairs = [(r0, r1), (r1, r1), (r1, w1), (r0, w1), (w0, w1), (w1, w1)]
                last_a[core] = packed([fold(one * two) for one, two in pairs] + [curve])
                for copy in last_a_copies:
                    copy.start()
                for copy in last_a_copies:
                    copy.wait_recv()
                last_b[me_far] = jnp.sum(last_a[...], axis=0)
                for copy in last_b_copies:
                    copy.start()

        return carry

    lax.fori_loop(0, ITERS + 1, one_turn, 0)
    for copy in first_a_copies + first_b_copies + last_a_copies + last_b_copies:
        copy.wait_send()


def far_first(n_lat, chips_lon):
    side = max(1, round(chips_lon**0.5))

    def away(step, size):
        return min(step, size - step)

    steps = [
        (across, along)
        for across in range(n_lat)
        for along in range(chips_lon)
        if across or along
    ]

    def distance(step):
        across, along = step
        return away(across, n_lat) + away(along // side, side) + away(along % side, side)

    return sorted(steps, key=distance, reverse=True)


def hand_out(x_in, r_in, x_out, r_out, sem):
    copies = [
        pltpu.make_async_copy(x_in, x_out, sem.at[0]),
        pltpu.make_async_copy(r_in, r_out, sem.at[1]),
    ]
    for copy in copies:
        copy.start()
    for copy in copies:
        copy.wait()


def on_device(
    n_lon,
    n_lat,
    kappa_sq,
    prior_scale,
    templates,
    block_counts,
    anchor_lon,
    anchor_lat,
    template_ids,
    readings,
    noise_prec,
):
    rows, cols = kappa_sq.shape
    kinds, reads, cells = templates.shape
    blocks = template_ids.shape[1]
    tiles = blocks // PER_TILE
    group_a, chips_lon = 2 * n_lat, n_lon // 2
    chips = n_lat * chips_lon
    vmem = pl.BlockSpec(memory_space=pltpu.VMEM)
    dma = pltpu.SemaphoreType.DMA
    field = jax.ShapeDtypeStruct((rows, cols), F32)
    plane = pltpu.VMEM((rows, cols), F32)
    fields = pl.pallas_call(
        functools.partial(kernel, n_lon, n_lat),
        out_shape=(pltpu.VMEM((rows, cols), F32), pltpu.VMEM((rows, cols), F32)),
        in_specs=[pl.BlockSpec(memory_space=pl.ANY)] * 9,
        out_specs=(vmem, vmem),
        scratch_shapes=[
            plane,
            plane,
            pltpu.VMEM((kinds, reads, cells), BF16),
            pltpu.SMEM((1,), jnp.int32),
            pltpu.SMEM((1, blocks), jnp.int32),
            pltpu.SMEM((1, blocks), jnp.int32),
            pltpu.VMEM((1, blocks), jnp.int32),
            pltpu.VMEM((blocks, reads), F32),
            pltpu.VMEM((blocks, reads), F32),
            pltpu.VMEM((blocks * PSIDE, cols), BF16),
            pltpu.VMEM((cols, blocks * PSIDE), BF16),
            pltpu.VMEM((tiles, rows, LANES), F32),
            pltpu.VMEM((tiles, 2 * rows - PSIDE, LANES), F32),
            pltpu.VMEM((2 * rows, blocks * PSIDE), BF16),
            pltpu.VMEM((blocks, cells), F32),
            pltpu.VMEM((blocks, blocks), F32),
            pltpu.VMEM((blocks, reads), F32),
            plane,
            plane,
            plane,
            plane,
            plane,
            plane,
            plane,
            pltpu.VMEM((1, LANES), F32),
            pltpu.VMEM((2, ITERS, 2, ROWS, cols), F32),
            pltpu.VMEM((2, ITERS, 2, rows, LANES), F32),
            pltpu.VMEM((group_a, 1, LANES), F32),
            pltpu.VMEM((chips_lon, 1, LANES), F32),
            pltpu.VMEM((2, 1, LANES), F32),
            pltpu.VMEM((chips, 1, LANES), F32),
            dma((8 + TEMPLATE_PARTS,)),
            dma((2, ITERS, 4)),
            dma((2, ITERS, 4)),
            dma((group_a - 1,)),
            dma((group_a - 1,)),
            dma((chips_lon - 1,)),
            dma((chips_lon - 1,)),
            dma((1,)),
            dma((1,)),
            dma((chips - 1,)),
            dma((chips - 1,)),
        ],
        compiler_params=pltpu.CompilerParams(
            collective_id=0, has_side_effects=True, vmem_limit_bytes=56 * 1024 * 1024
        ),
    )(
        kappa_sq,
        prior_scale,
        templates,
        block_counts,
        anchor_lon,
        anchor_lat,
        template_ids,
        readings[0],
        noise_prec[0],
    )
    return pl.pallas_call(
        hand_out,
        out_shape=(field, field),
        in_specs=[vmem, vmem],
        out_specs=(pl.BlockSpec(memory_space=pl.ANY),) * 2,
        scratch_shapes=[dma((2,))],
    )(*fields)


def solution(mesh):
    return jax.shard_map(
        functools.partial(on_device, mesh.shape["lon"], mesh.shape["lat"]),
        mesh=mesh,
        in_specs=(
            P("lon", "lat"),
            P("lon", "lat"),
            P(),
            P(("lon", "lat")),
            P("lon", "lat"),
            P("lon", "lat"),
            P("lon", "lat"),
            P("lon", "lat", None),
            P("lon", "lat", None),
        ),
        out_specs=(P("lon", "lat"), P("lon", "lat")),
        check_vma=False,
    )
```

```python
import functools

import jax
import jax.numpy as jnp
from jax import lax
from jax.experimental import pallas as pl
from jax.experimental.pallas import tpu as pltpu
from jax.sharding import PartitionSpec as P

PSIDE = 16
ITERS = 3
TEMPLATE_PARTS = 8
LANES = 128
ROWS = 8
PER_TILE = LANES // PSIDE
F32 = jnp.float32
BF16 = jnp.bfloat16
MESH = pl.DeviceIdType.MESH


def split(value):
    high = value.astype(BF16)
    low = (value - high.astype(F32)).astype(BF16)
    return high, low


def block_transpose(value):
    row = lax.broadcasted_iota(jnp.int32, value.shape, 1)
    chunk = lax.broadcasted_iota(jnp.int32, value.shape, 2) // PSIDE
    for k in (4, 2, 1):
        row_bit = (row // k) % 2
        chunk_bit = (chunk // k) % 2
        ahead = pltpu.roll(pltpu.roll(value, ROWS - k, 1), PSIDE * k, 2)
        if k == 4:
            other = ahead
        else:
            behind = pltpu.roll(pltpu.roll(value, k, 1), LANES - PSIDE * k, 2)
            other = jnp.where(row_bit == 0, ahead, behind)
        value = jnp.where(row_bit == chunk_bit, value, other)
    return value


def fold(value):
    total = jnp.sum(value.reshape(value.shape[0] // ROWS, ROWS, value.shape[1]), axis=0)
    parts = [total[:, i : i + LANES] for i in range(0, total.shape[1], LANES)]
    return functools.reduce(jnp.add, parts)


def to_row(column):
    wide = jnp.broadcast_to(column, (column.shape[0], LANES))
    row = lax.broadcasted_iota(jnp.int32, wide.shape, 0)
    lane = lax.broadcasted_iota(jnp.int32, wide.shape, 1)
    return jnp.sum(jnp.where(row == lane, wide, 0.0), axis=0, keepdims=True)


def to_column(row_value, rows):
    wide = jnp.broadcast_to(row_value, (rows, LANES))
    row = lax.broadcasted_iota(jnp.int32, wide.shape, 0)
    lane = lax.broadcasted_iota(jnp.int32, wide.shape, 1)
    return jnp.sum(jnp.where(row == lane, wide, 0.0), axis=1, keepdims=True)


def shifted(field, prev_lon, next_lon, prev_lat, next_lat):
    rows, cols = field.shape
    row = lax.broadcasted_iota(jnp.int32, field.shape, 0)
    lane = lax.broadcasted_iota(jnp.int32, (rows, LANES), 1)
    west = jnp.where(row == 0, prev_lon, pltpu.roll(field, 1, 0))
    east = jnp.where(row == rows - 1, next_lon, pltpu.roll(field, rows - 1, 0))
    south = pltpu.roll(field, 1, 1)
    north = pltpu.roll(field, cols - 1, 1)
    first = jnp.where(lane == 0, prev_lat, south[:, :LANES])
    last = jnp.where(lane == LANES - 1, next_lat, north[:, cols - LANES :])
    south = jnp.concatenate([first, south[:, LANES:]], 1)
    north = jnp.concatenate([north[:, : cols - LANES], last], 1)
    return west + east + south + north


def kernel(
    n_lon,
    n_lat,
    kappa_hbm,
    prior_hbm,
    templates_hbm,
    count_hbm,
    lon_hbm,
    lat_hbm,
    ids_hbm,
    readings_hbm,
    noise_hbm,
    x_ref,
    r_ref,
    kappa_ref,
    prior_ref,
    templates_ref,
    count_ref,
    lon_ref,
    lat_ref,
    ids_ref,
    readings_ref,
    weights_ref,
    select_ref,
    turned_ref,
    columns_ref,
    padded_ref,
    spread_ref,
    patch_ref,
    ids_rows_ref,
    term_ref,
    r0_ref,
    w0_ref,
    r1_ref,
    w1_ref,
    image_ref,
    v_ref,
    u_ref,
    first_ref,
    curve_ref,
    out_lon,
    out_lat,
    out_corner,
    edge_lon,
    edge_lat,
    edge_corner,
    first_a,
    first_b,
    last_a,
    last_b,
    load_sem,
    edge_send,
    edge_recv,
    first_a_send,
    first_a_recv,
    first_b_send,
    first_b_recv,
    last_a_send,
    last_a_recv,
    last_b_send,
    last_b_recv,
):
    kinds, reads, cells = templates_ref.shape
    rows, cols = kappa_ref.shape
    blocks = ids_ref.shape[1]
    tiles = blocks // PER_TILE
    lon, lat = lax.axis_index("lon"), lax.axis_index("lat")
    chips_lon = n_lon // 2
    core, chip = lon % 2, lon // 2

    part = kinds // TEMPLATE_PARTS
    loads = [
        pltpu.make_async_copy(source, target, load_sem.at[place])
        for place, (source, target) in enumerate(
            [
                (lat_hbm, lat_ref),
                (lon_hbm, lon_ref),
                (ids_hbm, ids_ref),
                (count_hbm, count_ref),
                (noise_hbm, weights_ref),
                (readings_hbm, readings_ref),
            ]
            + [
                (templates_hbm.at[pl.ds(i * part, part)], templates_ref.at[pl.ds(i * part, part)])
                for i in range(TEMPLATE_PARTS)
            ]
            + [
                (kappa_hbm, kappa_ref),
                (prior_hbm, prior_ref),
            ]
        )
    ]
    for copy in loads:
        copy.start()

    me_a = lat * 2 + core
    group_a = 2 * n_lat

    def peer_a(step):
        index = (me_a + step) % group_a
        return (chip * 2 + index % 2, index // 2)

    peers_a = [peer_a(step) for step in range(1, group_a)]
    peers_b = [(((chip + step) % chips_lon) * 2 + core, lat) for step in range(1, chips_lon)]
    twin = (chip * 2 + 1 - core, lat)
    peers_far = [
        (((chip + along) % chips_lon) * 2 + core, (lat + across) % n_lat)
        for across, along in far_first(n_lat, chips_lon)
    ]
    lon_next, lon_prev = ((lon + 1) % n_lon, lat), ((lon + n_lon - 1) % n_lon, lat)
    lat_next, lat_prev = (lon, (lat + 1) % n_lat), (lon, (lat + n_lat - 1) % n_lat)
    corners = [(one[0], two[1]) for one in (lon_next, lon_prev) for two in (lat_next, lat_prev)]

    barrier = pltpu.get_barrier_semaphore()
    peers = [lon_next, lon_prev, lat_next, lat_prev] + corners + peers_a + peers_b
    for peer in peers:
        pl.semaphore_signal(barrier, inc=1, device_id=peer, device_id_type=MESH)

    def pack_vector(field):
        out_lon[0, 0, 0] = field[rows - 1 : rows, :]
        out_lon[0, 0, 1] = field[rows - 2 : rows - 1, :]
        out_lon[0, 1, 0] = field[0:1, :]
        out_lon[0, 1, 1] = field[1:2, :]
        out_lat[0, 0, 0] = to_row(field[:, cols - 1 : cols])
        out_lat[0, 0, 1] = to_row(field[:, cols - 2 : cols - 1])
        out_lat[0, 1, 0] = to_row(field[:, 0:1])
        out_lat[0, 1, 1] = to_row(field[:, 1:2])
        for place, (row, col) in enumerate([(rows - 1, cols - 1), (rows - 1, 0), (0, cols - 1), (0, 0)]):
            value = field[row : row + 1, col : col + 1]
            out_corner[place] = jnp.broadcast_to(value, (1, LANES))

    def pack_coefficients(kappa, prior):
        for place, field in enumerate((kappa, prior)):
            out_lon[1, 0, place] = field[rows - 1 : rows, :]
            out_lon[1, 1, place] = field[0:1, :]
            out_lat[1, 0, place] = to_row(field[:, cols - 1 : cols])
            out_lat[1, 1, place] = to_row(field[:, 0:1])

    def remote(src, dst, slot, place, peer):
        return pltpu.make_async_remote_copy(
            src_ref=src,
            dst_ref=dst,
            send_sem=edge_send.at[slot, place],
            recv_sem=edge_recv.at[slot, place],
            device_id=peer,
            device_id_type=MESH,
        )

    def sides(kind, slot):
        return [
            remote(out_lon.at[kind, 0], edge_lon.at[slot, 0], slot, 0, lon_next),
            remote(out_lon.at[kind, 1], edge_lon.at[slot, 1], slot, 1, lon_prev),
            remote(out_lat.at[kind, 0], edge_lat.at[slot, 0], slot, 2, lat_next),
            remote(out_lat.at[kind, 1], edge_lat.at[slot, 1], slot, 3, lat_prev),
        ]

    def diagonals(slot):
        return [
            remote(out_corner.at[place], edge_corner.at[slot, place], slot, 4 + place, peer)
            for place, peer in enumerate(corners)
        ]

    coefficient_copies = sides(1, ITERS)

    def sums(buffer, me, send, recv, peers):
        return [
            pltpu.make_async_remote_copy(
                src_ref=buffer.at[me],
                dst_ref=buffer.at[me],
                send_sem=send.at[step],
                recv_sem=recv.at[step],
                device_id=peer,
                device_id_type=MESH,
            )
            for step, peer in enumerate(peers)
        ]

    first_a_copies = sums(first_a, me_a, first_a_send, first_a_recv, peers_a)
    first_b_copies = sums(first_b, chip, first_b_send, first_b_recv, peers_b)
    last_a_copies = sums(last_a, core, last_a_send, last_a_recv, [twin])
    me_far = chip * n_lat + lat
    last_b_copies = sums(last_b, me_far, last_b_send, last_b_recv, peers_far)

    has_prev = (lat > 0).astype(F32)
    has_next = (lat < n_lat - 1).astype(F32)

    def inner_stencil(turn):
        field = v_ref[...]
        around = shifted(
            field,
            edge_lon[turn, 0, 0],
            edge_lon[turn, 1, 0],
            to_column(edge_lat[turn, 0, 0] * has_prev, rows),
            to_column(edge_lat[turn, 1, 0] * has_next, rows),
        )
        inner = (kappa_ref[...] + 4.0) * field - around
        scaled = prior_ref[...] * inner
        u_ref[...] = scaled
        return inner, scaled

    def outer_stencil(turn):
        lane_wide = lax.broadcasted_iota(jnp.int32, (1, cols), 1)
        lane_row = lax.broadcasted_iota(jnp.int32, (1, LANES), 1)
        present = (has_prev, has_next)
        beside_lon, beside_lat = [], []
        for side, at in ((0, 0), (1, rows - 1)):
            near, far = edge_lon[turn, side, 0], edge_lon[turn, side, 1]
            kappa, prior = edge_lon[ITERS, side, 0], edge_lon[ITERS, side, 1]
            first = edge_corner[turn, 2 * side][:, :1] * has_prev
            last = edge_corner[turn, 2 * side + 1][:, :1] * has_next
            south = jnp.where(lane_wide == 0, first, pltpu.roll(near, 1, 1))
            north = jnp.where(lane_wide == cols - 1, last, pltpu.roll(near, cols - 1, 1))
            around = far + v_ref[at : at + 1, :] + south + north
            beside_lon.append(prior * ((kappa + 4.0) * near - around))
        for side in (0, 1):
            near, far = edge_lat[turn, side, 0], edge_lat[turn, side, 1]
            kappa, prior = edge_lat[ITERS, side, 0], edge_lat[ITERS, side, 1]
            first, last = edge_corner[turn, side][:, :1], edge_corner[turn, 2 + side][:, :1]
            west = jnp.where(lane_row == 0, first, pltpu.roll(near, 1, 1))
            east = jnp.where(lane_row == rows - 1, last, pltpu.roll(near, LANES - 1, 1))
            around = far + out_lat[0, 1 - side, 0] + west + east
            value = prior * ((kappa + 4.0) * near - around) * present[side]
            beside_lat.append(to_column(value, rows))
        scaled = u_ref[...]
        return (kappa_ref[...] + 4.0) * scaled - shifted(scaled, *beside_lon, *beside_lat)

    padded_ref[...] = jnp.zeros(padded_ref.shape, F32)
    offset = lax.broadcasted_iota(jnp.int32, (PSIDE, cols), 1) - lax.broadcasted_iota(
        jnp.int32, (PSIDE, cols), 0
    )

    def one_selector(block, carry):
        start = pl.multiple_of(block * PSIDE, PSIDE)
        chosen = jnp.where(offset == lat_ref[0, block], 1.0, 0.0)
        select_ref[pl.ds(start, PSIDE), :] = chosen.astype(BF16)
        return carry

    loads[0].wait()
    lax.fori_loop(0, blocks, one_selector, 0, unroll=16)
    lane = lax.broadcasted_iota(jnp.int32, (ROWS, LANES), 1)
    chunk = lane // PSIDE
    cell = lax.broadcasted_iota(jnp.int32, (cols, LANES), 0)

    def one_turned(tile, carry):
        place = jnp.zeros((ROWS, LANES), jnp.int32)
        for block in range(PER_TILE):
            place = jnp.where(chunk == block, lat_ref[0, tile * PER_TILE + block], place)
        place = (place + lane % PSIDE)[:1]
        start = pl.multiple_of(tile * LANES, LANES)
        turned_ref[:, pl.ds(start, LANES)] = jnp.where(cell == place, 1.0, 0.0).astype(BF16)
        return carry

    lax.fori_loop(0, tiles, one_turned, 0, unroll=2)
    for copy in loads[1:6]:
        copy.wait()
    slot = lax.broadcasted_iota(jnp.int32, (blocks, reads), 0)
    weights = jnp.where(slot < count_ref[0], weights_ref[...], 0.0)
    weights_ref[...] = weights
    term_ref[...] = weights * readings_ref[...]
    ids_row = jnp.broadcast_to(ids_ref[...].astype(F32), (blocks, blocks))
    ids_rows_ref[...] = jnp.transpose(ids_row)

    def gather(field):
        high, low = split(field)
        both = jnp.dot(
            jnp.concatenate([high, low], 0), turned_ref[...], preferred_element_type=F32
        )
        both = both[:rows] + both[rows:]
        for tile in range(tiles):
            columns_ref[tile] = both[:, tile * LANES : (tile + 1) * LANES]
        for tile in range(tiles):
            halves = []
            for half in range(2):
                picked = jnp.zeros((ROWS, LANES), F32)
                for place in range(PER_TILE):
                    start = lon_ref[0, tile * PER_TILE + place] + half * ROWS
                    window = columns_ref[tile, pl.ds(start, ROWS), :]
                    picked = jnp.where(chunk == place, window, picked)
                halves.append(picked)
            done = block_transpose(jnp.stack(halves))
            for half in range(2):
                patch_ref[
                    tile * ROWS : (tile + 1) * ROWS, half * LANES : (half + 1) * LANES
                ] = done[half]

    def read():
        high, low = split(jnp.transpose(patch_ref[...]))
        patches = jnp.concatenate([high, low], 1)
        ids = jnp.broadcast_to(ids_ref[...], (ROWS, blocks))
        ids = jnp.concatenate([ids, ids], 1)
        acc = jnp.zeros((reads, 2 * blocks), F32)
        for kind in range(kinds):
            result = jnp.dot(templates_ref[kind], patches, preferred_element_type=F32)
            acc = jnp.where((ids == kind)[:1], result, acc)
        return jnp.transpose(acc[:, :blocks] + acc[:, blocks:])

    def spread(mixed):
        high, low = split(mixed)
        both = jnp.concatenate([high, low], 0)
        ids = ids_rows_ref[...].astype(BF16)
        ids = jnp.concatenate([ids, ids], 0)
        terms = jnp.zeros((2 * blocks, cells), F32)
        some = 8
        for first in range(0, kinds, some):
            left = [
                jnp.where(ids == kind, both, jnp.zeros_like(both))
                for kind in range(first, first + some)
            ]
            table = templates_ref[first : first + some].reshape(some * reads, cells)
            terms += jnp.dot(jnp.concatenate(left, 1), table, preferred_element_type=F32)
        terms = terms[:blocks] + terms[blocks:]
        lead = rows - PSIDE
        for half in range(2):
            part = terms[:, half * LANES : (half + 1) * LANES].reshape(tiles, ROWS, LANES)
            padded_ref[:, lead + half * ROWS : lead + (half + 1) * ROWS, :] = block_transpose(part)
        wide = lax.broadcasted_iota(jnp.int32, (rows, LANES), 1) // PSIDE

        def one_tile(tile, carry):
            picked = jnp.zeros((rows, LANES), F32)
            for place in range(PER_TILE):
                start = lead - lon_ref[0, tile * PER_TILE + place]
                window = padded_ref[tile, pl.ds(start, rows), :]
                picked = jnp.where(wide == place, window, picked)
            high, low = split(picked)
            start = pl.multiple_of(tile * LANES, LANES)
            spread_ref[0:rows, pl.ds(start, LANES)] = high
            spread_ref[rows : 2 * rows, pl.ds(start, LANES)] = low
            return carry

        lax.fori_loop(0, tiles, one_tile, 0, unroll=tiles)
        both = jnp.dot(spread_ref[...], select_ref[...], preferred_element_type=F32)
        return both[:rows] + both[rows:]

    row_at = lax.broadcasted_iota(jnp.int32, (ROWS, LANES), 0)

    def packed(parts):
        parts = [jnp.sum(part, axis=0, keepdims=True) for part in parts]
        parts += [jnp.zeros((1, LANES), F32)] * (ROWS - len(parts))
        total = jnp.sum(jnp.concatenate(parts, 0), axis=1, keepdims=True)
        return jnp.sum(jnp.where(row_at == lane, total, 0.0), axis=0, keepdims=True)

    def unpacked(total, count):
        return [
            jnp.sum(jnp.where(lane[:1] == place, total, 0.0), axis=1, keepdims=True)
            for place in range(count)
        ]

    for copy in loads[6:]:
        copy.wait()
    pack_coefficients(kappa_ref[...], prior_ref[...])

    def one_turn(turn, carry):
        image_ref[...] = spread(term_ref[...])

        @pl.when(turn == 2)
        def _():
            for copy in sides(0, turn - 1):
                copy.wait_recv()
            inner_stencil(turn - 1)

        @pl.when(turn == 1)
        def _():
            for copy in coefficient_copies:
                copy.wait_recv()

        @pl.when(turn > 0)
        def _():
            for copy in diagonals(turn - 1):
                copy.wait_recv()
            image_ref[...] += outer_stencil(turn - 1)
            for copy in sides(0, turn - 1) + diagonals(turn - 1):
                copy.wait_send()

        @pl.when(turn == 0)
        def _():
            right = image_ref[...]
            r0_ref[...] = right
            v_ref[...] = right
            pl.semaphore_wait(barrier, len(peers))

        @pl.when(turn == 1)
        def _():
            image = image_ref[...]
            w0_ref[...] = image
            v_ref[...] = image

        @pl.when(turn == 2)
        def _():
            for copy in first_b_copies:
                copy.wait_recv()
            norm, curve = unpacked(jnp.sum(first_b[...], axis=0), 2)
            alpha = norm / curve
            w0 = w0_ref[...]
            w1 = w0 - alpha * image_ref[...]
            r1_ref[...] = r0_ref[...] - alpha * w0
            w1_ref[...] = w1
            v_ref[...] = w1
            lane_row = lane[:1]
            first_ref[...] = jnp.where(lane_row == 0, alpha, jnp.where(lane_row == 1, curve, 0.0))

        @pl.when(turn == ITERS)
        def _():
            for copy in last_b_copies:
                copy.wait_recv()
            sizes = unpacked(jnp.sum(last_b[...], axis=0), 7)
            alpha, a = unpacked(first_ref[...], 2)
            g0, g1, d, b, c, e, f = sizes
            g2 = d
            l1, l2 = b / a, c / a
            d, e, f = d - l1 * b, e - l1 * c, f - l2 * c
            m = e / d
            f = f - m * e
            g1 = g1 - l1 * g0
            g2 = g2 - l2 * g0 - m * g1
            c2 = g2 / f
            c1 = g1 / d - m * c2
            c0 = g0 / a - l1 * c1 - l2 * c2
            w1, r1 = w1_ref[...], r1_ref[...]
            x_ref[...] = (alpha + c0) * r0_ref[...] + c1 * r1 + c2 * w1
            r_ref[...] = r1 - c0 * w0_ref[...] - c1 * w1 - c2 * image_ref[...]

        @pl.when(turn < ITERS)
        def _():
            pack_vector(v_ref[...])
            for copy in sides(0, turn) + diagonals(turn):
                copy.start()

            @pl.when(turn == 0)
            def _():
                for copy in coefficient_copies:
                    copy.start()

            gather(v_ref[...])

            @pl.when(turn == 1)
            def _():
                for copy in first_a_copies:
                    copy.wait_recv()
                first_b[chip] = jnp.sum(first_a[...], axis=0)
                for copy in first_b_copies:
                    copy.start()

            image = read()
            mixed = weights_ref[...] * image
            term_ref[...] = mixed

            @pl.when(turn != 1)
            def _():
                for copy in sides(0, turn):
                    copy.wait_recv()
                inner, scaled = inner_stencil(turn)
                curve_ref[...] = fold(scaled * inner) + fold(mixed * image)

            @pl.when(turn == 0)
            def _():
                first_a[me_a] = packed([fold(r0_ref[...] * r0_ref[...]), curve_ref[...]])
                for copy in first_a_copies:
                    copy.start()

            @pl.when(turn == 2)
            def _():
                r0, w0, r1, w1 = r0_ref[...], w0_ref[...], r1_ref[...], w1_ref[...]
                pairs = [(r0, r1), (r1, r1), (r1, w1), (r0, w1), (w0, w1), (w1, w1)]
                last_a[core] = packed([fold(one * two) for one, two in pairs] + [curve_ref[...]])
                for copy in last_a_copies:
                    copy.start()
                for copy in last_a_copies:
                    copy.wait_recv()
                last_b[me_far] = jnp.sum(last_a[...], axis=0)
                for copy in last_b_copies:
                    copy.start()

        return carry

    lax.fori_loop(0, ITERS + 1, one_turn, 0)
    for copy in first_a_copies + first_b_copies + last_a_copies + last_b_copies + coefficient_copies:
        copy.wait_send()


def far_first(n_lat, chips_lon):
    side = max(1, round(chips_lon**0.5))

    def away(step, size):
        return min(step, size - step)

    steps = [
        (across, along)
        for across in range(n_lat)
        for along in range(chips_lon)
        if across or along
    ]

    def distance(step):
        across, along = step
        return away(across, n_lat) + away(along // side, side) + away(along % side, side)

    return sorted(steps, key=distance, reverse=True)


def hand_out(x_in, r_in, x_out, r_out, sem):
    copies = [
        pltpu.make_async_copy(x_in, x_out, sem.at[0]),
        pltpu.make_async_copy(r_in, r_out, sem.at[1]),
    ]
    for copy in copies:
        copy.start()
    for copy in copies:
        copy.wait()


def on_device(
    n_lon,
    n_lat,
    kappa_sq,
    prior_scale,
    templates,
    block_counts,
    anchor_lon,
    anchor_lat,
    template_ids,
    readings,
    noise_prec,
):
    rows, cols = kappa_sq.shape
    kinds, reads, cells = templates.shape
    blocks = template_ids.shape[1]
    tiles = blocks // PER_TILE
    group_a, chips_lon = 2 * n_lat, n_lon // 2
    chips = n_lat * chips_lon
    vmem = pl.BlockSpec(memory_space=pltpu.VMEM)
    dma = pltpu.SemaphoreType.DMA
    field = jax.ShapeDtypeStruct((rows, cols), F32)
    plane = pltpu.VMEM((rows, cols), F32)
    fields = pl.pallas_call(
        functools.partial(kernel, n_lon, n_lat),
        out_shape=(pltpu.VMEM((rows, cols), F32), pltpu.VMEM((rows, cols), F32)),
        in_specs=[pl.BlockSpec(memory_space=pl.ANY)] * 9,
        out_specs=(vmem, vmem),
        scratch_shapes=[
            plane,
            plane,
            pltpu.VMEM((kinds, reads, cells), BF16),
            pltpu.SMEM((1,), jnp.int32),
            pltpu.SMEM((1, blocks), jnp.int32),
            pltpu.SMEM((1, blocks), jnp.int32),
            pltpu.VMEM((1, blocks), jnp.int32),
            pltpu.VMEM((blocks, reads), F32),
            pltpu.VMEM((blocks, reads), F32),
            pltpu.VMEM((blocks * PSIDE, cols), BF16),
            pltpu.VMEM((cols, blocks * PSIDE), BF16),
            pltpu.VMEM((tiles, rows, LANES), F32),
            pltpu.VMEM((tiles, 2 * rows - PSIDE, LANES), F32),
            pltpu.VMEM((2 * rows, blocks * PSIDE), BF16),
            pltpu.VMEM((blocks, cells), F32),
            pltpu.VMEM((blocks, blocks), F32),
            pltpu.VMEM((blocks, reads), F32),
            plane,
            plane,
            plane,
            plane,
            plane,
            plane,
            plane,
            pltpu.VMEM((1, LANES), F32),
            pltpu.VMEM((ROWS, LANES), F32),
            pltpu.VMEM((2, 2, 2, 1, cols), F32),
            pltpu.VMEM((2, 2, 2, 1, LANES), F32),
            pltpu.VMEM((4, 1, LANES), F32),
            pltpu.VMEM((ITERS + 1, 2, 2, 1, cols), F32),
            pltpu.VMEM((ITERS + 1, 2, 2, 1, LANES), F32),
            pltpu.VMEM((ITERS, 4, 1, LANES), F32),
            pltpu.VMEM((group_a, 1, LANES), F32),
            pltpu.VMEM((chips_lon, 1, LANES), F32),
            pltpu.VMEM((2, 1, LANES), F32),
            pltpu.VMEM((chips, 1, LANES), F32),
            dma((8 + TEMPLATE_PARTS,)),
            dma((ITERS + 1, 8)),
            dma((ITERS + 1, 8)),
            dma((group_a - 1,)),
            dma((group_a - 1,)),
            dma((chips_lon - 1,)),
            dma((chips_lon - 1,)),
            dma((1,)),
            dma((1,)),
            dma((chips - 1,)),
            dma((chips - 1,)),
        ],
        compiler_params=pltpu.CompilerParams(
            collective_id=0, has_side_effects=True, vmem_limit_bytes=56 * 1024 * 1024
        ),
    )(
        kappa_sq,
        prior_scale,
        templates,
        block_counts,
        anchor_lon,
        anchor_lat,
        template_ids,
        readings[0],
        noise_prec[0],
    )
    return pl.pallas_call(
        hand_out,
        out_shape=(field, field),
        in_specs=[pl.BlockSpec(memory_space=pl.ANY)] * 2,
        out_specs=(pl.BlockSpec(memory_space=pl.ANY),) * 2,
        scratch_shapes=[dma((2,))],
        compiler_params=pltpu.CompilerParams(vmem_limit_bytes=1024 * 1024),
    )(*fields)


def solution(mesh):
    return jax.shard_map(
        functools.partial(on_device, mesh.shape["lon"], mesh.shape["lat"]),
        mesh=mesh,
        in_specs=(
            P("lon", "lat"),
            P("lon", "lat"),
            P(),
            P(("lon", "lat")),
            P("lon", "lat"),
            P("lon", "lat"),
            P("lon", "lat"),
            P("lon", "lat", None),
            P("lon", "lat", None),
        ),
        out_specs=(P("lon", "lat"), P("lon", "lat")),
        check_vma=False,
    )
```

```python
import functools

import jax
import jax.numpy as jnp
from jax import lax
from jax.experimental import pallas as pl
from jax.experimental.pallas import tpu as pltpu
from jax.sharding import PartitionSpec as P

PSIDE = 16
ITERS = 3
LANES = 128
ROWS = 8
PER_TILE = LANES // PSIDE
F32 = jnp.float32
BF16 = jnp.bfloat16
MESH = pl.DeviceIdType.MESH


def split(value):
    high = value.astype(BF16)
    low = (value - high.astype(F32)).astype(BF16)
    return high, low


def block_transpose(value):
    row = lax.broadcasted_iota(jnp.int32, value.shape, 1)
    chunk = lax.broadcasted_iota(jnp.int32, value.shape, 2) // PSIDE
    for k in (4, 2, 1):
        row_bit = (row // k) % 2
        chunk_bit = (chunk // k) % 2
        ahead = pltpu.roll(pltpu.roll(value, ROWS - k, 1), PSIDE * k, 2)
        if k == 4:
            other = ahead
        else:
            behind = pltpu.roll(pltpu.roll(value, k, 1), LANES - PSIDE * k, 2)
            other = jnp.where(row_bit == 0, ahead, behind)
        value = jnp.where(row_bit == chunk_bit, value, other)
    return value


def fold(value):
    total = jnp.sum(value.reshape(value.shape[0] // ROWS, ROWS, value.shape[1]), axis=0)
    parts = [total[:, i : i + LANES] for i in range(0, total.shape[1], LANES)]
    return functools.reduce(jnp.add, parts)


def to_row(column):
    wide = jnp.broadcast_to(column, (column.shape[0], LANES))
    row = lax.broadcasted_iota(jnp.int32, wide.shape, 0)
    lane = lax.broadcasted_iota(jnp.int32, wide.shape, 1)
    return jnp.sum(jnp.where(row == lane, wide, 0.0), axis=0, keepdims=True)


def to_column(row_value, rows):
    wide = jnp.broadcast_to(row_value, (rows, LANES))
    row = lax.broadcasted_iota(jnp.int32, wide.shape, 0)
    lane = lax.broadcasted_iota(jnp.int32, wide.shape, 1)
    return jnp.sum(jnp.where(row == lane, wide, 0.0), axis=1, keepdims=True)


def shifted(field, prev_lon, next_lon, prev_lat, next_lat):
    rows, cols = field.shape
    row = lax.broadcasted_iota(jnp.int32, field.shape, 0)
    lane = lax.broadcasted_iota(jnp.int32, (rows, LANES), 1)
    west = jnp.where(row == 0, prev_lon, pltpu.roll(field, 1, 0))
    east = jnp.where(row == rows - 1, next_lon, pltpu.roll(field, rows - 1, 0))
    south = pltpu.roll(field, 1, 1)
    north = pltpu.roll(field, cols - 1, 1)
    first = jnp.where(lane == 0, prev_lat, south[:, :LANES])
    last = jnp.where(lane == LANES - 1, next_lat, north[:, cols - LANES :])
    south = jnp.concatenate([first, south[:, LANES:]], 1)
    north = jnp.concatenate([north[:, : cols - LANES], last], 1)
    return west + east + south + north


def kernel(
    n_lon,
    n_lat,
    kappa_hbm,
    prior_hbm,
    templates_hbm,
    count_hbm,
    lon_hbm,
    lat_hbm,
    ids_hbm,
    readings_hbm,
    noise_hbm,
    x_ref,
    r_ref,
    kappa_ref,
    prior_ref,
    templates_ref,
    count_ref,
    lon_ref,
    lat_ref,
    ids_ref,
    readings_ref,
    weights_ref,
    select_ref,
    turned_ref,
    columns_ref,
    padded_ref,
    spread_ref,
    patch_ref,
    ids_rows_ref,
    term_ref,
    r0_ref,
    w0_ref,
    r1_ref,
    w1_ref,
    image_ref,
    v_ref,
    u_ref,
    first_ref,
    curve_ref,
    out_lon,
    out_lat,
    out_corner,
    edge_lon,
    edge_lat,
    edge_corner,
    first_a,
    first_b,
    last_a,
    last_b,
    load_sem,
    edge_send,
    edge_recv,
    corner_sem,
    first_a_sem,
    first_b_sem,
    last_a_sem,
    last_b_sem,
):
    kinds, reads, cells = templates_ref.shape
    rows, cols = kappa_ref.shape
    blocks = ids_ref.shape[1]
    tiles = blocks // PER_TILE
    lon, lat = lax.axis_index("lon"), lax.axis_index("lat")
    chips_lon = n_lon // 2
    core, chip = lon % 2, lon // 2

    loads = [
        pltpu.make_async_copy(source, target, load_sem.at[place])
        for place, (source, target) in enumerate(
            [
                (lat_hbm, lat_ref),
                (templates_hbm, templates_ref),
                (lon_hbm, lon_ref),
                (ids_hbm, ids_ref),
                (count_hbm, count_ref),
                (noise_hbm, weights_ref),
                (readings_hbm, readings_ref),
                (kappa_hbm, kappa_ref),
                (prior_hbm, prior_ref),
            ]
        )
    ]
    for copy in loads:
        copy.start()

    me_a = lat * 2 + core
    group_a = 2 * n_lat

    def peer_a(step):
        index = (me_a + step) % group_a
        return (chip * 2 + index % 2, index // 2)

    peers_a = [peer_a(step) for step in range(1, group_a)]
    peers_b = [(((chip + step) % chips_lon) * 2 + core, lat) for step in range(1, chips_lon)]
    twin = (chip * 2 + 1 - core, lat)
    peers_far = [
        (((chip + along) % chips_lon) * 2 + core, (lat + across) % n_lat)
        for across, along in far_first(n_lat, chips_lon)
    ]
    lon_next, lon_prev = ((lon + 1) % n_lon, lat), ((lon + n_lon - 1) % n_lon, lat)
    lat_next, lat_prev = (lon, (lat + 1) % n_lat), (lon, (lat + n_lat - 1) % n_lat)
    corners = [(one[0], two[1]) for one in (lon_next, lon_prev) for two in (lat_next, lat_prev)]

    barrier = pltpu.get_barrier_semaphore()
    peers = [lon_next, lon_prev, lat_next, lat_prev] + corners + peers_a + peers_b
    for peer in peers:
        pl.semaphore_signal(barrier, inc=1, device_id=peer, device_id_type=MESH)

    def pack_vector(field):
        out_lon[0, 0, 0] = field[rows - 1 : rows, :]
        out_lon[0, 0, 1] = field[rows - 2 : rows - 1, :]
        out_lon[0, 1, 0] = field[0:1, :]
        out_lon[0, 1, 1] = field[1:2, :]
        out_lat[0, 0, 0] = to_row(field[:, cols - 1 : cols])
        out_lat[0, 0, 1] = to_row(field[:, cols - 2 : cols - 1])
        out_lat[0, 1, 0] = to_row(field[:, 0:1])
        out_lat[0, 1, 1] = to_row(field[:, 1:2])
        for place, (row, col) in enumerate([(rows - 1, cols - 1), (rows - 1, 0), (0, cols - 1), (0, 0)]):
            value = field[row : row + 1, col : col + 1]
            out_corner[place] = jnp.broadcast_to(value, (1, LANES))

    def pack_coefficients(kappa, prior):
        for place, field in enumerate((kappa, prior)):
            out_lon[1, 0, place] = field[rows - 1 : rows, :]
            out_lon[1, 1, place] = field[0:1, :]
            out_lat[1, 0, place] = to_row(field[:, cols - 1 : cols])
            out_lat[1, 1, place] = to_row(field[:, 0:1])

    def remote(src, dst, send_sem, recv_sem, peer):
        return pltpu.make_async_remote_copy(
            src_ref=src,
            dst_ref=dst,
            send_sem=send_sem,
            recv_sem=recv_sem,
            device_id=peer,
            device_id_type=MESH,
        )

    def whole(ref, sem):
        pltpu.make_async_copy(ref, ref, sem).wait()

    def send_sides(kind, slot):
        for side, peer in enumerate((lon_next, lon_prev)):
            remote(
                out_lon.at[kind, side],
                edge_lon.at[slot, side],
                edge_send.at[kind, 0],
                edge_recv.at[slot, 0],
                peer,
            ).start()
        for side, peer in enumerate((lat_next, lat_prev)):
            remote(
                out_lat.at[kind, side],
                edge_lat.at[slot, side],
                edge_send.at[kind, 1],
                edge_recv.at[slot, 1],
                peer,
            ).start()

    def receive_sides(slot):
        whole(edge_lon.at[slot], edge_recv.at[slot, 0])
        whole(edge_lat.at[slot], edge_recv.at[slot, 1])

    def finish_sides(kind):
        whole(out_lon.at[kind], edge_send.at[kind, 0])
        whole(out_lat.at[kind], edge_send.at[kind, 1])

    def send_corners(slot):
        for place, peer in enumerate(corners):
            remote(
                out_corner.at[place],
                edge_corner.at[slot, place],
                corner_sem.at[ITERS],
                corner_sem.at[slot],
                peer,
            ).start()

    def send_sum(buffer, me, sems, peers):
        for peer in peers:
            remote(buffer.at[me], buffer.at[me], sems.at[0], sems.at[1], peer).start()

    def receive_sum(buffer, sems):
        others = buffer.at[pl.ds(0, buffer.shape[0] - 1)]
        whole(others, sems.at[1])
        return jnp.sum(buffer[...], axis=0)

    def finish_sum(buffer, sems):
        whole(buffer.at[pl.ds(0, buffer.shape[0] - 1)], sems.at[0])

    me_far = chip * n_lat + lat
    has_prev = (lat > 0).astype(F32)
    has_next = (lat < n_lat - 1).astype(F32)

    def inner_stencil(turn):
        field = v_ref[...]
        around = shifted(
            field,
            edge_lon[turn, 0, 0],
            edge_lon[turn, 1, 0],
            to_column(edge_lat[turn, 0, 0] * has_prev, rows),
            to_column(edge_lat[turn, 1, 0] * has_next, rows),
        )
        u_ref[...] = prior_ref[...] * ((kappa_ref[...] + 4.0) * field - around)

    def inner_square():
        field = v_ref[...]
        nothing = jnp.zeros((1, cols), F32), jnp.zeros((rows, 1), F32)
        around = shifted(field, nothing[0], nothing[0], nothing[1], nothing[1])
        inner = (kappa_ref[...] + 4.0) * field - around
        lon_sides = inner[0:1, :], inner[rows - 1 : rows, :]
        lat_sides = to_row(inner[:, 0:1]), to_row(inner[:, cols - 1 : cols])
        return fold(prior_ref[...] * inner * inner), lon_sides, lat_sides

    def side_square(turn, lon_sides, lat_sides):
        lane_row = lax.broadcasted_iota(jnp.int32, (1, LANES), 1)
        total = jnp.zeros((1, LANES), F32)
        for side in (0, 1):
            beside, own = edge_lon[turn, side, 0], lon_sides[side]
            change = out_lon[1, 1 - side, 1] * beside * (beside - 2.0 * own)
            for at in range(0, cols, LANES):
                total += change[:, at : at + LANES]
        ends = edge_lon[turn, 0, 0], edge_lon[turn, 1, 0]
        for side, (at, present) in enumerate(((0, has_prev), (cols - 1, has_next))):
            beside, own = edge_lat[turn, side, 0] * present, lat_sides[side]
            own = own - jnp.where(lane_row == 0, ends[0][:, at : at + 1], 0.0)
            own = own - jnp.where(lane_row == rows - 1, ends[1][:, at : at + 1], 0.0)
            total += out_lat[1, 1 - side, 1] * beside * (beside - 2.0 * own)
        return total

    def outer_stencil(turn):
        lane_wide = lax.broadcasted_iota(jnp.int32, (1, cols), 1)
        lane_row = lax.broadcasted_iota(jnp.int32, (1, LANES), 1)
        present = (has_prev, has_next)
        beside_lon, beside_lat = [], []
        for side, at in ((0, 0), (1, rows - 1)):
            near, far = edge_lon[turn, side, 0], edge_lon[turn, side, 1]
            kappa, prior = edge_lon[ITERS, side, 0], edge_lon[ITERS, side, 1]
            first = edge_corner[turn, 2 * side][:, :1] * has_prev
            last = edge_corner[turn, 2 * side + 1][:, :1] * has_next
            south = jnp.where(lane_wide == 0, first, pltpu.roll(near, 1, 1))
            north = jnp.where(lane_wide == cols - 1, last, pltpu.roll(near, cols - 1, 1))
            around = far + v_ref[at : at + 1, :] + south + north
            beside_lon.append(prior * ((kappa + 4.0) * near - around))
        for side in (0, 1):
            near, far = edge_lat[turn, side, 0], edge_lat[turn, side, 1]
            kappa, prior = edge_lat[ITERS, side, 0], edge_lat[ITERS, side, 1]
            first, last = edge_corner[turn, side][:, :1], edge_corner[turn, 2 + side][:, :1]
            west = jnp.where(lane_row == 0, first, pltpu.roll(near, 1, 1))
            east = jnp.where(lane_row == rows - 1, last, pltpu.roll(near, LANES - 1, 1))
            around = far + out_lat[0, 1 - side, 0] + west + east
            value = prior * ((kappa + 4.0) * near - around) * present[side]
            beside_lat.append(to_column(value, rows))
        scaled = u_ref[...]
        return (kappa_ref[...] + 4.0) * scaled - shifted(scaled, *beside_lon, *beside_lat)

    padded_ref[...] = jnp.zeros(padded_ref.shape, F32)
    offset = lax.broadcasted_iota(jnp.int32, (PSIDE, cols), 1) - lax.broadcasted_iota(
        jnp.int32, (PSIDE, cols), 0
    )

    def one_selector(block, carry):
        start = pl.multiple_of(block * PSIDE, PSIDE)
        chosen = jnp.where(offset == lat_ref[0, block], 1.0, 0.0)
        select_ref[pl.ds(start, PSIDE), :] = chosen.astype(BF16)
        return carry

    loads[0].wait()
    lax.fori_loop(0, blocks, one_selector, 0, unroll=16)
    lane = lax.broadcasted_iota(jnp.int32, (ROWS, LANES), 1)
    chunk = lane // PSIDE
    cell = lax.broadcasted_iota(jnp.int32, (cols, LANES), 0)

    def one_turned(tile, carry):
        place = jnp.zeros((ROWS, LANES), jnp.int32)
        for block in range(PER_TILE):
            place = jnp.where(chunk == block, lat_ref[0, tile * PER_TILE + block], place)
        place = (place + lane % PSIDE)[:1]
        start = pl.multiple_of(tile * LANES, LANES)
        turned_ref[:, pl.ds(start, LANES)] = jnp.where(cell == place, 1.0, 0.0).astype(BF16)
        return carry

    lax.fori_loop(0, tiles, one_turned, 0, unroll=2)
    for copy in loads[2:]:
        copy.wait()
    slot = lax.broadcasted_iota(jnp.int32, (blocks, reads), 0)
    weights = jnp.where(slot < count_ref[0], weights_ref[...], 0.0)
    weights_ref[...] = weights
    term_ref[...] = weights * readings_ref[...]
    ids_row = jnp.broadcast_to(ids_ref[...].astype(F32), (blocks, blocks))
    ids_rows_ref[...] = jnp.transpose(ids_row)

    def gather(field):
        high, low = split(field)
        both = jnp.dot(
            jnp.concatenate([high, low], 0), turned_ref[...], preferred_element_type=F32
        )
        both = both[:rows] + both[rows:]
        for tile in range(tiles):
            columns_ref[tile] = both[:, tile * LANES : (tile + 1) * LANES]
        for tile in range(tiles):
            halves = []
            for half in range(2):
                picked = jnp.zeros((ROWS, LANES), F32)
                for place in range(PER_TILE):
                    start = lon_ref[0, tile * PER_TILE + place] + half * ROWS
                    window = columns_ref[tile, pl.ds(start, ROWS), :]
                    picked = jnp.where(chunk == place, window, picked)
                halves.append(picked)
            done = block_transpose(jnp.stack(halves))
            for half in range(2):
                patch_ref[
                    tile * ROWS : (tile + 1) * ROWS, half * LANES : (half + 1) * LANES
                ] = done[half]

    def read():
        high, low = split(jnp.transpose(patch_ref[...]))
        patches = jnp.concatenate([high, low], 1)
        ids = jnp.broadcast_to(ids_ref[...], (ROWS, blocks))
        ids = jnp.concatenate([ids, ids], 1)
        acc = jnp.zeros((reads, 2 * blocks), F32)
        for kind in range(kinds):
            result = jnp.dot(templates_ref[kind], patches, preferred_element_type=F32)
            acc = jnp.where((ids == kind)[:1], result, acc)
        return jnp.transpose(acc[:, :blocks] + acc[:, blocks:])

    def spread(mixed):
        high, low = split(mixed)
        both = jnp.concatenate([high, low], 0)
        ids = ids_rows_ref[...].astype(BF16)
        ids = jnp.concatenate([ids, ids], 0)
        terms = jnp.zeros((2 * blocks, cells), F32)
        some = 8
        for first in range(0, kinds, some):
            left = [
                jnp.where(ids == kind, both, jnp.zeros_like(both))
                for kind in range(first, first + some)
            ]
            table = templates_ref[first : first + some].reshape(some * reads, cells)
            terms += jnp.dot(jnp.concatenate(left, 1), table, preferred_element_type=F32)
        terms = terms[:blocks] + terms[blocks:]
        lead = rows - PSIDE
        for half in range(2):
            part = terms[:, half * LANES : (half + 1) * LANES].reshape(tiles, ROWS, LANES)
            padded_ref[:, lead + half * ROWS : lead + (half + 1) * ROWS, :] = block_transpose(part)
        wide = lax.broadcasted_iota(jnp.int32, (rows, LANES), 1) // PSIDE

        def one_tile(tile, carry):
            picked = jnp.zeros((rows, LANES), F32)
            for place in range(PER_TILE):
                start = lead - lon_ref[0, tile * PER_TILE + place]
                window = padded_ref[tile, pl.ds(start, rows), :]
                picked = jnp.where(wide == place, window, picked)
            high, low = split(picked)
            start = pl.multiple_of(tile * LANES, LANES)
            spread_ref[0:rows, pl.ds(start, LANES)] = high
            spread_ref[rows : 2 * rows, pl.ds(start, LANES)] = low
            return carry

        lax.fori_loop(0, tiles, one_tile, 0, unroll=tiles)
        both = jnp.dot(spread_ref[...], select_ref[...], preferred_element_type=F32)
        return both[:rows] + both[rows:]

    row_at = lax.broadcasted_iota(jnp.int32, (ROWS, LANES), 0)

    def packed(parts, more):
        parts = [jnp.sum(part, axis=0, keepdims=True) for part in parts]
        parts[-1] = parts[-1] + more
        parts += [jnp.zeros((1, LANES), F32)] * (ROWS - len(parts))
        total = jnp.sum(jnp.concatenate(parts, 0), axis=1, keepdims=True)
        return jnp.sum(jnp.where(row_at == lane, total, 0.0), axis=0, keepdims=True)

    def unpacked(total, count):
        return [
            jnp.sum(jnp.where(lane[:1] == place, total, 0.0), axis=1, keepdims=True)
            for place in range(count)
        ]

    pack_coefficients(kappa_ref[...], prior_ref[...])
    loads[1].wait()

    def one_turn(turn, carry):
        image_ref[...] = spread(term_ref[...])

        @pl.when(turn == 1)
        def _():
            receive_sides(ITERS)

        @pl.when(turn == 2)
        def _():
            receive_sides(turn - 1)

        @pl.when(turn > 0)
        def _():
            inner_stencil(turn - 1)
            whole(edge_corner.at[turn - 1], corner_sem.at[turn - 1])
            image_ref[...] += outer_stencil(turn - 1)
            finish_sides(0)
            whole(out_corner, corner_sem.at[ITERS])

        @pl.when(turn == 0)
        def _():
            right = image_ref[...]
            r0_ref[...] = right
            v_ref[...] = right
            pl.semaphore_wait(barrier, len(peers))

        @pl.when(turn == 1)
        def _():
            image = image_ref[...]
            w0_ref[...] = image
            v_ref[...] = image

        @pl.when(turn == 2)
        def _():
            norm, curve = unpacked(receive_sum(first_b, first_b_sem), 2)
            alpha = norm / curve
            w0 = w0_ref[...]
            w1 = w0 - alpha * image_ref[...]
            r1_ref[...] = r0_ref[...] - alpha * w0
            w1_ref[...] = w1
            v_ref[...] = w1
            lane_row = lane[:1]
            first_ref[...] = jnp.where(lane_row == 0, alpha, jnp.where(lane_row == 1, curve, 0.0))

        @pl.when(turn == ITERS)
        def _():
            sizes = unpacked(receive_sum(last_b, last_b_sem), 7)
            alpha, a = unpacked(first_ref[...], 2)
            g0, g1, d, b, c, e, f = sizes
            g2 = d
            l1, l2 = b / a, c / a
            d, e, f = d - l1 * b, e - l1 * c, f - l2 * c
            m = e / d
            f = f - m * e
            g1 = g1 - l1 * g0
            g2 = g2 - l2 * g0 - m * g1
            c2 = g2 / f
            c1 = g1 / d - m * c2
            c0 = g0 / a - l1 * c1 - l2 * c2
            w1, r1 = w1_ref[...], r1_ref[...]
            x_ref[...] = (alpha + c0) * r0_ref[...] + c1 * r1 + c2 * w1
            r_ref[...] = r1 - c0 * w0_ref[...] - c1 * w1 - c2 * image_ref[...]

        @pl.when(turn < ITERS)
        def _():
            pack_vector(v_ref[...])
            send_sides(0, turn)
            send_corners(turn)

            @pl.when(turn == 0)
            def _():
                send_sides(1, ITERS)

            gather(v_ref[...])

            @pl.when(turn == 1)
            def _():
                first_b[chip] = receive_sum(first_a, first_a_sem)
                send_sum(first_b, chip, first_b_sem, peers_b)

            image = read()
            mixed = weights_ref[...] * image
            term_ref[...] = mixed
            curve_ref[...] = fold(mixed * image)

            def curve():
                inside, lon_sides, lat_sides = inner_square()
                return curve_ref[...] + inside, lon_sides, lat_sides

            @pl.when(turn == 0)
            def _():
                inside, lon_sides, lat_sides = curve()
                parts = [fold(r0_ref[...] * r0_ref[...]), inside]
                receive_sides(turn)
                first_a[me_a] = packed(parts, side_square(turn, lon_sides, lat_sides))
                send_sum(first_a, me_a, first_a_sem, peers_a)

            @pl.when(turn == 2)
            def _():
                r0, w0, r1, w1 = r0_ref[...], w0_ref[...], r1_ref[...], w1_ref[...]
                pairs = [(r0, r1), (r1, r1), (r1, w1), (r0, w1), (w0, w1), (w1, w1)]
                inside, lon_sides, lat_sides = curve()
                parts = [fold(one * two) for one, two in pairs] + [inside]
                receive_sides(turn)
                last_a[core] = packed(parts, side_square(turn, lon_sides, lat_sides))
                send_sum(last_a, core, last_a_sem, [twin])
                last_b[me_far] = receive_sum(last_a, last_a_sem)
                send_sum(last_b, me_far, last_b_sem, peers_far)

        return carry

    lax.fori_loop(0, ITERS + 1, one_turn, 0)
    finish_sides(1)
    finish_sum(first_a, first_a_sem)
    finish_sum(first_b, first_b_sem)
    finish_sum(last_a, last_a_sem)
    finish_sum(last_b, last_b_sem)


def far_first(n_lat, chips_lon):
    side = max(1, round(chips_lon**0.5))

    def away(step, size):
        return min(step, size - step)

    steps = [
        (across, along)
        for across in range(n_lat)
        for along in range(chips_lon)
        if across or along
    ]

    def distance(step):
        across, along = step
        return away(across, n_lat) + away(along // side, side) + away(along % side, side)

    return sorted(steps, key=distance, reverse=True)


def hand_out(x_in, r_in, x_out, r_out, sem):
    copies = [
        pltpu.make_async_copy(x_in, x_out, sem.at[0]),
        pltpu.make_async_copy(r_in, r_out, sem.at[1]),
    ]
    for copy in copies:
        copy.start()
    for copy in copies:
        copy.wait()


def on_device(
    n_lon,
    n_lat,
    kappa_sq,
    prior_scale,
    templates,
    block_counts,
    anchor_lon,
    anchor_lat,
    template_ids,
    readings,
    noise_prec,
):
    rows, cols = kappa_sq.shape
    kinds, reads, cells = templates.shape
    blocks = template_ids.shape[1]
    tiles = blocks // PER_TILE
    group_a, chips_lon = 2 * n_lat, n_lon // 2
    chips = n_lat * chips_lon
    vmem = pl.BlockSpec(memory_space=pltpu.VMEM)
    dma = pltpu.SemaphoreType.DMA
    field = jax.ShapeDtypeStruct((rows, cols), F32)
    plane = pltpu.VMEM((rows, cols), F32)
    fields = pl.pallas_call(
        functools.partial(kernel, n_lon, n_lat),
        out_shape=(pltpu.VMEM((rows, cols), F32), pltpu.VMEM((rows, cols), F32)),
        in_specs=[pl.BlockSpec(memory_space=pl.ANY)] * 9,
        out_specs=(vmem, vmem),
        scratch_shapes=[
            plane,
            plane,
            pltpu.VMEM((kinds, reads, cells), BF16),
            pltpu.SMEM((1,), jnp.int32),
            pltpu.SMEM((1, blocks), jnp.int32),
            pltpu.SMEM((1, blocks), jnp.int32),
            pltpu.VMEM((1, blocks), jnp.int32),
            pltpu.VMEM((blocks, reads), F32),
            pltpu.VMEM((blocks, reads), F32),
            pltpu.VMEM((blocks * PSIDE, cols), BF16),
            pltpu.VMEM((cols, blocks * PSIDE), BF16),
            pltpu.VMEM((tiles, rows, LANES), F32),
            pltpu.VMEM((tiles, 2 * rows - PSIDE, LANES), F32),
            pltpu.VMEM((2 * rows, blocks * PSIDE), BF16),
            pltpu.VMEM((blocks, cells), F32),
            pltpu.VMEM((blocks, blocks), F32),
            pltpu.VMEM((blocks, reads), F32),
            plane,
            plane,
            plane,
            plane,
            plane,
            plane,
            plane,
            pltpu.VMEM((1, LANES), F32),
            pltpu.VMEM((ROWS, LANES), F32),
            pltpu.VMEM((2, 2, 2, 1, cols), F32),
            pltpu.VMEM((2, 2, 2, 1, LANES), F32),
            pltpu.VMEM((4, 1, LANES), F32),
            pltpu.VMEM((ITERS + 1, 2, 2, 1, cols), F32),
            pltpu.VMEM((ITERS + 1, 2, 2, 1, LANES), F32),
            pltpu.VMEM((ITERS, 4, 1, LANES), F32),
            pltpu.VMEM((group_a, 1, LANES), F32),
            pltpu.VMEM((chips_lon, 1, LANES), F32),
            pltpu.VMEM((2, 1, LANES), F32),
            pltpu.VMEM((chips, 1, LANES), F32),
            dma((9,)),
            dma((2, 2)),
            dma((ITERS + 1, 2)),
            dma((ITERS + 1,)),
            dma((2,)),
            dma((2,)),
            dma((2,)),
            dma((2,)),
        ],
        compiler_params=pltpu.CompilerParams(
            collective_id=0, has_side_effects=True, vmem_limit_bytes=56 * 1024 * 1024
        ),
    )(
        kappa_sq,
        prior_scale,
        templates,
        block_counts,
        anchor_lon,
        anchor_lat,
        template_ids,
        readings[0],
        noise_prec[0],
    )
    return pl.pallas_call(
        hand_out,
        out_shape=(field, field),
        in_specs=[pl.BlockSpec(memory_space=pl.ANY)] * 2,
        out_specs=(pl.BlockSpec(memory_space=pl.ANY),) * 2,
        scratch_shapes=[dma((2,))],
        compiler_params=pltpu.CompilerParams(vmem_limit_bytes=1024 * 1024),
    )(*fields)


def solution(mesh):
    return jax.shard_map(
        functools.partial(on_device, mesh.shape["lon"], mesh.shape["lat"]),
        mesh=mesh,
        in_specs=(
            P("lon", "lat"),
            P("lon", "lat"),
            P(),
            P(("lon", "lat")),
            P("lon", "lat"),
            P("lon", "lat"),
            P("lon", "lat"),
            P("lon", "lat", None),
            P("lon", "lat", None),
        ),
        out_specs=(P("lon", "lat"), P("lon", "lat")),
        check_vma=False,
    )
```

```python
import functools

import jax
import jax.numpy as jnp
from jax import lax
from jax.experimental import pallas as pl
from jax.experimental.pallas import tpu as pltpu
from jax.sharding import PartitionSpec as P

PSIDE = 16
ITERS = 3
LANES = 128
ROWS = 8
PER_TILE = LANES // PSIDE
F32 = jnp.float32
BF16 = jnp.bfloat16
MESH = pl.DeviceIdType.MESH


def split(value):
    high = value.astype(BF16)
    low = (value - high.astype(F32)).astype(BF16)
    return high, low


def slide(value):
    chunk = lax.broadcasted_iota(jnp.int32, value.shape, 2) // PSIDE
    for k in (1, 2, 4):
        value = jnp.where((chunk // k) % 2 == 1, pltpu.roll(value, ROWS - k, 1), value)
    return value


def turn_blocks(value):
    return slide(pltpu.roll(slide(value), 0, 2, stride=PSIDE, stride_axis=1))


def negate_rows(value):
    row = lax.broadcasted_iota(jnp.int32, value.shape, 1)
    value = pltpu.roll(value, 4, 1)
    for k in (2, 1):
        ahead, behind = pltpu.roll(value, ROWS - k, 1), pltpu.roll(value, k, 1)
        value = jnp.where((row // k) % 2 == 0, ahead, behind)
    return pltpu.roll(value, 1, 1)


def fold(value):
    total = jnp.sum(value.reshape(value.shape[0] // ROWS, ROWS, value.shape[1]), axis=0)
    parts = [total[:, i : i + LANES] for i in range(0, total.shape[1], LANES)]
    return functools.reduce(jnp.add, parts)


def to_row(column):
    wide = jnp.broadcast_to(column, (column.shape[0], LANES))
    row = lax.broadcasted_iota(jnp.int32, wide.shape, 0)
    lane = lax.broadcasted_iota(jnp.int32, wide.shape, 1)
    return jnp.sum(jnp.where(row == lane, wide, 0.0), axis=0, keepdims=True)


def to_column(row_value, rows):
    wide = jnp.broadcast_to(row_value, (rows, LANES))
    row = lax.broadcasted_iota(jnp.int32, wide.shape, 0)
    lane = lax.broadcasted_iota(jnp.int32, wide.shape, 1)
    return jnp.sum(jnp.where(row == lane, wide, 0.0), axis=1, keepdims=True)


def shifted(field, prev_lon, next_lon, prev_lat, next_lat):
    rows, cols = field.shape
    row = lax.broadcasted_iota(jnp.int32, field.shape, 0)
    lane = lax.broadcasted_iota(jnp.int32, (rows, LANES), 1)
    west = jnp.where(row == 0, prev_lon, pltpu.roll(field, 1, 0))
    east = jnp.where(row == rows - 1, next_lon, pltpu.roll(field, rows - 1, 0))
    south = pltpu.roll(field, 1, 1)
    north = pltpu.roll(field, cols - 1, 1)
    first = jnp.where(lane == 0, prev_lat, south[:, :LANES])
    last = jnp.where(lane == LANES - 1, next_lat, north[:, cols - LANES :])
    south = jnp.concatenate([first, south[:, LANES:]], 1)
    north = jnp.concatenate([north[:, : cols - LANES], last], 1)
    return west + east + south + north


def kernel(
    n_lon,
    n_lat,
    kappa_hbm,
    prior_hbm,
    templates_hbm,
    count_hbm,
    lon_hbm,
    lat_hbm,
    ids_hbm,
    readings_hbm,
    noise_hbm,
    x_ref,
    r_ref,
    kappa_ref,
    prior_ref,
    templates_ref,
    count_ref,
    lon_ref,
    lat_ref,
    ids_ref,
    readings_ref,
    weights_ref,
    select_ref,
    turned_ref,
    columns_ref,
    padded_ref,
    spread_ref,
    patch_ref,
    ids_rows_ref,
    term_ref,
    r0_ref,
    w0_ref,
    r1_ref,
    w1_ref,
    image_ref,
    v_ref,
    u_ref,
    first_ref,
    curve_ref,
    out_lon,
    out_lat,
    out_corner,
    edge_lon,
    edge_lat,
    edge_corner,
    first_a,
    first_b,
    last_a,
    last_b,
    load_sem,
    edge_send,
    edge_recv,
    corner_sem,
    first_a_sem,
    first_b_sem,
    last_a_sem,
    last_b_sem,
):
    kinds, reads, cells = templates_ref.shape
    rows, cols = kappa_ref.shape
    blocks = ids_ref.shape[1]
    tiles = blocks // PER_TILE
    lon, lat = lax.axis_index("lon"), lax.axis_index("lat")
    chips_lon = n_lon // 2
    core, chip = lon % 2, lon // 2

    loads = [
        pltpu.make_async_copy(source, target, load_sem.at[place])
        for place, (source, target) in enumerate(
            [
                (lat_hbm, lat_ref),
                (templates_hbm, templates_ref),
                (lon_hbm, lon_ref),
                (ids_hbm, ids_ref),
                (count_hbm, count_ref),
                (noise_hbm, weights_ref),
                (readings_hbm, readings_ref),
                (kappa_hbm, kappa_ref),
                (prior_hbm, prior_ref),
            ]
        )
    ]
    for copy in loads:
        copy.start()

    me_a = lat * 2 + core
    group_a = 2 * n_lat

    def peer_a(step):
        index = (me_a + step) % group_a
        return (chip * 2 + index % 2, index // 2)

    peers_a = [peer_a(step) for step in range(1, group_a)]
    peers_b = [(((chip + step) % chips_lon) * 2 + core, lat) for step in range(1, chips_lon)]
    twin = (chip * 2 + 1 - core, lat)
    peers_far = [
        (((chip + along) % chips_lon) * 2 + core, (lat + across) % n_lat)
        for across, along in far_first(n_lat, chips_lon)
    ]
    lon_next, lon_prev = ((lon + 1) % n_lon, lat), ((lon + n_lon - 1) % n_lon, lat)
    lat_next, lat_prev = (lon, (lat + 1) % n_lat), (lon, (lat + n_lat - 1) % n_lat)
    corners = [(one[0], two[1]) for one in (lon_next, lon_prev) for two in (lat_next, lat_prev)]

    barrier = pltpu.get_barrier_semaphore()
    peers = [lon_next, lon_prev, lat_next, lat_prev] + corners + peers_a + peers_b
    for peer in peers:
        pl.semaphore_signal(barrier, inc=1, device_id=peer, device_id_type=MESH)

    def send_vector(ref, slot):
        for side, near, far in ((0, rows - 1, rows - 2), (1, 0, 1)):
            out_lon[0, side, 0] = ref[near : near + 1, :]
            out_lon[0, side, 1] = ref[far : far + 1, :]
        send_lon(0, slot)
        for side, at in ((0, cols - LANES), (1, 0)):
            near, far = ((0, 1), (LANES - 1, LANES - 2))[1 - side]
            tile = ref[:, at : at + LANES]
            out_lat[0, side, 0] = to_row(tile[:, near : near + 1])
            out_lat[0, side, 1] = to_row(tile[:, far : far + 1])
        send_lat(0, slot)
        for place, (row, col) in enumerate(
            [(rows - 1, cols - 1), (rows - 1, 0), (0, cols - 1), (0, 0)]
        ):
            value = ref[row : row + 1, col // LANES * LANES : col // LANES * LANES + LANES]
            lane_at = col % LANES
            out_corner[place] = jnp.broadcast_to(value[:, lane_at : lane_at + 1], (1, LANES))
        send_corners(slot)

    def pack_coefficients(kappa, prior):
        for place, field in enumerate((kappa, prior)):
            out_lon[1, 0, place] = field[rows - 1 : rows, :]
            out_lon[1, 1, place] = field[0:1, :]
            out_lat[1, 0, place] = to_row(field[:, cols - 1 : cols])
            out_lat[1, 1, place] = to_row(field[:, 0:1])

    def remote(src, dst, send_sem, recv_sem, peer):
        return pltpu.make_async_remote_copy(
            src_ref=src,
            dst_ref=dst,
            send_sem=send_sem,
            recv_sem=recv_sem,
            device_id=peer,
            device_id_type=MESH,
        )

    def whole(ref, sem):
        pltpu.make_async_copy(ref, ref, sem).wait()

    def send_lon(kind, slot):
        for side, peer in enumerate((lon_next, lon_prev)):
            remote(
                out_lon.at[kind, side],
                edge_lon.at[slot, side],
                edge_send.at[kind, 0],
                edge_recv.at[slot, 0],
                peer,
            ).start()

    def send_lat(kind, slot):
        for side, peer in enumerate((lat_next, lat_prev)):
            remote(
                out_lat.at[kind, side],
                edge_lat.at[slot, side],
                edge_send.at[kind, 1],
                edge_recv.at[slot, 1],
                peer,
            ).start()

    def receive_sides(slot):
        whole(edge_lon.at[slot], edge_recv.at[slot, 0])
        whole(edge_lat.at[slot], edge_recv.at[slot, 1])

    def finish_sides(kind):
        whole(out_lon.at[kind], edge_send.at[kind, 0])
        whole(out_lat.at[kind], edge_send.at[kind, 1])

    def send_corners(slot):
        for place, peer in enumerate(corners):
            remote(
                out_corner.at[place],
                edge_corner.at[slot, place],
                corner_sem.at[ITERS],
                corner_sem.at[slot],
                peer,
            ).start()

    def send_sum(buffer, me, sems, peers):
        for peer in peers:
            remote(buffer.at[me], buffer.at[me], sems.at[0], sems.at[1], peer).start()

    def receive_sum(buffer, sems):
        others = buffer.at[pl.ds(0, buffer.shape[0] - 1)]
        whole(others, sems.at[1])
        return jnp.sum(buffer[...], axis=0)

    def finish_sum(buffer, sems):
        whole(buffer.at[pl.ds(0, buffer.shape[0] - 1)], sems.at[0])

    me_far = chip * n_lat + lat
    has_prev = (lat > 0).astype(F32)
    has_next = (lat < n_lat - 1).astype(F32)

    def inner_stencil(turn):
        field = v_ref[...]
        around = shifted(
            field,
            edge_lon[turn, 0, 0],
            edge_lon[turn, 1, 0],
            to_column(edge_lat[turn, 0, 0] * has_prev, rows),
            to_column(edge_lat[turn, 1, 0] * has_next, rows),
        )
        u_ref[...] = prior_ref[...] * ((kappa_ref[...] + 4.0) * field - around)

    def inner_square():
        field = v_ref[...]
        nothing = jnp.zeros((1, cols), F32), jnp.zeros((rows, 1), F32)
        around = shifted(field, nothing[0], nothing[0], nothing[1], nothing[1])
        inner = (kappa_ref[...] + 4.0) * field - around
        lon_sides = inner[0:1, :], inner[rows - 1 : rows, :]
        lat_sides = to_row(inner[:, 0:1]), to_row(inner[:, cols - 1 : cols])
        return fold(prior_ref[...] * inner * inner), lon_sides, lat_sides

    def side_square(turn, lon_sides, lat_sides):
        lane_row = lax.broadcasted_iota(jnp.int32, (1, LANES), 1)
        total = jnp.zeros((1, LANES), F32)
        for side in (0, 1):
            beside, own = edge_lon[turn, side, 0], lon_sides[side]
            change = out_lon[1, 1 - side, 1] * beside * (beside - 2.0 * own)
            for at in range(0, cols, LANES):
                total += change[:, at : at + LANES]
        ends = edge_lon[turn, 0, 0], edge_lon[turn, 1, 0]
        for side, (at, present) in enumerate(((0, has_prev), (cols - 1, has_next))):
            beside, own = edge_lat[turn, side, 0] * present, lat_sides[side]
            own = own - jnp.where(lane_row == 0, ends[0][:, at : at + 1], 0.0)
            own = own - jnp.where(lane_row == rows - 1, ends[1][:, at : at + 1], 0.0)
            total += out_lat[1, 1 - side, 1] * beside * (beside - 2.0 * own)
        return total

    def outer_stencil(turn):
        lane_wide = lax.broadcasted_iota(jnp.int32, (1, cols), 1)
        lane_row = lax.broadcasted_iota(jnp.int32, (1, LANES), 1)
        present = (has_prev, has_next)
        own = to_row(v_ref[:, 0:1]), to_row(v_ref[:, cols - 1 : cols])
        beside_lon, beside_lat = [], []
        for side, at in ((0, 0), (1, rows - 1)):
            near, far = edge_lon[turn, side, 0], edge_lon[turn, side, 1]
            kappa, prior = edge_lon[ITERS, side, 0], edge_lon[ITERS, side, 1]
            first = edge_corner[turn, 2 * side][:, :1] * has_prev
            last = edge_corner[turn, 2 * side + 1][:, :1] * has_next
            south = jnp.where(lane_wide == 0, first, pltpu.roll(near, 1, 1))
            north = jnp.where(lane_wide == cols - 1, last, pltpu.roll(near, cols - 1, 1))
            around = far + v_ref[at : at + 1, :] + south + north
            beside_lon.append(prior * ((kappa + 4.0) * near - around))
        for side in (0, 1):
            near, far = edge_lat[turn, side, 0], edge_lat[turn, side, 1]
            kappa, prior = edge_lat[ITERS, side, 0], edge_lat[ITERS, side, 1]
            first, last = edge_corner[turn, side][:, :1], edge_corner[turn, 2 + side][:, :1]
            west = jnp.where(lane_row == 0, first, pltpu.roll(near, 1, 1))
            east = jnp.where(lane_row == rows - 1, last, pltpu.roll(near, LANES - 1, 1))
            around = far + own[side] + west + east
            value = prior * ((kappa + 4.0) * near - around) * present[side]
            beside_lat.append(to_column(value, rows))
        scaled = u_ref[...]
        return (kappa_ref[...] + 4.0) * scaled - shifted(scaled, *beside_lon, *beside_lat)

    padded_ref[...] = jnp.zeros(padded_ref.shape, F32)
    offset = lax.broadcasted_iota(jnp.int32, (PSIDE, cols), 1) - lax.broadcasted_iota(
        jnp.int32, (PSIDE, cols), 0
    )

    def one_selector(block, carry):
        start = pl.multiple_of(block * PSIDE, PSIDE)
        chosen = jnp.where(offset == lat_ref[0, block], 1.0, 0.0)
        select_ref[pl.ds(start, PSIDE), :] = chosen.astype(BF16)
        return carry

    loads[0].wait()
    lax.fori_loop(0, blocks, one_selector, 0, unroll=16)
    lane = lax.broadcasted_iota(jnp.int32, (ROWS, LANES), 1)
    chunk = lane // PSIDE
    cell = lax.broadcasted_iota(jnp.int32, (cols, LANES), 0)

    def one_turned(tile, carry):
        place = jnp.zeros((ROWS, LANES), jnp.int32)
        for block in range(PER_TILE):
            anchor = lat_ref[0, tile * PER_TILE + -block % PER_TILE]
            place = jnp.where(chunk == block, anchor, place)
        place = (place + lane % PSIDE)[:1]
        start = pl.multiple_of(tile * LANES, LANES)
        turned_ref[:, pl.ds(start, LANES)] = jnp.where(cell == place, 1.0, 0.0).astype(BF16)
        return carry

    lax.fori_loop(0, tiles, one_turned, 0, unroll=2)
    for copy in loads[2:]:
        copy.wait()
    slot = lax.broadcasted_iota(jnp.int32, (blocks, reads), 0)
    weights = jnp.where(slot < count_ref[...], weights_ref[...], 0.0)
    weights_ref[...] = weights
    term_ref[...] = weights * readings_ref[...]
    ids_row = jnp.broadcast_to(ids_ref[...].astype(F32), (blocks, blocks))
    ids_rows_ref[...] = jnp.transpose(ids_row)

    def gather(field):
        high, low = split(field)
        both = jnp.dot(
            jnp.concatenate([high, low], 0), turned_ref[...], preferred_element_type=F32
        )
        both = both[:rows] + both[rows:]
        for tile in range(tiles):
            columns_ref[tile] = both[:, tile * LANES : (tile + 1) * LANES]
        for tile in range(tiles):
            halves = []
            for half in range(2):
                picked = jnp.zeros((ROWS, LANES), F32)
                for place in range(PER_TILE):
                    start = lon_ref[0, tile * PER_TILE + -place % PER_TILE] + half * ROWS
                    window = columns_ref[tile, pl.ds(start, ROWS), :]
                    picked = jnp.where(chunk == place, window, picked)
                halves.append(picked)
            done = turn_blocks(jnp.stack(halves))
            for half in range(2):
                patch_ref[
                    tile * ROWS : (tile + 1) * ROWS, half * LANES : (half + 1) * LANES
                ] = done[half]

    def read():
        high, low = split(jnp.transpose(patch_ref[...]))
        patches = jnp.concatenate([high, low], 1)
        ids = jnp.broadcast_to(ids_ref[...], (ROWS, blocks))
        ids = jnp.concatenate([ids, ids], 1)
        acc = jnp.zeros((reads, 2 * blocks), F32)
        for kind in range(kinds):
            result = jnp.dot(templates_ref[kind], patches, preferred_element_type=F32)
            acc = jnp.where((ids == kind)[:1], result, acc)
        return jnp.transpose(acc[:, :blocks] + acc[:, blocks:])

    def spread(mixed):
        high, low = split(mixed)
        both = jnp.concatenate([high, low], 0)
        ids = ids_rows_ref[...].astype(BF16)
        ids = jnp.concatenate([ids, ids], 0)
        terms = jnp.zeros((2 * blocks, cells), F32)
        some = 8
        for first in range(0, kinds, some):
            left = [
                jnp.where(ids == kind, both, jnp.zeros_like(both))
                for kind in range(first, first + some)
            ]
            table = templates_ref[first : first + some].reshape(some * reads, cells)
            terms += jnp.dot(jnp.concatenate(left, 1), table, preferred_element_type=F32)
        terms = terms[:blocks] + terms[blocks:]
        lead = rows - PSIDE
        for half in range(2):
            part = terms[:, half * LANES : (half + 1) * LANES].reshape(tiles, ROWS, LANES)
            part = negate_rows(turn_blocks(part))
            padded_ref[:, lead + half * ROWS : lead + (half + 1) * ROWS, :] = part
        wide = lax.broadcasted_iota(jnp.int32, (rows, LANES), 1) // PSIDE

        def one_tile(tile, carry):
            picked = jnp.zeros((rows, LANES), F32)
            for place in range(PER_TILE):
                start = lead - lon_ref[0, tile * PER_TILE + place]
                window = padded_ref[tile, pl.ds(start, rows), :]
                picked = jnp.where(wide == place, window, picked)
            high, low = split(picked)
            start = pl.multiple_of(tile * LANES, LANES)
            spread_ref[0:rows, pl.ds(start, LANES)] = high
            spread_ref[rows : 2 * rows, pl.ds(start, LANES)] = low
            return carry

        lax.fori_loop(0, tiles, one_tile, 0, unroll=tiles)
        both = jnp.dot(spread_ref[...], select_ref[...], preferred_element_type=F32)
        return both[:rows] + both[rows:]

    row_at = lax.broadcasted_iota(jnp.int32, (ROWS, LANES), 0)

    def packed(parts, more):
        parts = [jnp.sum(part, axis=0, keepdims=True) for part in parts]
        parts[-1] = parts[-1] + more
        parts += [jnp.zeros((1, LANES), F32)] * (ROWS - len(parts))
        total = jnp.sum(jnp.concatenate(parts, 0), axis=1, keepdims=True)
        return jnp.sum(jnp.where(row_at == lane, total, 0.0), axis=0, keepdims=True)

    def unpacked(total, count):
        return [
            jnp.sum(jnp.where(lane[:1] == place, total, 0.0), axis=1, keepdims=True)
            for place in range(count)
        ]

    pack_coefficients(kappa_ref[...], prior_ref[...])
    loads[1].wait()

    def one_turn(turn, carry):
        image_ref[...] = spread(term_ref[...])

        @pl.when(turn == 1)
        def _():
            receive_sides(ITERS)

        @pl.when((turn > 0) & (turn < ITERS))
        def _():
            receive_sides(turn - 1)

        @pl.when(turn > 0)
        def _():
            inner_stencil(turn - 1)
            whole(edge_corner.at[turn - 1], corner_sem.at[turn - 1])

            @pl.when(turn == ITERS)
            def _():
                edge_corner[2] = edge_corner[1] - first_ref[...] * edge_corner[2]

            image_ref[...] += outer_stencil(turn - 1)
            finish_sides(0)
            whole(out_corner, corner_sem.at[ITERS])

        @pl.when(turn == 0)
        def _():
            pl.semaphore_wait(barrier, len(peers))

        @pl.when(turn < ITERS)
        def _():
            send_vector(image_ref, turn)

        @pl.when(turn == 0)
        def _():
            right = image_ref[...]
            r0_ref[...] = right
            v_ref[...] = right
            send_lon(1, ITERS)
            send_lat(1, ITERS)

        @pl.when(turn == 1)
        def _():
            image = image_ref[...]
            w0_ref[...] = image
            v_ref[...] = image

        @pl.when(turn == 2)
        def _():
            norm, curve = unpacked(receive_sum(first_b, first_b_sem), 2)
            step = norm / curve
            w0 = w0_ref[...]
            w1 = w0 - step * image_ref[...]
            r1_ref[...] = r0_ref[...] - step * w0
            w1_ref[...] = w1
            v_ref[...] = w1
            first_ref[...] = jnp.broadcast_to(step, (1, LANES))

        @pl.when(turn == ITERS)
        def _():
            g0, g1, d, b, c, e, a, f = unpacked(receive_sum(last_b, last_b_sem), 8)
            step = first_ref[:, 0:1]
            g2 = d
            l1, l2 = b / a, c / a
            d, e, f = d - l1 * b, e - l1 * c, f - l2 * c
            m = e / d
            f = f - m * e
            g1 = g1 - l1 * g0
            g2 = g2 - l2 * g0 - m * g1
            c2 = g2 / f
            c1 = g1 / d - m * c2
            c0 = g0 / a - l1 * c1 - l2 * c2
            w1, r1 = w1_ref[...], r1_ref[...]
            x_ref[...] = (step + c0) * r0_ref[...] + c1 * r1 + c2 * w1
            r_ref[...] = r1 - c0 * w0_ref[...] - c1 * w1 - c2 * image_ref[...]

        @pl.when(turn < ITERS)
        def _():
            gather(v_ref[...])

            @pl.when(turn == 1)
            def _():
                first_b[chip] = receive_sum(first_a, first_a_sem)
                send_sum(first_b, chip, first_b_sem, peers_b)

            image = read()
            mixed = weights_ref[...] * image
            term_ref[...] = mixed
            curve_ref[...] = fold(mixed * image)

            def curve():
                inside, lon_sides, lat_sides = inner_square()
                return curve_ref[...] + inside, lon_sides, lat_sides

            @pl.when(turn == 0)
            def _():
                parts = [fold(r0_ref[...] * r0_ref[...]), curve()[0]]
                first_a[me_a] = packed(parts, jnp.zeros((1, LANES), F32))
                send_sum(first_a, me_a, first_a_sem, peers_a)

            @pl.when(turn == 2)
            def _():
                r0, w0, r1, w1 = r0_ref[...], w0_ref[...], r1_ref[...], w1_ref[...]
                pairs = [(r0, r1), (r1, r1), (r1, w1), (r0, w1), (w0, w1), (w1, w1), (r0, w0)]
                inside, lon_sides, lat_sides = curve()
                parts = [fold(one * two) for one, two in pairs] + [inside]
                receive_sides(turn)
                step = first_ref[:, 0:1]
                edge_lon[2] = edge_lon[1] - step * edge_lon[2]
                edge_lat[2] = edge_lat[1] - step * edge_lat[2]
                last_a[core] = packed(parts, side_square(turn, lon_sides, lat_sides))
                send_sum(last_a, core, last_a_sem, [twin])
                last_b[me_far] = receive_sum(last_a, last_a_sem)
                send_sum(last_b, me_far, last_b_sem, peers_far)

        return carry

    lax.fori_loop(0, ITERS + 1, one_turn, 0)
    finish_sides(1)
    finish_sum(first_a, first_a_sem)
    finish_sum(first_b, first_b_sem)
    finish_sum(last_a, last_a_sem)
    finish_sum(last_b, last_b_sem)


def far_first(n_lat, chips_lon):
    side = max(1, round(chips_lon**0.5))

    def away(step, size):
        return min(step, size - step)

    steps = [
        (across, along)
        for across in range(n_lat)
        for along in range(chips_lon)
        if across or along
    ]

    def distance(step):
        across, along = step
        return away(across, n_lat) + away(along // side, side) + away(along % side, side)

    return sorted(steps, key=distance, reverse=True)


def hand_out(x_in, r_in, x_out, r_out, sem):
    copies = [
        pltpu.make_async_copy(x_in, x_out, sem.at[0]),
        pltpu.make_async_copy(r_in, r_out, sem.at[1]),
    ]
    for copy in copies:
        copy.start()
    for copy in copies:
        copy.wait()


def on_device(
    n_lon,
    n_lat,
    kappa_sq,
    prior_scale,
    templates,
    block_counts,
    anchor_lon,
    anchor_lat,
    template_ids,
    readings,
    noise_prec,
):
    rows, cols = kappa_sq.shape
    kinds, reads, cells = templates.shape
    blocks = template_ids.shape[1]
    tiles = blocks // PER_TILE
    group_a, chips_lon = 2 * n_lat, n_lon // 2
    chips = n_lat * chips_lon
    vmem = pl.BlockSpec(memory_space=pltpu.VMEM)
    dma = pltpu.SemaphoreType.DMA
    field = jax.ShapeDtypeStruct((rows, cols), F32)
    plane = pltpu.VMEM((rows, cols), F32)
    fields = pl.pallas_call(
        functools.partial(kernel, n_lon, n_lat),
        out_shape=(pltpu.VMEM((rows, cols), F32), pltpu.VMEM((rows, cols), F32)),
        in_specs=[pl.BlockSpec(memory_space=pl.ANY)] * 9,
        out_specs=(vmem, vmem),
        scratch_shapes=[
            plane,
            plane,
            pltpu.VMEM((kinds, reads, cells), BF16),
            pltpu.VMEM((1, 1), jnp.int32),
            pltpu.SMEM((1, blocks), jnp.int32),
            pltpu.SMEM((1, blocks), jnp.int32),
            pltpu.VMEM((1, blocks), jnp.int32),
            pltpu.VMEM((blocks, reads), F32),
            pltpu.VMEM((blocks, reads), F32),
            pltpu.VMEM((blocks * PSIDE, cols), BF16),
            pltpu.VMEM((cols, blocks * PSIDE), BF16),
            pltpu.VMEM((tiles, rows, LANES), F32),
            pltpu.VMEM((tiles, 2 * rows - PSIDE, LANES), F32),
            pltpu.VMEM((2 * rows, blocks * PSIDE), BF16),
            pltpu.VMEM((blocks, cells), F32),
            pltpu.VMEM((blocks, blocks), F32),
            pltpu.VMEM((blocks, reads), F32),
            plane,
            plane,
            plane,
            plane,
            plane,
            plane,
            plane,
            pltpu.VMEM((1, LANES), F32),
            pltpu.VMEM((ROWS, LANES), F32),
            pltpu.VMEM((2, 2, 2, 1, cols), F32),
            pltpu.VMEM((2, 2, 2, 1, LANES), F32),
            pltpu.VMEM((4, 1, LANES), F32),
            pltpu.VMEM((ITERS + 1, 2, 2, 1, cols), F32),
            pltpu.VMEM((ITERS + 1, 2, 2, 1, LANES), F32),
            pltpu.VMEM((ITERS, 4, 1, LANES), F32),
            pltpu.VMEM((group_a, 1, LANES), F32),
            pltpu.VMEM((chips_lon, 1, LANES), F32),
            pltpu.VMEM((2, 1, LANES), F32),
            pltpu.VMEM((chips, 1, LANES), F32),
            dma((9,)),
            dma((2, 2)),
            dma((ITERS + 1, 2)),
            dma((ITERS + 1,)),
            dma((2,)),
            dma((2,)),
            dma((2,)),
            dma((2,)),
        ],
        compiler_params=pltpu.CompilerParams(
            collective_id=0, has_side_effects=True, vmem_limit_bytes=56 * 1024 * 1024
        ),
    )(
        kappa_sq,
        prior_scale,
        templates,
        block_counts.reshape(1, 1),
        anchor_lon,
        anchor_lat,
        template_ids,
        readings[0],
        noise_prec[0],
    )
    return pl.pallas_call(
        hand_out,
        out_shape=(field, field),
        in_specs=[pl.BlockSpec(memory_space=pl.ANY)] * 2,
        out_specs=(pl.BlockSpec(memory_space=pl.ANY),) * 2,
        scratch_shapes=[dma((2,))],
        compiler_params=pltpu.CompilerParams(vmem_limit_bytes=1024 * 1024),
    )(*fields)


def solution(mesh):
    return jax.shard_map(
        functools.partial(on_device, mesh.shape["lon"], mesh.shape["lat"]),
        mesh=mesh,
        in_specs=(
            P("lon", "lat"),
            P("lon", "lat"),
            P(),
            P(("lon", "lat")),
            P("lon", "lat"),
            P("lon", "lat"),
            P("lon", "lat"),
            P("lon", "lat", None),
            P("lon", "lat", None),
        ),
        out_specs=(P("lon", "lat"), P("lon", "lat")),
        check_vma=False,
    )
```

```python
import functools

import jax
import jax.numpy as jnp
from jax import lax
from jax.experimental import pallas as pl
from jax.experimental.pallas import tpu as pltpu
from jax.sharding import PartitionSpec as P

PSIDE = 16
ITERS = 3
PART = 16
LANES = 128
ROWS = 8
PER_TILE = LANES // PSIDE
F32 = jnp.float32
BF16 = jnp.bfloat16
MESH = pl.DeviceIdType.MESH


def split(value):
    high = value.astype(BF16)
    low = (value - high.astype(F32)).astype(BF16)
    return high, low


def slide(value):
    chunk = lax.broadcasted_iota(jnp.int32, value.shape, 2) // PSIDE
    for k in (1, 2, 4):
        value = jnp.where((chunk // k) % 2 == 1, pltpu.roll(value, ROWS - k, 1), value)
    return value


def turn_blocks(value):
    return slide(pltpu.roll(slide(value), 0, 2, stride=PSIDE, stride_axis=1))


def negate_rows(value):
    row = lax.broadcasted_iota(jnp.int32, value.shape, 1)
    value = pltpu.roll(value, 4, 1)
    for k in (2, 1):
        ahead, behind = pltpu.roll(value, ROWS - k, 1), pltpu.roll(value, k, 1)
        value = jnp.where((row // k) % 2 == 0, ahead, behind)
    return pltpu.roll(value, 1, 1)


def fold(value):
    total = jnp.sum(value.reshape(value.shape[0] // ROWS, ROWS, value.shape[1]), axis=0)
    parts = [total[:, i : i + LANES] for i in range(0, total.shape[1], LANES)]
    return functools.reduce(jnp.add, parts)


def to_row(column):
    wide = jnp.broadcast_to(column, (column.shape[0], LANES))
    row = lax.broadcasted_iota(jnp.int32, wide.shape, 0)
    lane = lax.broadcasted_iota(jnp.int32, wide.shape, 1)
    return jnp.sum(jnp.where(row == lane, wide, 0.0), axis=0, keepdims=True)


def to_column(row_value, rows):
    wide = jnp.broadcast_to(row_value, (rows, LANES))
    row = lax.broadcasted_iota(jnp.int32, wide.shape, 0)
    lane = lax.broadcasted_iota(jnp.int32, wide.shape, 1)
    return jnp.sum(jnp.where(row == lane, wide, 0.0), axis=1, keepdims=True)


def shifted(field, prev_lon, next_lon, prev_lat, next_lat):
    rows, cols = field.shape
    row = lax.broadcasted_iota(jnp.int32, field.shape, 0)
    lane = lax.broadcasted_iota(jnp.int32, (rows, LANES), 1)
    west = jnp.where(row == 0, prev_lon, pltpu.roll(field, 1, 0))
    east = jnp.where(row == rows - 1, next_lon, pltpu.roll(field, rows - 1, 0))
    south = pltpu.roll(field, 1, 1)
    north = pltpu.roll(field, cols - 1, 1)
    first = jnp.where(lane == 0, prev_lat, south[:, :LANES])
    last = jnp.where(lane == LANES - 1, next_lat, north[:, cols - LANES :])
    south = jnp.concatenate([first, south[:, LANES:]], 1)
    north = jnp.concatenate([north[:, : cols - LANES], last], 1)
    return west + east + south + north


def kernel(
    n_lon,
    n_lat,
    kappa_hbm,
    prior_hbm,
    templates_hbm,
    count_hbm,
    lon_hbm,
    lat_hbm,
    ids_hbm,
    readings_hbm,
    noise_hbm,
    x_ref,
    r_ref,
    kappa_ref,
    prior_ref,
    templates_ref,
    count_ref,
    lon_ref,
    lat_ref,
    ids_ref,
    readings_ref,
    weights_ref,
    select_ref,
    turned_ref,
    columns_ref,
    padded_ref,
    patch_ref,
    ids_rows_ref,
    term_ref,
    terms_ref,
    r0_ref,
    w0_ref,
    r1_ref,
    w1_ref,
    image_ref,
    v_ref,
    u_ref,
    first_ref,
    pairs_ref,
    own_ref,
    out_lon,
    out_lat,
    out_corner,
    edge_lon,
    edge_lat,
    edge_corner,
    first_a,
    first_b,
    last_a,
    last_b,
    load_sem,
    template_sem,
    edge_send,
    edge_recv,
    corner_sem,
    first_a_sem,
    first_b_sem,
    last_a_sem,
    last_b_sem,
):
    kinds, reads, cells = templates_ref.shape
    rows, cols = kappa_ref.shape
    blocks = ids_ref.shape[1]
    tiles = blocks // PER_TILE
    lon, lat = lax.axis_index("lon"), lax.axis_index("lat")
    chips_lon = n_lon // 2
    core, chip = lon % 2, lon // 2

    loads = [
        pltpu.make_async_copy(source, target, load_sem.at[place])
        for place, (source, target) in enumerate(
            [
                (lat_hbm, lat_ref),
                (ids_hbm, ids_ref),
                (count_hbm, count_ref),
                (noise_hbm, weights_ref),
                (readings_hbm, readings_ref),
                (lon_hbm, lon_ref),
                (kappa_hbm, kappa_ref),
                (prior_hbm, prior_ref),
            ]
        )
    ]

    def template_part(part):
        some = pl.ds(part * PART, PART)
        return pltpu.make_async_copy(
            templates_hbm.at[some], templates_ref.at[some], template_sem.at[part]
        )

    for copy in loads[:5]:
        copy.start()
    for part in range(kinds // PART):
        template_part(part).start()
    for copy in loads[5:]:
        copy.start()

    me_a = lat * 2 + core
    group_a = 2 * n_lat

    def peer_a(step):
        index = (me_a + step) % group_a
        return (chip * 2 + index % 2, index // 2)

    peers_a = [peer_a(step) for step in range(1, group_a)]
    peers_b = [(((chip + step) % chips_lon) * 2 + core, lat) for step in range(1, chips_lon)]
    twin = (chip * 2 + 1 - core, lat)
    peers_far = [
        (((chip + along) % chips_lon) * 2 + core, (lat + across) % n_lat)
        for across, along in far_first(n_lat, chips_lon)
    ]
    lon_next, lon_prev = ((lon + 1) % n_lon, lat), ((lon + n_lon - 1) % n_lon, lat)
    lat_next, lat_prev = (lon, (lat + 1) % n_lat), (lon, (lat + n_lat - 1) % n_lat)
    corners = [(one[0], two[1]) for one in (lon_next, lon_prev) for two in (lat_next, lat_prev)]

    barrier = pltpu.get_barrier_semaphore()
    peers = [lon_next, lon_prev, lat_next, lat_prev] + corners + peers_a + peers_b
    for peer in peers:
        pl.semaphore_signal(barrier, inc=1, device_id=peer, device_id_type=MESH)

    def send_vector(ref, slot):
        for side, near, far in ((0, rows - 1, rows - 2), (1, 0, 1)):
            out_lon[0, side, 0] = ref[near : near + 1, :]
            out_lon[0, side, 1] = ref[far : far + 1, :]
        send_lon(0, slot)
        for side, at in ((0, cols - LANES), (1, 0)):
            near, far = ((0, 1), (LANES - 1, LANES - 2))[1 - side]
            tile = ref[:, at : at + LANES]
            out_lat[0, side, 0] = to_row(tile[:, near : near + 1])
            out_lat[0, side, 1] = to_row(tile[:, far : far + 1])
        send_lat(0, slot)
        for place, (row, col) in enumerate(
            [(rows - 1, cols - 1), (rows - 1, 0), (0, cols - 1), (0, 0)]
        ):
            value = ref[row : row + 1, col // LANES * LANES : col // LANES * LANES + LANES]
            lane_at = col % LANES
            out_corner[place] = jnp.broadcast_to(value[:, lane_at : lane_at + 1], (1, LANES))
        send_corners(slot)

    def pack_coefficients(kappa, prior):
        for place, field in enumerate((kappa, prior)):
            out_lon[1, 0, place] = field[rows - 1 : rows, :]
            out_lon[1, 1, place] = field[0:1, :]
            out_lat[1, 0, place] = to_row(field[:, cols - 1 : cols])
            out_lat[1, 1, place] = to_row(field[:, 0:1])

    def remote(src, dst, send_sem, recv_sem, peer):
        return pltpu.make_async_remote_copy(
            src_ref=src,
            dst_ref=dst,
            send_sem=send_sem,
            recv_sem=recv_sem,
            device_id=peer,
            device_id_type=MESH,
        )

    def whole(ref, sem):
        pltpu.make_async_copy(ref, ref, sem).wait()

    def send_lon(kind, slot):
        for side, peer in enumerate((lon_next, lon_prev)):
            remote(
                out_lon.at[kind, side],
                edge_lon.at[slot, side],
                edge_send.at[kind, 0],
                edge_recv.at[slot, 0],
                peer,
            ).start()

    def send_lat(kind, slot):
        for side, peer in enumerate((lat_next, lat_prev)):
            remote(
                out_lat.at[kind, side],
                edge_lat.at[slot, side],
                edge_send.at[kind, 1],
                edge_recv.at[slot, 1],
                peer,
            ).start()

    def receive_sides(slot):
        whole(edge_lon.at[slot], edge_recv.at[slot, 0])
        whole(edge_lat.at[slot], edge_recv.at[slot, 1])

    def finish_sides(kind):
        whole(out_lon.at[kind], edge_send.at[kind, 0])
        whole(out_lat.at[kind], edge_send.at[kind, 1])

    def send_corners(slot):
        for place, peer in enumerate(corners):
            remote(
                out_corner.at[place],
                edge_corner.at[slot, place],
                corner_sem.at[ITERS],
                corner_sem.at[slot],
                peer,
            ).start()

    def send_sum(buffer, me, sems, peers):
        for peer in peers:
            remote(buffer.at[me], buffer.at[me], sems.at[0], sems.at[1], peer).start()

    def receive_sum(buffer, sems):
        others = buffer.at[pl.ds(0, buffer.shape[0] - 1)]
        whole(others, sems.at[1])
        return jnp.sum(buffer[...], axis=0)

    def finish_sum(buffer, sems):
        whole(buffer.at[pl.ds(0, buffer.shape[0] - 1)], sems.at[0])

    me_far = chip * n_lat + lat
    has_prev = (lat > 0).astype(F32)
    has_next = (lat < n_lat - 1).astype(F32)

    def complete_inner(turn):
        for side, at in ((0, 0), (1, rows - 1)):
            change = prior_ref[at : at + 1, :] * edge_lon[turn, side, 0]
            u_ref[at : at + 1, :] = u_ref[at : at + 1, :] - change
        lane_tile = lax.broadcasted_iota(jnp.int32, (rows, LANES), 1)
        for side, (at, end, present) in enumerate(
            ((0, 0, has_prev), (cols - LANES, LANES - 1, has_next))
        ):
            beside = to_column(edge_lat[turn, side, 0] * present, rows)
            change = prior_ref[:, at : at + LANES] * jnp.where(lane_tile == end, beside, 0.0)
            u_ref[:, at : at + LANES] = u_ref[:, at : at + LANES] - change

    def inner_square():
        field = v_ref[...]
        nothing = jnp.zeros((1, cols), F32), jnp.zeros((rows, 1), F32)
        around = shifted(field, nothing[0], nothing[0], nothing[1], nothing[1])
        inner = (kappa_ref[...] + 4.0) * field - around
        lon_sides = inner[0:1, :], inner[rows - 1 : rows, :]
        lat_sides = to_row(inner[:, 0:1]), to_row(inner[:, cols - 1 : cols])
        scaled = prior_ref[...] * inner
        u_ref[...] = scaled
        own_ref[0] = to_row(field[:, 0:1])
        own_ref[1] = to_row(field[:, cols - 1 : cols])
        return fold(scaled * inner), lon_sides, lat_sides

    def side_square(turn, lon_sides, lat_sides):
        lane_row = lax.broadcasted_iota(jnp.int32, (1, LANES), 1)
        total = jnp.zeros((1, LANES), F32)
        for side in (0, 1):
            beside, own = edge_lon[turn, side, 0], lon_sides[side]
            change = out_lon[1, 1 - side, 1] * beside * (beside - 2.0 * own)
            for at in range(0, cols, LANES):
                total += change[:, at : at + LANES]
        ends = edge_lon[turn, 0, 0], edge_lon[turn, 1, 0]
        for side, (at, present) in enumerate(((0, has_prev), (cols - 1, has_next))):
            beside, own = edge_lat[turn, side, 0] * present, lat_sides[side]
            own = own - jnp.where(lane_row == 0, ends[0][:, at : at + 1], 0.0)
            own = own - jnp.where(lane_row == rows - 1, ends[1][:, at : at + 1], 0.0)
            total += out_lat[1, 1 - side, 1] * beside * (beside - 2.0 * own)
        return total

    def outer_stencil(turn):
        lane_wide = lax.broadcasted_iota(jnp.int32, (1, cols), 1)
        lane_row = lax.broadcasted_iota(jnp.int32, (1, LANES), 1)
        present = (has_prev, has_next)
        beside_lon, beside_lat = [], []
        for side, at in ((0, 0), (1, rows - 1)):
            near, far = edge_lon[turn, side, 0], edge_lon[turn, side, 1]
            kappa, prior = edge_lon[ITERS, side, 0], edge_lon[ITERS, side, 1]
            first = edge_corner[turn, 2 * side][:, :1] * has_prev
            last = edge_corner[turn, 2 * side + 1][:, :1] * has_next
            south = jnp.where(lane_wide == 0, first, pltpu.roll(near, 1, 1))
            north = jnp.where(lane_wide == cols - 1, last, pltpu.roll(near, cols - 1, 1))
            around = far + v_ref[at : at + 1, :] + south + north
            beside_lon.append(prior * ((kappa + 4.0) * near - around))
        for side in (0, 1):
            near, far = edge_lat[turn, side, 0], edge_lat[turn, side, 1]
            kappa, prior = edge_lat[ITERS, side, 0], edge_lat[ITERS, side, 1]
            first, last = edge_corner[turn, side][:, :1], edge_corner[turn, 2 + side][:, :1]
            west = jnp.where(lane_row == 0, first, pltpu.roll(near, 1, 1))
            east = jnp.where(lane_row == rows - 1, last, pltpu.roll(near, LANES - 1, 1))
            around = far + own_ref[side] + west + east
            value = prior * ((kappa + 4.0) * near - around) * present[side]
            beside_lat.append(to_column(value, rows))
        scaled = u_ref[...]
        return (kappa_ref[...] + 4.0) * scaled - shifted(scaled, *beside_lon, *beside_lat)

    padded_ref[...] = jnp.zeros(padded_ref.shape, F32)
    offset = lax.broadcasted_iota(jnp.int32, (PSIDE, cols), 1) - lax.broadcasted_iota(
        jnp.int32, (PSIDE, cols), 0
    )

    lane = lax.broadcasted_iota(jnp.int32, (ROWS, LANES), 1)
    chunk = lane // PSIDE
    cell = lax.broadcasted_iota(jnp.int32, (cols, LANES), 0)

    def selectors(tile):
        for block in range(PER_TILE):
            start = pl.multiple_of((tile * PER_TILE + block) * PSIDE, PSIDE)
            chosen = jnp.where(offset == lat_ref[0, tile * PER_TILE + block], 1.0, 0.0)
            select_ref[pl.ds(start, PSIDE), :] = chosen.astype(BF16)
        place = jnp.zeros((ROWS, LANES), jnp.int32)
        for block in range(PER_TILE):
            anchor = lat_ref[0, tile * PER_TILE + -block % PER_TILE]
            place = jnp.where(chunk == block, anchor, place)
        place = (place + lane % PSIDE)[:1]
        start = pl.multiple_of(tile * LANES, LANES)
        turned_ref[:, pl.ds(start, LANES)] = jnp.where(cell == place, 1.0, 0.0).astype(BF16)

    def twice(value):
        return jnp.concatenate([value, value], 0)

    def one_product(both, ids, first, count):
        left = [
            jnp.where(ids == jnp.asarray(first + kind).astype(BF16), both, jnp.zeros_like(both))
            for kind in range(count)
        ]
        table = templates_ref[pl.ds(first, count)].reshape(count * reads, cells)
        return jnp.dot(jnp.concatenate(left, 1), table, preferred_element_type=F32)

    for copy in loads[:5]:
        copy.wait()
    slot = lax.broadcasted_iota(jnp.int32, (blocks, reads), 0)
    weights = jnp.where(slot < count_ref[...], weights_ref[...], 0.0)
    weights_ref[...] = weights
    ids_row = jnp.broadcast_to(ids_ref[...].astype(F32), (blocks, blocks))
    ids_rows = jnp.transpose(ids_row)
    ids_rows_ref[...] = ids_rows
    weighted = jnp.concatenate(split(weights * readings_ref[...]), 0)
    ids_twice = twice(ids_rows.astype(BF16))
    terms_ref[...] = jnp.zeros(terms_ref.shape, F32)
    for ref in (r0_ref, w0_ref, r1_ref, w1_ref):
        ref[...] = jnp.zeros(ref.shape, F32)
    parts = kinds // PART

    def one_part(part, carry):
        template_part(part).wait()
        terms_ref[...] += one_product(weighted, ids_twice, part * PART, PART)
        for tile in range(tiles // parts):
            selectors(part * (tiles // parts) + tile)
        return carry

    lax.fori_loop(0, parts, one_part, 0)
    for copy in loads[5:]:
        copy.wait()

    def gather(field):
        field = jnp.concatenate(split(field), 0)
        some = 4
        for first in range(0, tiles, some):
            beside = turned_ref[:, first * LANES : (first + some) * LANES]
            both = jnp.dot(field, beside, preferred_element_type=F32)
            both = both[:rows] + both[rows:]
            for tile in range(some):
                columns_ref[first + tile] = both[:, tile * LANES : (tile + 1) * LANES]
            pick(first, some)

    def pick(first, some):
        for tile in range(first, first + some):
            halves = []
            for half in range(2):
                picked = jnp.zeros((ROWS, LANES), F32)
                for place in range(PER_TILE):
                    start = lon_ref[0, tile * PER_TILE + -place % PER_TILE] + half * ROWS
                    window = columns_ref[tile, pl.ds(start, ROWS), :]
                    picked = jnp.where(chunk == place, window, picked)
                halves.append(picked)
            done = turn_blocks(jnp.stack(halves))
            for half in range(2):
                patch_ref[
                    tile * ROWS : (tile + 1) * ROWS, half * LANES : (half + 1) * LANES
                ] = done[half]

    def read():
        high, low = split(jnp.transpose(patch_ref[...]))
        patches = jnp.concatenate([high, low], 1)
        ids = jnp.broadcast_to(ids_ref[...], (ROWS, blocks))
        ids = jnp.concatenate([ids, ids], 1)
        acc = jnp.zeros((reads, 2 * blocks), F32)
        for kind in range(kinds):
            result = jnp.dot(templates_ref[kind], patches, preferred_element_type=F32)
            acc = jnp.where((ids == kind)[:1], result, acc)
        return jnp.transpose(acc[:, :blocks] + acc[:, blocks:])

    def spread(turn):
        @pl.when(turn > 0)
        def _():
            both = jnp.concatenate(split(term_ref[...]), 0)
            ids = twice(ids_rows_ref[...].astype(BF16))
            terms = jnp.zeros((2 * blocks, cells), F32)
            some = 8
            for first in range(0, kinds, some):
                terms += one_product(both, ids, first, some)
            terms_ref[...] = terms

        terms = terms_ref[...]
        terms = terms[:blocks] + terms[blocks:]
        lead = rows - PSIDE
        for half in range(2):
            part = terms[:, half * LANES : (half + 1) * LANES].reshape(tiles, ROWS, LANES)
            part = negate_rows(turn_blocks(part))
            padded_ref[:, lead + half * ROWS : lead + (half + 1) * ROWS, :] = part
        wide = lax.broadcasted_iota(jnp.int32, (rows, LANES), 1) // PSIDE

        placed = []
        for tile in range(tiles):
            picked = jnp.zeros((rows, LANES), F32)
            for place in range(PER_TILE):
                start = lead - lon_ref[0, tile * PER_TILE + place]
                window = padded_ref[tile, pl.ds(start, rows), :]
                picked = jnp.where(wide == place, window, picked)
            placed.append(jnp.concatenate(split(picked), 0))
        both = jnp.dot(
            jnp.concatenate(placed, 1), select_ref[...], preferred_element_type=F32
        )
        return both[:rows] + both[rows:]

    row_at = lax.broadcasted_iota(jnp.int32, (ROWS, LANES), 0)

    def packed(parts, more):
        parts = [jnp.sum(part, axis=0, keepdims=True) for part in parts]
        parts[-1] = parts[-1] + more
        parts += [jnp.zeros((1, LANES), F32)] * (ROWS - len(parts))
        total = jnp.sum(jnp.concatenate(parts, 0), axis=1, keepdims=True)
        return jnp.sum(jnp.where(row_at == lane, total, 0.0), axis=0, keepdims=True)

    def unpacked(total, count):
        return [
            jnp.sum(jnp.where(lane[:1] == place, total, 0.0), axis=1, keepdims=True)
            for place in range(count)
        ]

    pack_coefficients(kappa_ref[...], prior_ref[...])

    def one_turn(turn, carry):
        image_ref[...] = spread(turn)

        @pl.when(turn == 1)
        def _():
            receive_sides(ITERS)

        @pl.when((turn > 0) & (turn < ITERS))
        def _():
            receive_sides(turn - 1)

        @pl.when(turn > 0)
        def _():
            complete_inner(turn - 1)
            whole(edge_corner.at[turn - 1], corner_sem.at[turn - 1])

            @pl.when(turn == ITERS)
            def _():
                edge_corner[2] = edge_corner[1] - first_ref[...] * edge_corner[2]

            image_ref[...] += outer_stencil(turn - 1)
            finish_sides(0)
            whole(out_corner, corner_sem.at[ITERS])

        @pl.when(turn == 0)
        def _():
            pl.semaphore_wait(barrier, len(peers))

        @pl.when(turn < ITERS)
        def _():
            send_vector(image_ref, turn)

        @pl.when(turn == 0)
        def _():
            right = image_ref[...]
            r0_ref[...] = right
            v_ref[...] = right
            send_lon(1, ITERS)
            send_lat(1, ITERS)

        @pl.when(turn == 1)
        def _():
            image = image_ref[...]
            w0_ref[...] = image
            v_ref[...] = image

        @pl.when(turn == 2)
        def _():
            norm, curve = unpacked(receive_sum(first_b, first_b_sem), 2)
            step = norm / curve
            w0 = w0_ref[...]
            w1 = w0 - step * image_ref[...]
            r1_ref[...] = r0_ref[...] - step * w0
            w1_ref[...] = w1
            v_ref[...] = w1
            first_ref[...] = jnp.broadcast_to(step, (1, LANES))

        @pl.when(turn == ITERS)
        def _():
            g0, g1, d, b, c, e, a, f = unpacked(receive_sum(last_b, last_b_sem), 8)
            step = first_ref[:, 0:1]
            g2 = d
            l1, l2 = b / a, c / a
            d, e, f = d - l1 * b, e - l1 * c, f - l2 * c
            m = e / d
            f = f - m * e
            g1 = g1 - l1 * g0
            g2 = g2 - l2 * g0 - m * g1
            c2 = g2 / f
            c1 = g1 / d - m * c2
            c0 = g0 / a - l1 * c1 - l2 * c2
            w1, r1 = w1_ref[...], r1_ref[...]
            x_ref[...] = (step + c0) * r0_ref[...] + c1 * r1 + c2 * w1
            r_ref[...] = r1 - c0 * w0_ref[...] - c1 * w1 - c2 * image_ref[...]

        @pl.when(turn < ITERS)
        def _():
            gather(v_ref[...])

            @pl.when(turn == 1)
            def _():
                first_b[chip] = receive_sum(first_a, first_a_sem)
                send_sum(first_b, chip, first_b_sem, peers_b)

            inside, lon_sides, lat_sides = inner_square()
            r0, w0, r1, w1 = r0_ref[...], w0_ref[...], r1_ref[...], w1_ref[...]
            pairs = [(r0, r1), (r1, r1), (r1, w1), (r0, w1), (w0, w1), (w1, w1), (r0, w0)]
            for place, (one, two) in enumerate(pairs):
                pairs_ref[place] = fold(one * two)
            image = read()
            mixed = weights_ref[...] * image
            term_ref[...] = mixed
            pairs_ref[len(pairs)] = inside + fold(mixed * image)

            @pl.when(turn == 0)
            def _():
                parts = [fold(r0_ref[...] * r0_ref[...]), pairs_ref[7]]
                first_a[me_a] = packed(parts, jnp.zeros((1, LANES), F32))
                send_sum(first_a, me_a, first_a_sem, peers_a)

            @pl.when(turn == 2)
            def _():
                parts = [pairs_ref[place] for place in range(8)]
                receive_sides(turn)
                step = first_ref[:, 0:1]
                edge_lon[2] = edge_lon[1] - step * edge_lon[2]
                edge_lat[2] = edge_lat[1] - step * edge_lat[2]
                last_a[core] = packed(parts, side_square(turn, lon_sides, lat_sides))
                send_sum(last_a, core, last_a_sem, [twin])
                last_b[me_far] = receive_sum(last_a, last_a_sem)
                send_sum(last_b, me_far, last_b_sem, peers_far)

        return carry

    lax.fori_loop(0, ITERS + 1, one_turn, 0)
    finish_sides(1)
    finish_sum(first_a, first_a_sem)
    finish_sum(first_b, first_b_sem)
    finish_sum(last_a, last_a_sem)
    finish_sum(last_b, last_b_sem)


def far_first(n_lat, chips_lon):
    side = max(1, round(chips_lon**0.5))

    def away(step, size):
        return min(step, size - step)

    steps = [
        (across, along)
        for across in range(n_lat)
        for along in range(chips_lon)
        if across or along
    ]

    def distance(step):
        across, along = step
        return away(across, n_lat) + away(along // side, side) + away(along % side, side)

    return sorted(steps, key=distance, reverse=True)


def hand_out(x_in, r_in, x_out, r_out, sem):
    copies = [
        pltpu.make_async_copy(x_in, x_out, sem.at[0]),
        pltpu.make_async_copy(r_in, r_out, sem.at[1]),
    ]
    for copy in copies:
        copy.start()
    for copy in copies:
        copy.wait()


def on_device(
    n_lon,
    n_lat,
    kappa_sq,
    prior_scale,
    templates,
    block_counts,
    anchor_lon,
    anchor_lat,
    template_ids,
    readings,
    noise_prec,
):
    rows, cols = kappa_sq.shape
    kinds, reads, cells = templates.shape
    blocks = template_ids.shape[1]
    tiles = blocks // PER_TILE
    group_a, chips_lon = 2 * n_lat, n_lon // 2
    chips = n_lat * chips_lon
    vmem = pl.BlockSpec(memory_space=pltpu.VMEM)
    dma = pltpu.SemaphoreType.DMA
    field = jax.ShapeDtypeStruct((rows, cols), F32)
    plane = pltpu.VMEM((rows, cols), F32)
    fields = pl.pallas_call(
        functools.partial(kernel, n_lon, n_lat),
        out_shape=(pltpu.VMEM((rows, cols), F32), pltpu.VMEM((rows, cols), F32)),
        in_specs=[pl.BlockSpec(memory_space=pl.ANY)] * 9,
        out_specs=(vmem, vmem),
        scratch_shapes=[
            plane,
            plane,
            pltpu.VMEM((kinds, reads, cells), BF16),
            pltpu.VMEM((1, 1), jnp.int32),
            pltpu.SMEM((1, blocks), jnp.int32),
            pltpu.SMEM((1, blocks), jnp.int32),
            pltpu.VMEM((1, blocks), jnp.int32),
            pltpu.VMEM((blocks, reads), F32),
            pltpu.VMEM((blocks, reads), F32),
            pltpu.VMEM((blocks * PSIDE, cols), BF16),
            pltpu.VMEM((cols, blocks * PSIDE), BF16),
            pltpu.VMEM((tiles, rows, LANES), F32),
            pltpu.VMEM((tiles, 2 * rows - PSIDE, LANES), F32),
            pltpu.VMEM((blocks, cells), F32),
            pltpu.VMEM((blocks, blocks), F32),
            pltpu.VMEM((blocks, reads), F32),
            pltpu.VMEM((2 * blocks, cells), F32),
            plane,
            plane,
            plane,
            plane,
            plane,
            plane,
            plane,
            pltpu.VMEM((1, LANES), F32),
            pltpu.VMEM((8, ROWS, LANES), F32),
            pltpu.VMEM((2, 1, LANES), F32),
            pltpu.VMEM((2, 2, 2, 1, cols), F32),
            pltpu.VMEM((2, 2, 2, 1, LANES), F32),
            pltpu.VMEM((4, 1, LANES), F32),
            pltpu.VMEM((ITERS + 1, 2, 2, 1, cols), F32),
            pltpu.VMEM((ITERS + 1, 2, 2, 1, LANES), F32),
            pltpu.VMEM((ITERS, 4, 1, LANES), F32),
            pltpu.VMEM((group_a, 1, LANES), F32),
            pltpu.VMEM((chips_lon, 1, LANES), F32),
            pltpu.VMEM((2, 1, LANES), F32),
            pltpu.VMEM((chips, 1, LANES), F32),
            dma((8,)),
            dma((kinds // PART,)),
            dma((2, 2)),
            dma((ITERS + 1, 2)),
            dma((ITERS + 1,)),
            dma((2,)),
            dma((2,)),
            dma((2,)),
            dma((2,)),
        ],
        compiler_params=pltpu.CompilerParams(
            collective_id=0, has_side_effects=True, vmem_limit_bytes=56 * 1024 * 1024
        ),
    )(
        kappa_sq,
        prior_scale,
        templates,
        block_counts.reshape(1, 1),
        anchor_lon,
        anchor_lat,
        template_ids,
        readings[0],
        noise_prec[0],
    )
    return pl.pallas_call(
        hand_out,
        out_shape=(field, field),
        in_specs=[pl.BlockSpec(memory_space=pl.ANY)] * 2,
        out_specs=(pl.BlockSpec(memory_space=pl.ANY),) * 2,
        scratch_shapes=[dma((2,))],
        compiler_params=pltpu.CompilerParams(vmem_limit_bytes=1024 * 1024),
    )(*fields)


def solution(mesh):
    return jax.shard_map(
        functools.partial(on_device, mesh.shape["lon"], mesh.shape["lat"]),
        mesh=mesh,
        in_specs=(
            P("lon", "lat"),
            P("lon", "lat"),
            P(),
            P(("lon", "lat")),
            P("lon", "lat"),
            P("lon", "lat"),
            P("lon", "lat"),
            P("lon", "lat", None),
            P("lon", "lat", None),
        ),
        out_specs=(P("lon", "lat"), P("lon", "lat")),
        check_vma=False,
    )
```

```python
import functools

import jax
import jax.numpy as jnp
from jax import lax
from jax.experimental import pallas as pl
from jax.experimental.pallas import tpu as pltpu
from jax.sharding import PartitionSpec as P

PSIDE = 16
ITERS = 3
PART = 16
LANES = 128
ROWS = 8
PER_TILE = LANES // PSIDE
F32 = jnp.float32
BF16 = jnp.bfloat16
MESH = pl.DeviceIdType.MESH


def split(value):
    high = value.astype(BF16)
    low = (value - high.astype(F32)).astype(BF16)
    return high, low


def slide(value):
    chunk = lax.broadcasted_iota(jnp.int32, value.shape, 2) // PSIDE
    for k in (1, 2, 4):
        value = jnp.where((chunk // k) % 2 == 1, pltpu.roll(value, ROWS - k, 1), value)
    return value


def turn_blocks(value):
    return slide(pltpu.roll(slide(value), 0, 2, stride=PSIDE, stride_axis=1))


def negate_rows(value):
    row = lax.broadcasted_iota(jnp.int32, value.shape, 1)
    value = pltpu.roll(value, 4, 1)
    for k in (2, 1):
        ahead, behind = pltpu.roll(value, ROWS - k, 1), pltpu.roll(value, k, 1)
        value = jnp.where((row // k) % 2 == 0, ahead, behind)
    return pltpu.roll(value, 1, 1)


def fold(value):
    total = jnp.sum(value.reshape(value.shape[0] // ROWS, ROWS, value.shape[1]), axis=0)
    parts = [total[:, i : i + LANES] for i in range(0, total.shape[1], LANES)]
    return functools.reduce(jnp.add, parts)


def to_row(column):
    wide = jnp.broadcast_to(column, (column.shape[0], LANES))
    row = lax.broadcasted_iota(jnp.int32, wide.shape, 0)
    lane = lax.broadcasted_iota(jnp.int32, wide.shape, 1)
    return jnp.sum(jnp.where(row == lane, wide, 0.0), axis=0, keepdims=True)


def to_column(row_value, rows):
    wide = jnp.broadcast_to(row_value, (rows, LANES))
    row = lax.broadcasted_iota(jnp.int32, wide.shape, 0)
    lane = lax.broadcasted_iota(jnp.int32, wide.shape, 1)
    return jnp.sum(jnp.where(row == lane, wide, 0.0), axis=1, keepdims=True)


def shifted(field, prev_lon, next_lon, prev_lat, next_lat):
    rows, cols = field.shape
    row = lax.broadcasted_iota(jnp.int32, field.shape, 0)
    lane = lax.broadcasted_iota(jnp.int32, (rows, LANES), 1)
    west = jnp.where(row == 0, prev_lon, pltpu.roll(field, 1, 0))
    east = jnp.where(row == rows - 1, next_lon, pltpu.roll(field, rows - 1, 0))
    south = pltpu.roll(field, 1, 1)
    north = pltpu.roll(field, cols - 1, 1)
    first = jnp.where(lane == 0, prev_lat, south[:, :LANES])
    last = jnp.where(lane == LANES - 1, next_lat, north[:, cols - LANES :])
    south = jnp.concatenate([first, south[:, LANES:]], 1)
    north = jnp.concatenate([north[:, : cols - LANES], last], 1)
    return west + east + south + north


def kernel(
    n_lon,
    n_lat,
    kappa_hbm,
    prior_hbm,
    templates_hbm,
    count_hbm,
    lon_hbm,
    lat_hbm,
    ids_hbm,
    readings_hbm,
    noise_hbm,
    x_ref,
    r_ref,
    kappa_ref,
    prior_ref,
    templates_ref,
    count_ref,
    lon_ref,
    lat_ref,
    ids_ref,
    readings_ref,
    weights_ref,
    select_ref,
    turned_ref,
    columns_ref,
    padded_ref,
    patch_ref,
    ids_rows_ref,
    term_ref,
    terms_ref,
    r0_ref,
    w0_ref,
    r1_ref,
    w1_ref,
    image_ref,
    v_ref,
    u_ref,
    first_ref,
    pairs_ref,
    own_ref,
    out_lon,
    out_lat,
    out_corner,
    edge_lon,
    edge_lat,
    edge_corner,
    first_a,
    first_b,
    last_a,
    last_b,
    load_sem,
    template_sem,
    edge_send,
    edge_recv,
    corner_sem,
    first_a_sem,
    first_b_sem,
    last_a_sem,
    last_b_sem,
):
    kinds, reads, cells = templates_ref.shape
    rows, cols = kappa_ref.shape
    blocks = ids_ref.shape[1]
    tiles = blocks // PER_TILE
    lon, lat = lax.axis_index("lon"), lax.axis_index("lat")
    chips_lon = n_lon // 2
    core, chip = lon % 2, lon // 2

    loads = [
        pltpu.make_async_copy(source, target, load_sem.at[place])
        for place, (source, target) in enumerate(
            [
                (lat_hbm, lat_ref),
                (ids_hbm, ids_ref),
                (count_hbm, count_ref),
                (noise_hbm, weights_ref),
                (readings_hbm, readings_ref),
                (lon_hbm, lon_ref),
                (kappa_hbm, kappa_ref),
                (prior_hbm, prior_ref),
            ]
        )
    ]

    def template_part(part):
        some = pl.ds(part * PART, PART)
        return pltpu.make_async_copy(
            templates_hbm.at[some], templates_ref.at[some], template_sem.at[part]
        )

    for copy in loads[:5]:
        copy.start()
    for part in range(kinds // PART):
        template_part(part).start()
    for copy in loads[5:]:
        copy.start()

    me_a = lat * 2 + core
    group_a = 2 * n_lat

    def peer_a(step):
        index = (me_a + step) % group_a
        return (chip * 2 + index % 2, index // 2)

    peers_a = [peer_a(step) for step in range(1, group_a)]
    peers_b = [(((chip + step) % chips_lon) * 2 + core, lat) for step in range(1, chips_lon)]
    twin = (chip * 2 + 1 - core, lat)
    peers_far = [
        (((chip + along) % chips_lon) * 2 + core, (lat + across) % n_lat)
        for across, along in far_first(n_lat, chips_lon)
    ]
    lon_next, lon_prev = ((lon + 1) % n_lon, lat), ((lon + n_lon - 1) % n_lon, lat)
    lat_next, lat_prev = (lon, (lat + 1) % n_lat), (lon, (lat + n_lat - 1) % n_lat)
    corners = [(one[0], two[1]) for one in (lon_next, lon_prev) for two in (lat_next, lat_prev)]

    barrier = pltpu.get_barrier_semaphore()
    peers = [lon_next, lon_prev, lat_next, lat_prev] + corners + peers_a + peers_b
    for peer in peers:
        pl.semaphore_signal(barrier, inc=1, device_id=peer, device_id_type=MESH)

    def send_vector(ref, slot):
        for side, near, far in ((0, rows - 1, rows - 2), (1, 0, 1)):
            out_lon[0, side, 0] = ref[near : near + 1, :]
            out_lon[0, side, 1] = ref[far : far + 1, :]
        send_lon(0, slot)
        for side, at in ((0, cols - LANES), (1, 0)):
            near, far = ((0, 1), (LANES - 1, LANES - 2))[1 - side]
            tile = ref[:, at : at + LANES]
            out_lat[0, side, 0] = to_row(tile[:, near : near + 1])
            out_lat[0, side, 1] = to_row(tile[:, far : far + 1])
        send_lat(0, slot)
        for place, (row, col) in enumerate(
            [(rows - 1, cols - 1), (rows - 1, 0), (0, cols - 1), (0, 0)]
        ):
            value = ref[row : row + 1, col // LANES * LANES : col // LANES * LANES + LANES]
            lane_at = col % LANES
            out_corner[place] = jnp.broadcast_to(value[:, lane_at : lane_at + 1], (1, LANES))
        send_corners(slot)

    def pack_coefficients(kappa, prior):
        for place, field in enumerate((kappa, prior)):
            out_lon[1, 0, place] = field[rows - 1 : rows, :]
            out_lon[1, 1, place] = field[0:1, :]
            out_lat[1, 0, place] = to_row(field[:, cols - 1 : cols])
            out_lat[1, 1, place] = to_row(field[:, 0:1])

    def remote(src, dst, send_sem, recv_sem, peer):
        return pltpu.make_async_remote_copy(
            src_ref=src,
            dst_ref=dst,
            send_sem=send_sem,
            recv_sem=recv_sem,
            device_id=peer,
            device_id_type=MESH,
        )

    def whole(ref, sem):
        pltpu.make_async_copy(ref, ref, sem).wait()

    def send_lon(kind, slot):
        for side, peer in enumerate((lon_next, lon_prev)):
            remote(
                out_lon.at[kind, side],
                edge_lon.at[slot, side],
                edge_send.at[kind, 0],
                edge_recv.at[slot, 0],
                peer,
            ).start()

    def send_lat(kind, slot):
        for side, peer in enumerate((lat_next, lat_prev)):
            remote(
                out_lat.at[kind, side],
                edge_lat.at[slot, side],
                edge_send.at[kind, 1],
                edge_recv.at[slot, 1],
                peer,
            ).start()

    def receive_sides(slot):
        whole(edge_lon.at[slot], edge_recv.at[slot, 0])
        whole(edge_lat.at[slot], edge_recv.at[slot, 1])

    def finish_sides(kind):
        whole(out_lon.at[kind], edge_send.at[kind, 0])
        whole(out_lat.at[kind], edge_send.at[kind, 1])

    def send_corners(slot):
        for place, peer in enumerate(corners):
            remote(
                out_corner.at[place],
                edge_corner.at[slot, place],
                corner_sem.at[ITERS],
                corner_sem.at[slot],
                peer,
            ).start()

    def send_sum(buffer, me, sems, peers):
        for peer in peers:
            remote(buffer.at[me], buffer.at[me], sems.at[0], sems.at[1], peer).start()

    def receive_sum(buffer, sems):
        others = buffer.at[pl.ds(0, buffer.shape[0] - 1)]
        whole(others, sems.at[1])
        return jnp.sum(buffer[...], axis=0)

    def finish_sum(buffer, sems):
        whole(buffer.at[pl.ds(0, buffer.shape[0] - 1)], sems.at[0])

    me_far = chip * n_lat + lat
    has_prev = (lat > 0).astype(F32)
    has_next = (lat < n_lat - 1).astype(F32)

    def complete_inner(turn):
        for side, at in ((0, 0), (1, rows - 1)):
            change = prior_ref[at : at + 1, :] * edge_lon[turn, side, 0]
            u_ref[at : at + 1, :] = u_ref[at : at + 1, :] - change
        lane_tile = lax.broadcasted_iota(jnp.int32, (rows, LANES), 1)
        for side, (at, end, present) in enumerate(
            ((0, 0, has_prev), (cols - LANES, LANES - 1, has_next))
        ):
            beside = to_column(edge_lat[turn, side, 0] * present, rows)
            change = prior_ref[:, at : at + LANES] * jnp.where(lane_tile == end, beside, 0.0)
            u_ref[:, at : at + LANES] = u_ref[:, at : at + LANES] - change

    def inner_square():
        field = v_ref[...]
        nothing = jnp.zeros((1, cols), F32), jnp.zeros((rows, 1), F32)
        around = shifted(field, nothing[0], nothing[0], nothing[1], nothing[1])
        inner = (kappa_ref[...] + 4.0) * field - around
        lon_sides = inner[0:1, :], inner[rows - 1 : rows, :]
        lat_sides = to_row(inner[:, 0:1]), to_row(inner[:, cols - 1 : cols])
        scaled = prior_ref[...] * inner
        u_ref[...] = scaled
        own_ref[0] = to_row(field[:, 0:1])
        own_ref[1] = to_row(field[:, cols - 1 : cols])
        return fold(scaled * inner), lon_sides, lat_sides

    def side_square(turn, lon_sides, lat_sides):
        lane_row = lax.broadcasted_iota(jnp.int32, (1, LANES), 1)
        total = jnp.zeros((1, LANES), F32)
        for side in (0, 1):
            beside, own = edge_lon[turn, side, 0], lon_sides[side]
            change = out_lon[1, 1 - side, 1] * beside * (beside - 2.0 * own)
            for at in range(0, cols, LANES):
                total += change[:, at : at + LANES]
        ends = edge_lon[turn, 0, 0], edge_lon[turn, 1, 0]
        for side, (at, present) in enumerate(((0, has_prev), (cols - 1, has_next))):
            beside, own = edge_lat[turn, side, 0] * present, lat_sides[side]
            own = own - jnp.where(lane_row == 0, ends[0][:, at : at + 1], 0.0)
            own = own - jnp.where(lane_row == rows - 1, ends[1][:, at : at + 1], 0.0)
            total += out_lat[1, 1 - side, 1] * beside * (beside - 2.0 * own)
        return total

    def outer_stencil(turn):
        lane_wide = lax.broadcasted_iota(jnp.int32, (1, cols), 1)
        lane_row = lax.broadcasted_iota(jnp.int32, (1, LANES), 1)
        present = (has_prev, has_next)
        beside_lon, beside_lat = [], []
        for side, at in ((0, 0), (1, rows - 1)):
            near, far = edge_lon[turn, side, 0], edge_lon[turn, side, 1]
            kappa, prior = edge_lon[ITERS, side, 0], edge_lon[ITERS, side, 1]
            first = edge_corner[turn, 2 * side][:, :1] * has_prev
            last = edge_corner[turn, 2 * side + 1][:, :1] * has_next
            south = jnp.where(lane_wide == 0, first, pltpu.roll(near, 1, 1))
            north = jnp.where(lane_wide == cols - 1, last, pltpu.roll(near, cols - 1, 1))
            around = far + v_ref[at : at + 1, :] + south + north
            beside_lon.append(prior * ((kappa + 4.0) * near - around))
        for side in (0, 1):
            near, far = edge_lat[turn, side, 0], edge_lat[turn, side, 1]
            kappa, prior = edge_lat[ITERS, side, 0], edge_lat[ITERS, side, 1]
            first, last = edge_corner[turn, side][:, :1], edge_corner[turn, 2 + side][:, :1]
            west = jnp.where(lane_row == 0, first, pltpu.roll(near, 1, 1))
            east = jnp.where(lane_row == rows - 1, last, pltpu.roll(near, LANES - 1, 1))
            around = far + own_ref[side] + west + east
            value = prior * ((kappa + 4.0) * near - around) * present[side]
            beside_lat.append(to_column(value, rows))
        scaled = u_ref[...]
        return (kappa_ref[...] + 4.0) * scaled - shifted(scaled, *beside_lon, *beside_lat)

    padded_ref[...] = jnp.zeros(padded_ref.shape, F32)
    offset = lax.broadcasted_iota(jnp.int32, (PSIDE, cols), 1) - lax.broadcasted_iota(
        jnp.int32, (PSIDE, cols), 0
    )

    lane = lax.broadcasted_iota(jnp.int32, (ROWS, LANES), 1)
    chunk = lane // PSIDE
    cell = lax.broadcasted_iota(jnp.int32, (cols, LANES), 0)

    def selectors(tile):
        for block in range(PER_TILE):
            start = pl.multiple_of((tile * PER_TILE + block) * PSIDE, PSIDE)
            chosen = jnp.where(offset == lat_ref[0, tile * PER_TILE + block], 1.0, 0.0)
            select_ref[pl.ds(start, PSIDE), :] = chosen.astype(BF16)
        place = jnp.zeros((ROWS, LANES), jnp.int32)
        for block in range(PER_TILE):
            anchor = lat_ref[0, tile * PER_TILE + -block % PER_TILE]
            place = jnp.where(chunk == block, anchor, place)
        place = (place + lane % PSIDE)[:1]
        start = pl.multiple_of(tile * LANES, LANES)
        turned_ref[:, pl.ds(start, LANES)] = jnp.where(cell == place, 1.0, 0.0).astype(BF16)

    def twice(value):
        return jnp.concatenate([value, value], 0)

    def one_product(both, ids, first, count):
        left = [
            jnp.where(ids == jnp.asarray(first + kind).astype(BF16), both, jnp.zeros_like(both))
            for kind in range(count)
        ]
        table = templates_ref[pl.ds(first, count)].reshape(count * reads, cells)
        return jnp.dot(jnp.concatenate(left, 1), table, preferred_element_type=F32)

    terms_ref[...] = jnp.zeros(terms_ref.shape, F32)
    for ref in (r0_ref, w0_ref, r1_ref, w1_ref):
        ref[...] = jnp.zeros(ref.shape, F32)
    for copy in loads[:5]:
        copy.wait()
    slot = lax.broadcasted_iota(jnp.int32, (blocks, reads), 0)
    weights = jnp.where(slot < count_ref[...], weights_ref[...], 0.0)
    weights_ref[...] = weights
    ids_row = jnp.broadcast_to(ids_ref[...].astype(F32), (blocks, blocks))
    ids_rows = jnp.transpose(ids_row)
    ids_rows_ref[...] = ids_rows
    weighted = jnp.concatenate(split(weights * readings_ref[...]), 0)
    ids_twice = twice(ids_rows.astype(BF16))
    parts = kinds // PART

    def one_part(part, carry):
        template_part(part).wait()
        terms_ref[...] += one_product(weighted, ids_twice, part * PART, PART)
        for tile in range(tiles // parts):
            selectors(part * (tiles // parts) + tile)
        return carry

    lax.fori_loop(0, parts, one_part, 0)
    for copy in loads[5:]:
        copy.wait()

    def gather(field):
        field = jnp.concatenate(split(field), 0)
        some = 4
        for first in range(0, tiles, some):
            beside = turned_ref[:, first * LANES : (first + some) * LANES]
            both = jnp.dot(field, beside, preferred_element_type=F32)
            both = both[:rows] + both[rows:]
            for tile in range(some):
                columns_ref[first + tile] = both[:, tile * LANES : (tile + 1) * LANES]
            pick(first, some)

    def pick(first, some):
        for tile in range(first, first + some):
            halves = []
            for half in range(2):
                picked = jnp.zeros((ROWS, LANES), F32)
                for place in range(PER_TILE):
                    start = lon_ref[0, tile * PER_TILE + -place % PER_TILE] + half * ROWS
                    window = columns_ref[tile, pl.ds(start, ROWS), :]
                    picked = jnp.where(chunk == place, window, picked)
                halves.append(picked)
            done = turn_blocks(jnp.stack(halves))
            for half in range(2):
                patch_ref[
                    tile * ROWS : (tile + 1) * ROWS, half * LANES : (half + 1) * LANES
                ] = done[half]

    def read():
        high, low = split(jnp.transpose(patch_ref[...]))
        patches = jnp.concatenate([high, low], 1)
        ids = jnp.broadcast_to(ids_ref[...], (ROWS, blocks))
        ids = jnp.concatenate([ids, ids], 1)
        acc = jnp.zeros((reads, 2 * blocks), F32)
        for kind in range(kinds):
            result = jnp.dot(templates_ref[kind], patches, preferred_element_type=F32)
            acc = jnp.where((ids == kind)[:1], result, acc)
        return jnp.transpose(acc[:, :blocks] + acc[:, blocks:])

    def spread(turn):
        @pl.when(turn > 0)
        def _():
            both = jnp.concatenate(split(term_ref[...]), 0)
            ids = twice(ids_rows_ref[...].astype(BF16))
            terms = jnp.zeros((2 * blocks, cells), F32)
            some = 8
            for first in range(0, kinds, some):
                terms += one_product(both, ids, first, some)
            terms_ref[...] = terms

        terms = terms_ref[...]
        terms = terms[:blocks] + terms[blocks:]
        lead = rows - PSIDE
        for half in range(2):
            part = terms[:, half * LANES : (half + 1) * LANES].reshape(tiles, ROWS, LANES)
            part = negate_rows(turn_blocks(part))
            padded_ref[:, lead + half * ROWS : lead + (half + 1) * ROWS, :] = part
        wide = lax.broadcasted_iota(jnp.int32, (rows, LANES), 1) // PSIDE

        placed = []
        for tile in range(tiles):
            picked = jnp.zeros((rows, LANES), F32)
            for place in range(PER_TILE):
                start = lead - lon_ref[0, tile * PER_TILE + place]
                window = padded_ref[tile, pl.ds(start, rows), :]
                picked = jnp.where(wide == place, window, picked)
            placed.append(jnp.concatenate(split(picked), 0))
        both = jnp.dot(
            jnp.concatenate(placed, 1), select_ref[...], preferred_element_type=F32
        )
        return both[:rows] + both[rows:]

    row_at = lax.broadcasted_iota(jnp.int32, (ROWS, LANES), 0)

    def packed(parts):
        parts = [jnp.sum(part, axis=0, keepdims=True) for part in parts]
        parts += [jnp.zeros((1, LANES), F32)] * (ROWS - len(parts))
        total = jnp.sum(jnp.concatenate(parts, 0), axis=1, keepdims=True)
        return jnp.sum(jnp.where(row_at == lane, total, 0.0), axis=0, keepdims=True)

    def unpacked(total, count):
        return [
            jnp.sum(jnp.where(lane[:1] == place, total, 0.0), axis=1, keepdims=True)
            for place in range(count)
        ]

    pack_coefficients(kappa_ref[...], prior_ref[...])

    def one_turn(turn, carry):
        image_ref[...] = spread(turn)

        @pl.when(turn == 1)
        def _():
            receive_sides(ITERS)

        @pl.when((turn > 0) & (turn < ITERS))
        def _():
            receive_sides(turn - 1)

        @pl.when(turn > 0)
        def _():
            complete_inner(turn - 1)
            whole(edge_corner.at[turn - 1], corner_sem.at[turn - 1])

            @pl.when(turn == ITERS)
            def _():
                edge_corner[2] = edge_corner[1] - first_ref[...] * edge_corner[2]

            image_ref[...] += outer_stencil(turn - 1)
            finish_sides(0)
            whole(out_corner, corner_sem.at[ITERS])

        @pl.when(turn == 0)
        def _():
            pl.semaphore_wait(barrier, len(peers))

        @pl.when(turn < ITERS)
        def _():
            send_vector(image_ref, turn)

        @pl.when(turn == 0)
        def _():
            right = image_ref[...]
            r0_ref[...] = right
            v_ref[...] = right
            send_lon(1, ITERS)
            send_lat(1, ITERS)

        @pl.when(turn == 1)
        def _():
            image = image_ref[...]
            w0_ref[...] = image
            v_ref[...] = image

        @pl.when(turn == 2)
        def _():
            norm, curve = unpacked(receive_sum(first_b, first_b_sem), 2)
            step = norm / curve
            w0 = w0_ref[...]
            w1 = w0 - step * image_ref[...]
            r1_ref[...] = r0_ref[...] - step * w0
            w1_ref[...] = w1
            v_ref[...] = w1
            first_ref[...] = jnp.broadcast_to(step, (1, LANES))

        @pl.when(turn == ITERS)
        def _():
            g0, g1, d, b, c, e, a, f = unpacked(receive_sum(last_b, last_b_sem), 8)
            step = first_ref[:, 0:1]
            g2 = d
            l1, l2 = b / a, c / a
            d, e, f = d - l1 * b, e - l1 * c, f - l2 * c
            m = e / d
            f = f - m * e
            g1 = g1 - l1 * g0
            g2 = g2 - l2 * g0 - m * g1
            c2 = g2 / f
            c1 = g1 / d - m * c2
            c0 = g0 / a - l1 * c1 - l2 * c2
            w1, r1 = w1_ref[...], r1_ref[...]
            x_ref[...] = (step + c0) * r0_ref[...] + c1 * r1 + c2 * w1
            r_ref[...] = r1 - c0 * w0_ref[...] - c1 * w1 - c2 * image_ref[...]

        @pl.when(turn < ITERS)
        def _():
            gather(v_ref[...])

            @pl.when(turn == 1)
            def _():
                first_b[chip] = receive_sum(first_a, first_a_sem)
                send_sum(first_b, chip, first_b_sem, peers_b)

            inside, lon_sides, lat_sides = inner_square()
            r0, w0, r1, w1 = r0_ref[...], w0_ref[...], r1_ref[...], w1_ref[...]
            pairs = [(r0, r1), (r1, r1), (r1, w1), (r0, w1), (w0, w1), (w1, w1), (r0, w0)]
            for place, (one, two) in enumerate(pairs):
                pairs_ref[place] = fold(one * two)
            image = read()
            mixed = weights_ref[...] * image
            term_ref[...] = mixed
            pairs_ref[len(pairs)] = inside + fold(mixed * image)

            @pl.when(turn == 0)
            def _():
                parts = [fold(r0_ref[...] * r0_ref[...]), pairs_ref[7]]
                first_a[me_a] = packed(parts)
                send_sum(first_a, me_a, first_a_sem, peers_a)

            @pl.when(turn == 2)
            def _():
                known = packed([pairs_ref[place] for place in range(8)])
                receive_sides(turn)
                step = first_ref[:, 0:1]
                edge_lon[2] = edge_lon[1] - step * edge_lon[2]
                edge_lat[2] = edge_lat[1] - step * edge_lat[2]
                more = side_square(turn, lon_sides, lat_sides)
                more = jnp.sum(more, axis=1, keepdims=True)
                last_a[core] = known + jnp.where(lane[:1] == 7, more, 0.0)
                send_sum(last_a, core, last_a_sem, [twin])
                last_b[me_far] = receive_sum(last_a, last_a_sem)
                send_sum(last_b, me_far, last_b_sem, peers_far)

        return carry

    lax.fori_loop(0, ITERS + 1, one_turn, 0)
    finish_sides(1)
    finish_sum(first_a, first_a_sem)
    finish_sum(first_b, first_b_sem)
    finish_sum(last_a, last_a_sem)
    finish_sum(last_b, last_b_sem)


def far_first(n_lat, chips_lon):
    side = max(1, round(chips_lon**0.5))

    def away(step, size):
        return min(step, size - step)

    steps = [
        (across, along)
        for across in range(n_lat)
        for along in range(chips_lon)
        if across or along
    ]

    def distance(step):
        across, along = step
        return away(across, n_lat) + away(along // side, side) + away(along % side, side)

    return sorted(steps, key=distance, reverse=True)


def hand_out(x_in, r_in, x_out, r_out, sem):
    copies = [
        pltpu.make_async_copy(x_in, x_out, sem.at[0]),
        pltpu.make_async_copy(r_in, r_out, sem.at[1]),
    ]
    for copy in copies:
        copy.start()
    for copy in copies:
        copy.wait()


def on_device(
    n_lon,
    n_lat,
    kappa_sq,
    prior_scale,
    templates,
    block_counts,
    anchor_lon,
    anchor_lat,
    template_ids,
    readings,
    noise_prec,
):
    rows, cols = kappa_sq.shape
    kinds, reads, cells = templates.shape
    blocks = template_ids.shape[1]
    tiles = blocks // PER_TILE
    group_a, chips_lon = 2 * n_lat, n_lon // 2
    chips = n_lat * chips_lon
    vmem = pl.BlockSpec(memory_space=pltpu.VMEM)
    dma = pltpu.SemaphoreType.DMA
    field = jax.ShapeDtypeStruct((rows, cols), F32)
    plane = pltpu.VMEM((rows, cols), F32)
    fields = pl.pallas_call(
        functools.partial(kernel, n_lon, n_lat),
        out_shape=(pltpu.VMEM((rows, cols), F32), pltpu.VMEM((rows, cols), F32)),
        in_specs=[pl.BlockSpec(memory_space=pl.ANY)] * 9,
        out_specs=(vmem, vmem),
        scratch_shapes=[
            plane,
            plane,
            pltpu.VMEM((kinds, reads, cells), BF16),
            pltpu.VMEM((1, 1), jnp.int32),
            pltpu.SMEM((1, blocks), jnp.int32),
            pltpu.SMEM((1, blocks), jnp.int32),
            pltpu.VMEM((1, blocks), jnp.int32),
            pltpu.VMEM((blocks, reads), F32),
            pltpu.VMEM((blocks, reads), F32),
            pltpu.VMEM((blocks * PSIDE, cols), BF16),
            pltpu.VMEM((cols, blocks * PSIDE), BF16),
            pltpu.VMEM((tiles, rows, LANES), F32),
            pltpu.VMEM((tiles, 2 * rows - PSIDE, LANES), F32),
            pltpu.VMEM((blocks, cells), F32),
            pltpu.VMEM((blocks, blocks), F32),
            pltpu.VMEM((blocks, reads), F32),
            pltpu.VMEM((2 * blocks, cells), F32),
            plane,
            plane,
            plane,
            plane,
            plane,
            plane,
            plane,
            pltpu.VMEM((1, LANES), F32),
            pltpu.VMEM((8, ROWS, LANES), F32),
            pltpu.VMEM((2, 1, LANES), F32),
            pltpu.VMEM((2, 2, 2, 1, cols), F32),
            pltpu.VMEM((2, 2, 2, 1, LANES), F32),
            pltpu.VMEM((4, 1, LANES), F32),
            pltpu.VMEM((ITERS + 1, 2, 2, 1, cols), F32),
            pltpu.VMEM((ITERS + 1, 2, 2, 1, LANES), F32),
            pltpu.VMEM((ITERS, 4, 1, LANES), F32),
            pltpu.VMEM((group_a, 1, LANES), F32),
            pltpu.VMEM((chips_lon, 1, LANES), F32),
            pltpu.VMEM((2, 1, LANES), F32),
            pltpu.VMEM((chips, 1, LANES), F32),
            dma((8,)),
            dma((kinds // PART,)),
            dma((2, 2)),
            dma((ITERS + 1, 2)),
            dma((ITERS + 1,)),
            dma((2,)),
            dma((2,)),
            dma((2,)),
            dma((2,)),
        ],
        compiler_params=pltpu.CompilerParams(
            collective_id=0, has_side_effects=True, vmem_limit_bytes=56 * 1024 * 1024
        ),
    )(
        kappa_sq,
        prior_scale,
        templates,
        block_counts.reshape(1, 1),
        anchor_lon,
        anchor_lat,
        template_ids,
        readings[0],
        noise_prec[0],
    )
    return pl.pallas_call(
        hand_out,
        out_shape=(field, field),
        in_specs=[pl.BlockSpec(memory_space=pl.ANY)] * 2,
        out_specs=(pl.BlockSpec(memory_space=pl.ANY),) * 2,
        scratch_shapes=[dma((2,))],
        compiler_params=pltpu.CompilerParams(vmem_limit_bytes=1024 * 1024),
    )(*fields)


def solution(mesh):
    return jax.shard_map(
        functools.partial(on_device, mesh.shape["lon"], mesh.shape["lat"]),
        mesh=mesh,
        in_specs=(
            P("lon", "lat"),
            P("lon", "lat"),
            P(),
            P(("lon", "lat")),
            P("lon", "lat"),
            P("lon", "lat"),
            P("lon", "lat"),
            P("lon", "lat", None),
            P("lon", "lat", None),
        ),
        out_specs=(P("lon", "lat"), P("lon", "lat")),
        check_vma=False,
    )
```

```python
import functools

import jax
import jax.numpy as jnp
from jax import lax
from jax.experimental import pallas as pl
from jax.experimental.pallas import tpu as pltpu
from jax.sharding import PartitionSpec as P

PSIDE = 16
ITERS = 3
PART = 16
LANES = 128
ROWS = 8
PER_TILE = LANES // PSIDE
F32 = jnp.float32
BF16 = jnp.bfloat16
MESH = pl.DeviceIdType.MESH


def split(value):
    high = value.astype(BF16)
    low = (value - high.astype(F32)).astype(BF16)
    return high, low


def slide(value):
    chunk = lax.broadcasted_iota(jnp.int32, value.shape, 2) // PSIDE
    for k in (1, 2, 4):
        value = jnp.where((chunk // k) % 2 == 1, pltpu.roll(value, ROWS - k, 1), value)
    return value


def turn_blocks(value):
    return slide(pltpu.roll(slide(value), 0, 2, stride=PSIDE, stride_axis=1))


def negate_rows(value):
    row = lax.broadcasted_iota(jnp.int32, value.shape, 1)
    value = pltpu.roll(value, 4, 1)
    for k in (2, 1):
        ahead, behind = pltpu.roll(value, ROWS - k, 1), pltpu.roll(value, k, 1)
        value = jnp.where((row // k) % 2 == 0, ahead, behind)
    return pltpu.roll(value, 1, 1)


def fold(value):
    total = jnp.sum(value.reshape(value.shape[0] // ROWS, ROWS, value.shape[1]), axis=0)
    parts = [total[:, i : i + LANES] for i in range(0, total.shape[1], LANES)]
    return functools.reduce(jnp.add, parts)


def to_row(column):
    wide = jnp.broadcast_to(column, (column.shape[0], LANES))
    row = lax.broadcasted_iota(jnp.int32, wide.shape, 0)
    lane = lax.broadcasted_iota(jnp.int32, wide.shape, 1)
    return jnp.sum(jnp.where(row == lane, wide, 0.0), axis=0, keepdims=True)


def to_column(row_value, rows):
    wide = jnp.broadcast_to(row_value, (rows, LANES))
    row = lax.broadcasted_iota(jnp.int32, wide.shape, 0)
    lane = lax.broadcasted_iota(jnp.int32, wide.shape, 1)
    return jnp.sum(jnp.where(row == lane, wide, 0.0), axis=1, keepdims=True)


def shifted(field, prev_lon, next_lon, prev_lat, next_lat):
    rows, cols = field.shape
    row = lax.broadcasted_iota(jnp.int32, field.shape, 0)
    lane = lax.broadcasted_iota(jnp.int32, (rows, LANES), 1)
    west = jnp.where(row == 0, prev_lon, pltpu.roll(field, 1, 0))
    east = jnp.where(row == rows - 1, next_lon, pltpu.roll(field, rows - 1, 0))
    south = pltpu.roll(field, 1, 1)
    north = pltpu.roll(field, cols - 1, 1)
    first = jnp.where(lane == 0, prev_lat, south[:, :LANES])
    last = jnp.where(lane == LANES - 1, next_lat, north[:, cols - LANES :])
    south = jnp.concatenate([first, south[:, LANES:]], 1)
    north = jnp.concatenate([north[:, : cols - LANES], last], 1)
    return west + east + south + north


def kernel(
    n_lon,
    n_lat,
    kappa_hbm,
    prior_hbm,
    templates_hbm,
    count_hbm,
    lon_hbm,
    lat_hbm,
    ids_hbm,
    readings_hbm,
    noise_hbm,
    x_ref,
    r_ref,
    kappa_ref,
    prior_ref,
    templates_ref,
    count_ref,
    lon_ref,
    lat_ref,
    ids_ref,
    readings_ref,
    weights_ref,
    select_ref,
    turned_ref,
    columns_ref,
    padded_ref,
    patch_ref,
    ids_rows_ref,
    term_ref,
    terms_ref,
    r0_ref,
    w0_ref,
    r1_ref,
    w1_ref,
    image_ref,
    v_ref,
    u_ref,
    first_ref,
    pairs_ref,
    own_ref,
    out_lon,
    out_lat,
    out_corner,
    edge_lon,
    edge_lat,
    edge_corner,
    first_a,
    first_b,
    last_a,
    last_b,
    load_sem,
    template_sem,
    edge_send,
    edge_recv,
    corner_sem,
    first_a_sem,
    first_b_sem,
    last_a_sem,
    last_b_sem,
):
    kinds, reads, cells = templates_ref.shape
    rows, cols = kappa_ref.shape
    blocks = ids_ref.shape[1]
    tiles = blocks // PER_TILE
    lon, lat = lax.axis_index("lon"), lax.axis_index("lat")
    chips_lon = n_lon // 2
    core, chip = lon % 2, lon // 2

    loads = [
        pltpu.make_async_copy(source, target, load_sem.at[place])
        for place, (source, target) in enumerate(
            [
                (lat_hbm, lat_ref),
                (ids_hbm, ids_ref),
                (count_hbm, count_ref),
                (noise_hbm, weights_ref),
                (readings_hbm, readings_ref),
                (lon_hbm, lon_ref),
                (kappa_hbm, kappa_ref),
                (prior_hbm, prior_ref),
            ]
        )
    ]

    def template_part(part):
        some = pl.ds(part * PART, PART)
        return pltpu.make_async_copy(
            templates_hbm.at[some], templates_ref.at[some], template_sem.at[part]
        )

    for copy in loads[:5]:
        copy.start()
    for part in range(kinds // PART):
        template_part(part).start()
    for copy in loads[5:]:
        copy.start()

    me_a = lat * 2 + core
    group_a = 2 * n_lat

    def peer_a(step):
        index = (me_a + step) % group_a
        return (chip * 2 + index % 2, index // 2)

    peers_a = [peer_a(step) for step in range(1, group_a)]
    peers_b = [(((chip + step) % chips_lon) * 2 + core, lat) for step in range(1, chips_lon)]
    twin = (chip * 2 + 1 - core, lat)
    peers_far = [
        (((chip + along) % chips_lon) * 2 + core, (lat + across) % n_lat)
        for across, along in far_first(n_lat, chips_lon)
    ]
    lon_next, lon_prev = ((lon + 1) % n_lon, lat), ((lon + n_lon - 1) % n_lon, lat)
    lat_next, lat_prev = (lon, (lat + 1) % n_lat), (lon, (lat + n_lat - 1) % n_lat)
    corners = [(one[0], two[1]) for one in (lon_next, lon_prev) for two in (lat_next, lat_prev)]

    barrier = pltpu.get_barrier_semaphore()
    peers = [lon_next, lon_prev, lat_next, lat_prev] + corners + peers_a + peers_b
    for peer in peers:
        pl.semaphore_signal(barrier, inc=1, device_id=peer, device_id_type=MESH)

    def send_vector(ref, slot):
        for side, near, far in ((0, rows - 1, rows - 2), (1, 0, 1)):
            out_lon[0, side, 0] = ref[near : near + 1, :]
            out_lon[0, side, 1] = ref[far : far + 1, :]
        send_lon(0, slot)
        for side, at in ((0, cols - LANES), (1, 0)):
            near, far = ((0, 1), (LANES - 1, LANES - 2))[1 - side]
            tile = ref[:, at : at + LANES]
            out_lat[0, side, 0] = to_row(tile[:, near : near + 1])
            out_lat[0, side, 1] = to_row(tile[:, far : far + 1])
        send_lat(0, slot)
        for place, (row, col) in enumerate(
            [(rows - 1, cols - 1), (rows - 1, 0), (0, cols - 1), (0, 0)]
        ):
            value = ref[row : row + 1, col // LANES * LANES : col // LANES * LANES + LANES]
            lane_at = col % LANES
            out_corner[place] = jnp.broadcast_to(value[:, lane_at : lane_at + 1], (1, LANES))
        send_corners(slot)

    def pack_coefficients(kappa, prior):
        for place, field in enumerate((kappa, prior)):
            out_lon[1, 0, place] = field[rows - 1 : rows, :]
            out_lon[1, 1, place] = field[0:1, :]
            out_lat[1, 0, place] = to_row(field[:, cols - 1 : cols])
            out_lat[1, 1, place] = to_row(field[:, 0:1])

    def remote(src, dst, send_sem, recv_sem, peer):
        return pltpu.make_async_remote_copy(
            src_ref=src,
            dst_ref=dst,
            send_sem=send_sem,
            recv_sem=recv_sem,
            device_id=peer,
            device_id_type=MESH,
        )

    def whole(ref, sem):
        pltpu.make_async_copy(ref, ref, sem).wait()

    def send_lon(kind, slot):
        for side, peer in enumerate((lon_next, lon_prev)):
            remote(
                out_lon.at[kind, side],
                edge_lon.at[slot, side],
                edge_send.at[kind, 0],
                edge_recv.at[slot, 0],
                peer,
            ).start()

    def send_lat(kind, slot):
        for side, peer in enumerate((lat_next, lat_prev)):
            remote(
                out_lat.at[kind, side],
                edge_lat.at[slot, side],
                edge_send.at[kind, 1],
                edge_recv.at[slot, 1],
                peer,
            ).start()

    def receive_sides(slot):
        whole(edge_lon.at[slot], edge_recv.at[slot, 0])
        whole(edge_lat.at[slot], edge_recv.at[slot, 1])

    def finish_sides(kind):
        whole(out_lon.at[kind], edge_send.at[kind, 0])
        whole(out_lat.at[kind], edge_send.at[kind, 1])

    def send_corners(slot):
        for place, peer in enumerate(corners):
            remote(
                out_corner.at[place],
                edge_corner.at[slot, place],
                corner_sem.at[ITERS],
                corner_sem.at[slot],
                peer,
            ).start()

    def send_sum(buffer, me, sems, peers):
        for peer in peers:
            remote(buffer.at[me], buffer.at[me], sems.at[0], sems.at[1], peer).start()

    def receive_sum(buffer, sems):
        others = buffer.at[pl.ds(0, buffer.shape[0] - 1)]
        whole(others, sems.at[1])
        return jnp.sum(buffer[...], axis=0)

    def finish_sum(buffer, sems):
        whole(buffer.at[pl.ds(0, buffer.shape[0] - 1)], sems.at[0])

    me_far = chip * n_lat + lat
    has_prev = (lat > 0).astype(F32)
    has_next = (lat < n_lat - 1).astype(F32)

    def complete_inner(turn):
        for side, at in ((0, 0), (1, rows - 1)):
            change = prior_ref[at : at + 1, :] * edge_lon[turn, side, 0]
            u_ref[at : at + 1, :] = u_ref[at : at + 1, :] - change
        lane_tile = lax.broadcasted_iota(jnp.int32, (rows, LANES), 1)
        for side, (at, end, present) in enumerate(
            ((0, 0, has_prev), (cols - LANES, LANES - 1, has_next))
        ):
            beside = to_column(edge_lat[turn, side, 0] * present, rows)
            change = prior_ref[:, at : at + LANES] * jnp.where(lane_tile == end, beside, 0.0)
            u_ref[:, at : at + LANES] = u_ref[:, at : at + LANES] - change

    def inner_square():
        field = v_ref[...]
        nothing = jnp.zeros((1, cols), F32), jnp.zeros((rows, 1), F32)
        around = shifted(field, nothing[0], nothing[0], nothing[1], nothing[1])
        inner = (kappa_ref[...] + 4.0) * field - around
        lon_sides = inner[0:1, :], inner[rows - 1 : rows, :]
        lat_sides = to_row(inner[:, 0:1]), to_row(inner[:, cols - 1 : cols])
        scaled = prior_ref[...] * inner
        u_ref[...] = scaled
        own_ref[0] = to_row(field[:, 0:1])
        own_ref[1] = to_row(field[:, cols - 1 : cols])
        return fold(scaled * inner), lon_sides, lat_sides

    def side_square(turn, lon_sides, lat_sides):
        lane_row = lax.broadcasted_iota(jnp.int32, (1, LANES), 1)
        total = jnp.zeros((1, LANES), F32)
        for side in (0, 1):
            beside, own = edge_lon[turn, side, 0], lon_sides[side]
            change = out_lon[1, 1 - side, 1] * beside * (beside - 2.0 * own)
            for at in range(0, cols, LANES):
                total += change[:, at : at + LANES]
        ends = edge_lon[turn, 0, 0], edge_lon[turn, 1, 0]
        for side, (at, present) in enumerate(((0, has_prev), (cols - 1, has_next))):
            beside, own = edge_lat[turn, side, 0] * present, lat_sides[side]
            own = own - jnp.where(lane_row == 0, ends[0][:, at : at + 1], 0.0)
            own = own - jnp.where(lane_row == rows - 1, ends[1][:, at : at + 1], 0.0)
            total += out_lat[1, 1 - side, 1] * beside * (beside - 2.0 * own)
        return total

    def outer_stencil(turn):
        lane_wide = lax.broadcasted_iota(jnp.int32, (1, cols), 1)
        lane_row = lax.broadcasted_iota(jnp.int32, (1, LANES), 1)
        present = (has_prev, has_next)
        beside_lon, beside_lat = [], []
        for side, at in ((0, 0), (1, rows - 1)):
            near, far = edge_lon[turn, side, 0], edge_lon[turn, side, 1]
            kappa, prior = edge_lon[ITERS, side, 0], edge_lon[ITERS, side, 1]
            first = edge_corner[turn, 2 * side][:, :1] * has_prev
            last = edge_corner[turn, 2 * side + 1][:, :1] * has_next
            south = jnp.where(lane_wide == 0, first, pltpu.roll(near, 1, 1))
            north = jnp.where(lane_wide == cols - 1, last, pltpu.roll(near, cols - 1, 1))
            around = far + v_ref[at : at + 1, :] + south + north
            beside_lon.append(prior * ((kappa + 4.0) * near - around))
        for side in (0, 1):
            near, far = edge_lat[turn, side, 0], edge_lat[turn, side, 1]
            kappa, prior = edge_lat[ITERS, side, 0], edge_lat[ITERS, side, 1]
            first, last = edge_corner[turn, side][:, :1], edge_corner[turn, 2 + side][:, :1]
            west = jnp.where(lane_row == 0, first, pltpu.roll(near, 1, 1))
            east = jnp.where(lane_row == rows - 1, last, pltpu.roll(near, LANES - 1, 1))
            around = far + own_ref[side] + west + east
            value = prior * ((kappa + 4.0) * near - around) * present[side]
            beside_lat.append(to_column(value, rows))
        scaled = u_ref[...]
        return (kappa_ref[...] + 4.0) * scaled - shifted(scaled, *beside_lon, *beside_lat)

    padded_ref[...] = jnp.zeros(padded_ref.shape, F32)
    offset = lax.broadcasted_iota(jnp.int32, (PSIDE, cols), 1) - lax.broadcasted_iota(
        jnp.int32, (PSIDE, cols), 0
    )

    lane = lax.broadcasted_iota(jnp.int32, (ROWS, LANES), 1)
    chunk = lane // PSIDE
    cell = lax.broadcasted_iota(jnp.int32, (cols, LANES), 0)

    def selectors(tile):
        for block in range(PER_TILE):
            start = pl.multiple_of((tile * PER_TILE + block) * PSIDE, PSIDE)
            chosen = jnp.where(offset == lat_ref[0, tile * PER_TILE + block], 1.0, 0.0)
            select_ref[pl.ds(start, PSIDE), :] = chosen.astype(BF16)
        place = jnp.zeros((ROWS, LANES), jnp.int32)
        for block in range(PER_TILE):
            anchor = lat_ref[0, tile * PER_TILE + -block % PER_TILE]
            place = jnp.where(chunk == block, anchor, place)
        place = (place + lane % PSIDE)[:1]
        start = pl.multiple_of(tile * LANES, LANES)
        turned_ref[:, pl.ds(start, LANES)] = jnp.where(cell == place, 1.0, 0.0).astype(BF16)

    def twice(value):
        return jnp.concatenate([value, value], 0)

    def one_product(both, ids, first, count):
        left = [
            jnp.where(ids == jnp.asarray(first + kind).astype(BF16), both, jnp.zeros_like(both))
            for kind in range(count)
        ]
        table = templates_ref[pl.ds(first, count)].reshape(count * reads, cells)
        return jnp.dot(jnp.concatenate(left, 1), table, preferred_element_type=F32)

    terms_ref[...] = jnp.zeros(terms_ref.shape, F32)
    for ref in (r0_ref, w0_ref, r1_ref, w1_ref):
        ref[...] = jnp.zeros(ref.shape, F32)
    for copy in loads[:5]:
        copy.wait()
    slot = lax.broadcasted_iota(jnp.int32, (blocks, reads), 0)
    weights = jnp.where(slot < count_ref[...], weights_ref[...], 0.0)
    weights_ref[...] = weights
    ids_row = jnp.broadcast_to(ids_ref[...].astype(F32), (blocks, blocks))
    ids_rows = jnp.transpose(ids_row)
    ids_rows_ref[...] = ids_rows
    weighted = jnp.concatenate(split(weights * readings_ref[...]), 0)
    ids_twice = twice(ids_rows.astype(BF16))
    parts = kinds // PART

    def one_part(part, carry):
        template_part(part).wait()
        terms_ref[...] += one_product(weighted, ids_twice, part * PART, PART)
        for tile in range(tiles // parts):
            selectors(part * (tiles // parts) + tile)
        return carry

    lax.fori_loop(0, parts, one_part, 0)
    terms_ref[0:blocks, :] += terms_ref[blocks : 2 * blocks, :]
    for copy in loads[5:]:
        copy.wait()

    def gather(field):
        field = jnp.concatenate(split(field), 0)
        some = 4
        for first in range(0, tiles, some):
            beside = turned_ref[:, first * LANES : (first + some) * LANES]
            both = jnp.dot(field, beside, preferred_element_type=F32)
            both = both[:rows] + both[rows:]
            for tile in range(some):
                columns_ref[first + tile] = both[:, tile * LANES : (tile + 1) * LANES]
            pick(first, some)

    def pick(first, some):
        for tile in range(first, first + some):
            halves = []
            for half in range(2):
                picked = jnp.zeros((ROWS, LANES), F32)
                for place in range(PER_TILE):
                    start = lon_ref[0, tile * PER_TILE + -place % PER_TILE] + half * ROWS
                    window = columns_ref[tile, pl.ds(start, ROWS), :]
                    picked = jnp.where(chunk == place, window, picked)
                halves.append(picked)
            done = turn_blocks(jnp.stack(halves))
            for half in range(2):
                patch_ref[
                    tile * ROWS : (tile + 1) * ROWS, half * LANES : (half + 1) * LANES
                ] = done[half]

    def read():
        high, low = split(jnp.transpose(patch_ref[...]))
        patches = jnp.concatenate([high, low], 1)
        ids = jnp.broadcast_to(ids_ref[...], (ROWS, blocks))
        ids = jnp.concatenate([ids, ids], 1)
        acc = jnp.zeros((reads, 2 * blocks), F32)
        for kind in range(kinds):
            result = jnp.dot(templates_ref[kind], patches, preferred_element_type=F32)
            acc = jnp.where((ids == kind)[:1], result, acc)
        return jnp.transpose(acc[:, :blocks] + acc[:, blocks:])

    def spread(turn):
        @pl.when(turn > 0)
        def _():
            both = jnp.concatenate(split(term_ref[...]), 0)
            ids = twice(ids_rows_ref[...].astype(BF16))
            terms = jnp.zeros((2 * blocks, cells), F32)
            some = 8
            for first in range(0, kinds, some):
                terms += one_product(both, ids, first, some)
            terms_ref[0:blocks, :] = terms[:blocks] + terms[blocks:]

        terms = terms_ref[0:blocks, :]
        lead = rows - PSIDE
        for half in range(2):
            part = terms[:, half * LANES : (half + 1) * LANES].reshape(tiles, ROWS, LANES)
            part = negate_rows(turn_blocks(part))
            padded_ref[:, lead + half * ROWS : lead + (half + 1) * ROWS, :] = part
        wide = lax.broadcasted_iota(jnp.int32, (rows, LANES), 1) // PSIDE

        placed = []
        for tile in range(tiles):
            picked = jnp.zeros((rows, LANES), F32)
            for place in range(PER_TILE):
                start = lead - lon_ref[0, tile * PER_TILE + place]
                window = padded_ref[tile, pl.ds(start, rows), :]
                picked = jnp.where(wide == place, window, picked)
            placed.append(jnp.concatenate(split(picked), 0))
        both = jnp.dot(
            jnp.concatenate(placed, 1), select_ref[...], preferred_element_type=F32
        )
        return both[:rows] + both[rows:]

    row_at = lax.broadcasted_iota(jnp.int32, (ROWS, LANES), 0)

    def packed(parts):
        parts = [jnp.sum(part, axis=0, keepdims=True) for part in parts]
        parts += [jnp.zeros((1, LANES), F32)] * (ROWS - len(parts))
        total = jnp.sum(jnp.concatenate(parts, 0), axis=1, keepdims=True)
        return jnp.sum(jnp.where(row_at == lane, total, 0.0), axis=0, keepdims=True)

    def unpacked(total, count):
        return [
            jnp.sum(jnp.where(lane[:1] == place, total, 0.0), axis=1, keepdims=True)
            for place in range(count)
        ]

    pack_coefficients(kappa_ref[...], prior_ref[...])

    def one_turn(turn, carry):
        image_ref[...] = spread(turn)

        @pl.when(turn == 1)
        def _():
            receive_sides(ITERS)

        @pl.when((turn > 0) & (turn < ITERS))
        def _():
            receive_sides(turn - 1)

        @pl.when(turn > 0)
        def _():
            complete_inner(turn - 1)
            whole(edge_corner.at[turn - 1], corner_sem.at[turn - 1])

            @pl.when(turn == ITERS)
            def _():
                edge_corner[2] = edge_corner[1] - first_ref[...] * edge_corner[2]

            image_ref[...] += outer_stencil(turn - 1)
            finish_sides(0)
            whole(out_corner, corner_sem.at[ITERS])

        @pl.when(turn == 0)
        def _():
            pl.semaphore_wait(barrier, len(peers))

        @pl.when(turn < ITERS)
        def _():
            send_vector(image_ref, turn)

        @pl.when(turn == 0)
        def _():
            right = image_ref[...]
            r0_ref[...] = right
            v_ref[...] = right
            send_lon(1, ITERS)
            send_lat(1, ITERS)

        @pl.when(turn == 1)
        def _():
            image = image_ref[...]
            w0_ref[...] = image
            v_ref[...] = image

        @pl.when(turn == 2)
        def _():
            norm, curve = unpacked(receive_sum(first_b, first_b_sem), 2)
            step = norm / curve
            w0 = w0_ref[...]
            w1 = w0 - step * image_ref[...]
            r1_ref[...] = r0_ref[...] - step * w0
            w1_ref[...] = w1
            v_ref[...] = w1
            first_ref[...] = jnp.broadcast_to(step, (1, LANES))

        @pl.when(turn == ITERS)
        def _():
            g0, g1, d, b, c, e, a, f = unpacked(receive_sum(last_b, last_b_sem), 8)
            step = first_ref[:, 0:1]
            g2 = d
            l1, l2 = b / a, c / a
            d, e, f = d - l1 * b, e - l1 * c, f - l2 * c
            m = e / d
            f = f - m * e
            g1 = g1 - l1 * g0
            g2 = g2 - l2 * g0 - m * g1
            c2 = g2 / f
            c1 = g1 / d - m * c2
            c0 = g0 / a - l1 * c1 - l2 * c2
            w1, r1 = w1_ref[...], r1_ref[...]
            x_ref[...] = (step + c0) * r0_ref[...] + c1 * r1 + c2 * w1
            r_ref[...] = r1 - c0 * w0_ref[...] - c1 * w1 - c2 * image_ref[...]

        @pl.when(turn < ITERS)
        def _():
            gather(v_ref[...])

            @pl.when(turn == 1)
            def _():
                first_b[chip] = receive_sum(first_a, first_a_sem)
                send_sum(first_b, chip, first_b_sem, peers_b)

            inside, lon_sides, lat_sides = inner_square()
            r0, w0, r1, w1 = r0_ref[...], w0_ref[...], r1_ref[...], w1_ref[...]
            pairs = [(r0, r1), (r1, r1), (r1, w1), (r0, w1), (w0, w1), (w1, w1), (r0, w0)]
            for place, (one, two) in enumerate(pairs):
                pairs_ref[place] = fold(one * two)
            image = read()
            mixed = weights_ref[...] * image
            term_ref[...] = mixed
            pairs_ref[len(pairs)] = inside + fold(mixed * image)

            @pl.when(turn == 0)
            def _():
                parts = [fold(r0_ref[...] * r0_ref[...]), pairs_ref[7]]
                first_a[me_a] = packed(parts)
                send_sum(first_a, me_a, first_a_sem, peers_a)

            @pl.when(turn == 2)
            def _():
                known = packed([pairs_ref[place] for place in range(8)])
                receive_sides(turn)
                step = first_ref[:, 0:1]
                edge_lon[2] = edge_lon[1] - step * edge_lon[2]
                edge_lat[2] = edge_lat[1] - step * edge_lat[2]
                more = side_square(turn, lon_sides, lat_sides)
                more = jnp.sum(more, axis=1, keepdims=True)
                last_a[core] = known + jnp.where(lane[:1] == 7, more, 0.0)
                send_sum(last_a, core, last_a_sem, [twin])
                last_b[me_far] = receive_sum(last_a, last_a_sem)
                send_sum(last_b, me_far, last_b_sem, peers_far)

        return carry

    lax.fori_loop(0, ITERS + 1, one_turn, 0)
    finish_sides(1)
    finish_sum(first_a, first_a_sem)
    finish_sum(first_b, first_b_sem)
    finish_sum(last_a, last_a_sem)
    finish_sum(last_b, last_b_sem)


def far_first(n_lat, chips_lon):
    side = max(1, round(chips_lon**0.5))

    def away(step, size):
        return min(step, size - step)

    steps = [
        (across, along)
        for across in range(n_lat)
        for along in range(chips_lon)
        if across or along
    ]

    def distance(step):
        across, along = step
        return away(across, n_lat) + away(along // side, side) + away(along % side, side)

    return sorted(steps, key=distance, reverse=True)


def hand_out(x_in, r_in, x_out, r_out, sem):
    copies = [
        pltpu.make_async_copy(x_in, x_out, sem.at[0]),
        pltpu.make_async_copy(r_in, r_out, sem.at[1]),
    ]
    for copy in copies:
        copy.start()
    for copy in copies:
        copy.wait()


def on_device(
    n_lon,
    n_lat,
    kappa_sq,
    prior_scale,
    templates,
    block_counts,
    anchor_lon,
    anchor_lat,
    template_ids,
    readings,
    noise_prec,
):
    rows, cols = kappa_sq.shape
    kinds, reads, cells = templates.shape
    blocks = template_ids.shape[1]
    tiles = blocks // PER_TILE
    group_a, chips_lon = 2 * n_lat, n_lon // 2
    chips = n_lat * chips_lon
    vmem = pl.BlockSpec(memory_space=pltpu.VMEM)
    dma = pltpu.SemaphoreType.DMA
    field = jax.ShapeDtypeStruct((rows, cols), F32)
    plane = pltpu.VMEM((rows, cols), F32)
    fields = pl.pallas_call(
        functools.partial(kernel, n_lon, n_lat),
        out_shape=(pltpu.VMEM((rows, cols), F32), pltpu.VMEM((rows, cols), F32)),
        in_specs=[pl.BlockSpec(memory_space=pl.ANY)] * 9,
        out_specs=(vmem, vmem),
        scratch_shapes=[
            plane,
            plane,
            pltpu.VMEM((kinds, reads, cells), BF16),
            pltpu.VMEM((1, 1), jnp.int32),
            pltpu.SMEM((1, blocks), jnp.int32),
            pltpu.SMEM((1, blocks), jnp.int32),
            pltpu.VMEM((1, blocks), jnp.int32),
            pltpu.VMEM((blocks, reads), F32),
            pltpu.VMEM((blocks, reads), F32),
            pltpu.VMEM((blocks * PSIDE, cols), BF16),
            pltpu.VMEM((cols, blocks * PSIDE), BF16),
            pltpu.VMEM((tiles, rows, LANES), F32),
            pltpu.VMEM((tiles, 2 * rows - PSIDE, LANES), F32),
            pltpu.VMEM((blocks, cells), F32),
            pltpu.VMEM((blocks, blocks), F32),
            pltpu.VMEM((blocks, reads), F32),
            pltpu.VMEM((2 * blocks, cells), F32),
            plane,
            plane,
            plane,
            plane,
            plane,
            plane,
            plane,
            pltpu.VMEM((1, LANES), F32),
            pltpu.VMEM((8, ROWS, LANES), F32),
            pltpu.VMEM((2, 1, LANES), F32),
            pltpu.VMEM((2, 2, 2, 1, cols), F32),
            pltpu.VMEM((2, 2, 2, 1, LANES), F32),
            pltpu.VMEM((4, 1, LANES), F32),
            pltpu.VMEM((ITERS + 1, 2, 2, 1, cols), F32),
            pltpu.VMEM((ITERS + 1, 2, 2, 1, LANES), F32),
            pltpu.VMEM((ITERS, 4, 1, LANES), F32),
            pltpu.VMEM((group_a, 1, LANES), F32),
            pltpu.VMEM((chips_lon, 1, LANES), F32),
            pltpu.VMEM((2, 1, LANES), F32),
            pltpu.VMEM((chips, 1, LANES), F32),
            dma((8,)),
            dma((kinds // PART,)),
            dma((2, 2)),
            dma((ITERS + 1, 2)),
            dma((ITERS + 1,)),
            dma((2,)),
            dma((2,)),
            dma((2,)),
            dma((2,)),
        ],
        compiler_params=pltpu.CompilerParams(
            collective_id=0, has_side_effects=True, vmem_limit_bytes=56 * 1024 * 1024
        ),
    )(
        kappa_sq,
        prior_scale,
        templates,
        block_counts.reshape(1, 1),
        anchor_lon,
        anchor_lat,
        template_ids,
        readings[0],
        noise_prec[0],
    )
    return pl.pallas_call(
        hand_out,
        out_shape=(field, field),
        in_specs=[pl.BlockSpec(memory_space=pl.ANY)] * 2,
        out_specs=(pl.BlockSpec(memory_space=pl.ANY),) * 2,
        scratch_shapes=[dma((2,))],
        compiler_params=pltpu.CompilerParams(vmem_limit_bytes=1024 * 1024),
    )(*fields)


def solution(mesh):
    return jax.shard_map(
        functools.partial(on_device, mesh.shape["lon"], mesh.shape["lat"]),
        mesh=mesh,
        in_specs=(
            P("lon", "lat"),
            P("lon", "lat"),
            P(),
            P(("lon", "lat")),
            P("lon", "lat"),
            P("lon", "lat"),
            P("lon", "lat"),
            P("lon", "lat", None),
            P("lon", "lat", None),
        ),
        out_specs=(P("lon", "lat"), P("lon", "lat")),
        check_vma=False,
    )
```
